128 devices in a mesh: ctx: 8 (over x_hi, z), fsdp: 16 (over y, x_lo, core).
Axes of the slice: x: 4 (x_hi: 2, x_lo: 2; x = x_hi * 2 + x_lo), y: 4, z: 4, core: 2. Of those that a mesh axis runs over, the one named last changes fastest.
Arguments:
- tokens: bfloat16 [32, 1024, 1024], P('fsdp', 'ctx'), may hold values from -6 to 6
- span_order: int32 [32, 16], P('fsdp'), may hold values from 0 to 15, as said below
- w_query: bfloat16 [1024, 2048], P('fsdp'), may hold values from -0.1875 to 0.1875
- w_key: bfloat16 [1024, 1024], P('fsdp'), may hold values from -0.1875 to 0.1875
- w_value: bfloat16 [1024, 1024], P('fsdp'), may hold values from -0.1875 to 0.1875
- w_out: bfloat16 [2048, 1024], P('fsdp'), may hold values from -0.125 to 0.125
- w_gate: bfloat16 [1024, 3072], P('fsdp'), may hold values from -0.1875 to 0.1875
- w_up: bfloat16 [1024, 3072], P('fsdp'), may hold values from -0.1875 to 0.1875
- w_down: bfloat16 [3072, 1024], P('fsdp'), may hold values from -0.109375 to 0.109375
- query_gain: float32 [2048], P('fsdp'), may hold values from 0.1 to 1.9
- key_gain: float32 [1024], P('fsdp'), may hold values from 0.1 to 1.9
- attn_gain: float32 [1024], P('fsdp'), may hold values from 0.1 to 1.9
- ffn_gain: float32 [1024], P('fsdp'), may hold values from 0.1 to 1.9
- cotangent: bfloat16 [32, 1024, 1024], P('fsdp', 'ctx'), may hold values from -6 to 6
Outputs:
- layer_out: bfloat16 [32, 1024, 1024], P('fsdp', 'ctx')
- grad_tokens: bfloat16 [32, 1024, 1024], P('fsdp', 'ctx')
- grad_w_query: float32 [1024, 2048], P('fsdp')
- grad_w_key: float32 [1024, 1024], P('fsdp')
- grad_w_value: float32 [1024, 1024], P('fsdp')
- grad_w_out: float32 [2048, 1024], P('fsdp')
- grad_w_gate: float32 [1024, 3072], P('fsdp')
- grad_w_up: float32 [1024, 3072], P('fsdp')
- grad_w_down: float32 [3072, 1024], P('fsdp')
- grad_query_gain: float32 [2048], P('fsdp')
- grad_key_gain: float32 [1024], P('fsdp')
- grad_attn_gain: float32 [1024], P('fsdp')
- grad_ffn_gain: float32 [1024], P('fsdp')
The draws below stay inside these ranges and needn't reach their ends.
Inputs may be any that keep to these rules, and one draw needn't show every extreme that they name: `span_order`: each row is a permutation of the 16 block numbers in which slots 2 c and 2 c + 1 hold blocks p and 15 - p for some p, so that every index of ctx holds one early and one late block of each sequence.
All inputs are finite; a program needn't handle non-finite values.
Results may differ from the reference program's by a relative error of at most 0.028.
Values may be sent and summed in bfloat16 or wider, within the bound.
A program may use at most 256 MiB of HBM per device.

```python
import math
import jax
import jax.numpy as jnp
from jax import lax

D = 1024
HEADS = 16
HEAD = 128
KV_HEADS = 8
FF = 3072
LEN = 1024
QW = 2048
KW = 1024
SPAN = 64
SEQS = 32
N_CTX = 8


def draw_span_order(key, part):
    key = jax.random.fold_in(key, 7)
    pair_key, side_key = jax.random.split(key)
    base_order = jnp.arange(N_CTX, dtype=jnp.int32)
    pair_keys = jax.random.split(pair_key, SEQS)
    pairs = jax.vmap(lambda one_key: jax.random.permutation(one_key, base_order))(pair_keys)
    sides = jax.random.randint(side_key, (SEQS, N_CTX), 0, 2)
    mirror = 2 * N_CTX - 1 - pairs
    first_slot = jnp.where(sides == 1, pairs, mirror)
    second_slot = jnp.where(sides == 1, mirror, pairs)
    return jnp.stack([first_slot, second_slot], -1).reshape(SEQS, 2 * N_CTX).astype(jnp.int32)


def block_scale(rng, dims, shards, low, largest):
    gain = 1.0
    for dim, blocks in shards:
        draws = jax.random.uniform(jax.random.fold_in(jax.random.fold_in(rng, 6), dim), (blocks,), jnp.float32, low / len(shards), largest / len(shards))
        gain = gain * jnp.repeat(jnp.exp(draws), dims[dim] // blocks).reshape((-1,) + (1,) * (len(dims) - 1 - dim))
    return gain


def normal_values(rng, dims, spread, reach, cuts=(), kind=jnp.bfloat16):
    factor_of = block_scale(rng, dims, cuts, -0.22, 0.18) if cuts else 1.0
    drawn = jax.random.normal(rng, dims, jnp.float32) * spread * factor_of
    return jnp.minimum(jnp.maximum(drawn, -reach), reach).astype(kind)


def setup_inputs(seed: int = 0) -> dict:
    seeds = jax.random.split(jax.random.key(seed), 15)
    return {
        "tokens": normal_values(seeds[0], (SEQS, LEN, D), 1.0, 6.0, ((0, 16), (1, 8))),
        "span_order": draw_span_order(jax.random.fold_in(seeds[14], 71), 0),
        "w_query": normal_values(seeds[2], (D, QW), D ** -0.5, 0.1875, ((0, 16),)),
        "w_key": normal_values(seeds[3], (D, KW), D ** -0.5, 0.1875, ((0, 16),)),
        "w_value": normal_values(seeds[4], (D, KW), D ** -0.5, 0.1875, ((0, 16),)),
        "w_out": normal_values(seeds[5], (QW, D), QW ** -0.5, 0.125, ((0, 16),)),
        "w_gate": normal_values(seeds[6], (D, FF), D ** -0.5, 0.1875, ((0, 16),)),
        "w_up": normal_values(seeds[7], (D, FF), D ** -0.5, 0.1875, ((0, 16),)),
        "w_down": normal_values(seeds[8], (FF, D), FF ** -0.5, 0.109375, ((0, 16),)),
        "query_gain": jnp.clip(1.0 + 0.18 * jax.random.normal(seeds[9], (QW,), jnp.float32), 0.1, 1.9),
        "key_gain": jnp.clip(1.0 + 0.18 * jax.random.normal(seeds[10], (KW,), jnp.float32), 0.1, 1.9),
        "attn_gain": jnp.clip(1.0 + 0.18 * jax.random.normal(seeds[11], (D,), jnp.float32), 0.1, 1.9),
        "ffn_gain": jnp.clip(1.0 + 0.18 * jax.random.normal(seeds[12], (D,), jnp.float32), 0.1, 1.9),
        "cotangent": normal_values(seeds[13], (SEQS, LEN, D), 1.0, 6.0, ((0, 16), (1, 8))),
    }


@jax.custom_vjp
def low(v):
    return lax.optimization_barrier(v.astype(jnp.bfloat16)).astype(jnp.float32)

@jax.custom_vjp
def low_back(v):
    return v

def low_keep(v):
    return (low(v), None)

def low_pass(kept, grad):
    return (grad,)

def back_keep(v):
    return (v, None)

def back_low(kept, grad):
    return (low(grad),)
low.defvjp(low_keep, low_pass)
low_back.defvjp(back_keep, back_low)
rope_base = 1000000.0
norm_eps = 1e-06

def matmul_high(left_side, right_side):
    return jnp.dot(left_side, right_side, precision=lax.Precision.HIGHEST)

def rms_norm(values, norm_gain):
    return values * lax.rsqrt(lax.optimization_barrier(jnp.mean(values * values, -1, keepdims=True)) + norm_eps) * norm_gain

def angles(positions):
    steps_half = jnp.arange(HEAD // 2, dtype=jnp.float32)
    inverse_freq = rope_base ** (-2.0 * steps_half / HEAD)
    phase = positions.astype(jnp.float32)[..., None] * inverse_freq
    phase = jnp.concatenate([phase, phase], -1)
    return (jnp.cos(phase), jnp.sin(phase))

def rotate(values, cosine, sine):
    half_width = values.shape[-1] // 2
    turned = jnp.concatenate([-values[..., half_width:], values[..., :half_width]], -1)
    return values * cosine + turned * sine

def attend_one(items):
    query_seq, keys_seq, values_seq, pos_seq = items
    raw_scores = jnp.einsum('qkgd,tkd->kgqt', query_seq, keys_seq, precision=lax.Precision.HIGHEST) * HEAD ** (-0.5)
    raw_scores = low_back(raw_scores)
    visible = pos_seq[None, :] <= pos_seq[:, None]
    masked = jnp.where(visible, raw_scores, -1e+30)
    row_top = lax.optimization_barrier(jnp.max(masked, -1, keepdims=True))
    raised = jnp.exp(masked - row_top)
    probs = low(raised / lax.optimization_barrier(jnp.sum(raised, -1, keepdims=True)))
    result = jnp.einsum('kgqt,tkd->qkgd', probs, values_seq, precision=lax.Precision.HIGHEST)
    return low(low_back(result)).reshape(result.shape[0], HEADS * HEAD)

def layer(tokens_f, params, positions):
    w_query, w_key, w_value, w_out, w_gate, w_up, w_down, query_gain, key_gain, attn_gain, ffn_gain = params
    seq_count, length, width = tokens_f.shape
    rows_all = tokens_f.reshape(-1, width)
    query_raw = low_back(matmul_high(rows_all, w_query))
    key_raw = low_back(matmul_high(rows_all, w_key))
    value_rows = low(low_back(matmul_high(rows_all, w_value)))
    cosine, sine = angles(positions)
    cosine = cosine[:, :, None, :]
    sine = sine[:, :, None, :]
    query = low(rotate(rms_norm(query_raw, query_gain).reshape(seq_count, length, HEADS, HEAD), cosine, sine))
    keys = low(rotate(rms_norm(key_raw, key_gain).reshape(seq_count, length, KV_HEADS, HEAD), cosine, sine))
    values = value_rows.reshape(seq_count, length, KV_HEADS, HEAD)
    query = query.reshape(seq_count, length, KV_HEADS, HEADS // KV_HEADS, HEAD)
    attended = lax.map(jax.checkpoint(attend_one), (query, keys, values, positions))
    attended = attended.reshape(-1, HEADS * HEAD)
    branch = low_back(matmul_high(attended, w_out))
    mixed = rows_all + rms_norm(branch, attn_gain)
    mixed_low = low(mixed)
    gate = low_back(matmul_high(mixed_low, w_gate))
    upward = low_back(matmul_high(mixed_low, w_up))
    middle = low(jax.nn.silu(gate) * upward)
    ffn_out = low_back(matmul_high(middle, w_down))
    result = mixed + rms_norm(ffn_out, ffn_gain)
    return result.reshape(seq_count, length, width)

def reference(tokens, span_order, w_query, w_key, w_value, w_out, w_gate, w_up, w_down, query_gain, key_gain, attn_gain, ffn_gain, cotangent):
    group_seqs = math.gcd(SEQS, max(1, 4096 // LEN))
    group_count = SEQS // group_seqs
    weights = tuple((matrix.astype(jnp.float32) for matrix in (w_query, w_key, w_value, w_out, w_gate, w_up, w_down, query_gain, key_gain, attn_gain, ffn_gain)))
    shaped_tokens = tokens.reshape(group_count, group_seqs, LEN, D)
    shaped_order = span_order.reshape(group_count, group_seqs, 2 * N_CTX)
    shaped_grad = cotangent.reshape(group_count, group_seqs, LEN, D)
    offsets = jnp.arange(SPAN, dtype=jnp.int32)

    def one_group(totals, items):
        group_tokens, group_order, group_grad = items
        positions = (group_order[:, :, None] * SPAN + offsets).reshape(group_seqs, LEN).astype(jnp.int32)

        def forward(tokens_f, params):
            return layer(tokens_f, params, positions)
        result, pullback = jax.vjp(forward, group_tokens.astype(jnp.float32), weights)
        grad_input, grad_params = pullback(group_grad.astype(jnp.float32))
        totals = jax.tree.map(lambda running, fresh: running + fresh, totals, grad_params)
        return (totals, (result.astype(jnp.bfloat16), grad_input.astype(jnp.bfloat16)))
    initial = jax.tree.map(jnp.zeros_like, weights)
    totals, (outputs, grad_inputs) = lax.scan(one_group, initial, (shaped_tokens, shaped_order, shaped_grad))
    return (outputs.reshape(SEQS, LEN, D), grad_inputs.reshape(SEQS, LEN, D), totals[0], totals[1], totals[2], totals[3], totals[4], totals[5], totals[6], totals[7], totals[8], totals[9], totals[10])
```

```python
import functools

import jax
import jax.numpy as jnp
from jax import lax
from jax.experimental import pallas as pl
from jax.experimental.pallas import tpu as pltpu
from jax.sharding import PartitionSpec as P

MESH = pl.DeviceIdType.MESH


def torus_place():
    at_ctx, at_fsdp = lax.axis_index("ctx"), lax.axis_index("fsdp")
    x = at_ctx // 4 * 2 + at_fsdp // 2 % 2
    return {"x": x, "y": at_fsdp // 4, "z": at_ctx % 4, "core": at_fsdp % 2}


def device_at(place):
    at_ctx = place["x"] // 2 * 4 + place["z"]
    at_fsdp = place["y"] * 4 + place["x"] % 2 * 2 + place["core"]
    return (at_ctx, at_fsdp)


def shifted(place, axis, by):
    return {**place, axis: (place[axis] + by) % 4}


def regions(place, axis, at, whole, columns, rows):
    here = {**place, axis: at}
    step = columns // 8
    row = pl.ds(rows[0], rows[1])
    ys = pl.ds(0, 4) if "y" in whole else pl.ds(here["y"], 1)
    los = pl.ds(0, 2) if "x" in whole else pl.ds(here["x"] % 2, 1)
    if "x" in whole and "z" in whole:
        return [(ys, los, row, pl.ds(0, columns))]
    if "z" in whole:
        return [(ys, los, row, pl.ds(pl.multiple_of(here["x"] // 2 * (4 * step), 128), 4 * step))]
    his = [0, 1] if "x" in whole else [here["x"] // 2]
    return [(ys, los, row, pl.ds(pl.multiple_of((hi * 4 + here["z"]) * step, 128), step)) for hi in his]


def greet(place, axes, sibling):
    barrier = pltpu.get_barrier_semaphore()
    others = [device_at(shifted(place, axis, by)) for axis in axes for by in (1, -1)]
    if sibling:
        others.append(device_at({**place, "core": 1 - place["core"]}))
    for other in others:
        pl.semaphore_signal(barrier, inc=1, device_id=other, device_id_type=MESH)
    pl.semaphore_wait(barrier, len(others))


class Copies:
    def __init__(self, send, recv):
        self.send, self.recv, self.used, self.sent = send, recv, 0, []

    def slot(self, count):
        first = self.used
        self.used += count
        return list(range(first, first + count))

    def make(self, slot, src, dst, device):
        return pltpu.make_async_remote_copy(
            src_ref=src, dst_ref=dst, send_sem=self.send.at[slot], recv_sem=self.recv.at[slot],
            device_id=device, device_id_type=MESH)

    def start(self, slot, src, dst, device):
        copy = self.make(slot, src, dst, device)
        copy.start()
        self.sent.append(copy)

    def finish(self):
        for copy in self.sent:
            copy.wait_send()
        self.sent = []


GATHER_ORDER = ("xyz", "yzx", "zxy")


def gather_kernel(part_of, gains, count, *refs):
    n = len(part_of)
    shards, gain_in = refs[:n], refs[n] if gains else None
    refs = refs[n + gains:]
    outs, gain_out = refs[:n], refs[n] if gains else None
    local_sem, send, recv = refs[n + gains:]
    place = torus_place()
    copies = Copies(send, recv)
    greet(place, "xyz", gains)
    mine = []
    for i, (shard, out) in enumerate(zip(shards, outs)):
        columns = out.shape[3]
        step = columns // 8
        at = pl.ds(pl.multiple_of((place["x"] // 2 * 4 + place["z"]) * step, 128), step)
        copy = pltpu.make_async_copy(shard.at[:, at], out.at[place["y"], place["x"] % 2, :, at], local_sem.at[i])
        copy.start()
        mine.append(copy)
    if gains:
        own_gain = pltpu.make_async_copy(gain_in, gain_out.at[place["y"], place["x"] % 2, place["core"]], local_sem.at[n])
        own_gain.start()
        own_gain.wait()
    for copy in mine:
        copy.wait()
    parts = [[i for i in range(n) if part_of[i] == part] for part in range(3)]

    def send_all(members, axis, at, whole, half, by, slots):
        slots = iter(slots)
        for i in members:
            out = outs[i]
            for where in regions(place, axis, at, whole, out.shape[3], half_rows(out, half)):
                copies.start(next(slots), out.at[where], out.at[where], device_at(shifted(place, axis, by)))

    def wait_all(members, axis, at, whole, half, by, slots):
        slots = iter(slots)
        for i in members:
            out = outs[i]
            for where in regions(place, axis, at, whole, out.shape[3], half_rows(out, half)):
                copies.make(next(slots), out.at[where], out.at[where], device_at(shifted(place, axis, by))).wait_recv()

    def half_rows(out, half):
        rows = out.shape[2]
        return (0, rows) if half is None else (half * (rows // 2), rows // 2)

    for phase in range(3):
        held = []
        for part in range(3):
            axis, whole = GATHER_ORDER[part][phase], GATHER_ORDER[part][:phase]
            members = parts[part]
            pieces = sum(len(regions(place, axis, place[axis], whole, outs[i].shape[3], (0, 16))) for i in members)
            slots = {(step, by): copies.slot(pieces) for step in (0, 1) for by in (1, -1)}
            held.append((members, axis, whole, slots))
            for by in (1, -1):
                send_all(members, axis, place[axis], whole, None, by, slots[0, by])
        if gains and phase == 0:
            gain_slots = {(step, by): copies.slot(1)[0] for step in (0, 1) for by in (1, -1)}
            for by in (1, -1):
                where = gain_out.at[place["y"], place["x"] % 2, place["core"]]
                copies.start(gain_slots[0, by], where, where, device_at(shifted(place, "y", by)))
        for members, axis, whole, slots in held:
            for by in (1, -1):
                behind = (place[axis] - by) % 4
                wait_all(members, axis, behind, whole, None, -by, slots[0, by])
                send_all(members, axis, behind, whole, 0 if by == 1 else 1, by, slots[1, by])
        if gains and phase == 0:
            for by in (1, -1):
                behind = (place["y"] - by) % 4
                where = gain_out.at[behind, place["x"] % 2, place["core"]]
                copies.make(gain_slots[0, by], where, where, device_at(shifted(place, "y", -by))).wait_recv()
            behind = (place["y"] - 1) % 4
            where = gain_out.at[behind, place["x"] % 2, place["core"]]
            copies.start(gain_slots[1, 1], where, where, device_at(shifted(place, "y", 1)))
        for members, axis, whole, slots in held:
            for by in (1, -1):
                wait_all(members, axis, (place[axis] + 2) % 4, whole, 0 if by == 1 else 1, -by, slots[1, by])
        if gains and phase == 0:
            where = gain_out.at[(place["y"] + 2) % 4, place["x"] % 2, place["core"]]
            copies.make(gain_slots[1, 1], where, where, device_at(shifted(place, "y", -1))).wait_recv()
        if gains and phase == 1:
            other = {**place, "x": place["x"] // 2 * 2 + (1 - place["x"] % 2)}
            slot = copies.slot(1)[0]
            where = gain_out.at[:, place["x"] % 2, place["core"]]
            copies.start(slot, where, where, device_at(other))
            where = gain_out.at[:, 1 - place["x"] % 2, place["core"]]
            copies.make(slot, where, where, device_at(other)).wait_recv()
    copies.finish()
    if gains:
        other = device_at({**place, "core": 1 - place["core"]})
        slot = copies.slot(1)[0]
        where = gain_out.at[:, :, place["core"]]
        copies.start(slot, where, where, other)
        where = gain_out.at[:, :, 1 - place["core"]]
        copies.make(slot, where, where, other).wait_recv()
        copies.finish()
    assert copies.used <= count, copies.used


def gather_weights(shards, part_of, gain_tile, collective_id, count):
    gains = gain_tile is not None
    outs = [jax.ShapeDtypeStruct((4, 2) + s.shape, s.dtype) for s in shards]
    operands = list(shards)
    if gains:
        outs.append(jax.ShapeDtypeStruct((4, 2, 2) + gain_tile.shape, gain_tile.dtype))
        operands.append(gain_tile)
    return pl.pallas_call(
        functools.partial(gather_kernel, part_of, gains, count),
        out_shape=outs,
        in_specs=[pl.BlockSpec(memory_space=pl.ANY)] * len(operands),
        out_specs=[pl.BlockSpec(memory_space=pl.ANY)] * len(outs),
        scratch_shapes=[pltpu.SemaphoreType.DMA((len(operands),)), pltpu.SemaphoreType.DMA((count,)), pltpu.SemaphoreType.DMA((count,))],
        compiler_params=pltpu.CompilerParams(collective_id=collective_id, has_side_effects=True),
        name="gather_weights",
    )(*operands)


def add_region(acc, temp, at, extra=()):
    ys, los, rows, columns = at
    chunk = 32
    per = rows.size // chunk

    def one(step, carry):
        del carry
        row = step % per * chunk
        lo = step // per % los.size
        y = step // (per * los.size)

        def view(ref, where):
            r = pl.ds(pl.multiple_of(where[2].start + row, 16), chunk)
            return ref.at[where[0].start + y, where[1].start + lo, r, where[3]]

        total = view(acc, at)[...].astype(jnp.float32)
        for t in extra:
            total += view(temp, t)[...].astype(jnp.float32)
        view(acc, at)[...] = total.astype(jnp.bfloat16)
        return 0

    lax.fori_loop(0, per * los.size * ys.size, one, 0)


def reduce_kernel(part_of, count, *refs):
    n = len(part_of)
    grads, outs = refs[:n], refs[n:2 * n]
    accs, temps = refs[2 * n:3 * n], refs[3 * n:4 * n]
    local_sem, send, recv = refs[4 * n:]
    place = torus_place()
    copies = Copies(send, recv)
    loads = []
    for i in range(n):
        load = pltpu.make_async_copy(grads[i], accs[i], local_sem.at[i])
        load.start()
        loads.append(load)
    barrier = pltpu.get_barrier_semaphore()
    far = device_at(shifted(place, "x", 2))
    others = [device_at(shifted(place, axis, by)) for axis in "xyz" for by in (1, -1)] + [far]
    for other in others:
        pl.semaphore_signal(barrier, inc=1, device_id=other, device_id_type=MESH)
    pl.semaphore_wait(barrier, len(others))
    parts = [[i for i in range(n) if part_of[i] == part] for part in range(3)]

    def half_rows(i, half):
        rows = accs[i].shape[2]
        return (half * (rows // 2), rows // 2)

    def blocks(i, phase, part, at, half, landing):
        order = GATHER_ORDER[part]
        here = place
        if landing:
            for axis in order[phase + 1:]:
                here = shifted(here, axis, 1 if half else -1)
        return regions(here, order[phase], at % 4, order[:phase], accs[i].shape[3], half_rows(i, half))

    def send_block(phase, part, at, half, by, land_at, slots):
        slots = iter(slots)
        device = device_at(shifted(place, GATHER_ORDER[part][phase], by))
        for i in parts[part]:
            for src, dst in zip(blocks(i, phase, part, at, half, False), blocks(i, phase, part, land_at, half, True)):
                copies.start(next(slots), accs[i].at[src], temps[i].at[dst], device)

    def wait_block(phase, part, half, by, land_at, slots):
        slots = iter(slots)
        device = device_at(shifted(place, GATHER_ORDER[part][phase], -by))
        for i in parts[part]:
            for dst in blocks(i, phase, part, land_at, half, True):
                copies.make(next(slots), temps[i].at[dst], temps[i].at[dst], device).wait_recv()

    def add_block(phase, part, at, half, land_ats):
        for i in parts[part]:
            where = blocks(i, phase, part, at, half, False)
            landed = [blocks(i, phase, part, land_at, half, True) for land_at in land_ats]
            for k, region in enumerate(where):
                add_region(accs[i], temps[i], region, [t[k] for t in landed])

    for phase in (2, 1, 0):
        slots = {}
        for part in range(3):
            c = place[GATHER_ORDER[part][phase]]
            pieces = sum(len(blocks(i, phase, part, c, 0, False)) for i in parts[part])
            if phase == 2:
                for i in parts[part]:
                    loads[i].wait()
            for by in (1, -1):
                half = 0 if by == 1 else 1
                slots[part, by] = [copies.slot(pieces) for _ in range(3)]
                send_block(phase, part, c + 2, half, by, c + 2, slots[part, by][0])
            for by in (1, -1):
                half = 0 if by == 1 else 1
                send_block(phase, part, c + by, 1 - half, by, c + by if by == 1 else c + 1, slots[part, by][1])
        for part in range(3):
            c = place[GATHER_ORDER[part][phase]]
            for by in (1, -1):
                half = 0 if by == 1 else 1
                wait_block(phase, part, half, by, c + by, slots[part, by][0])
                add_block(phase, part, c + by, half, [c + by])
                send_block(phase, part, c + by, half, by, c + by if by == 1 else c + 1, slots[part, by][2])
        for part in range(3):
            c = place[GATHER_ORDER[part][phase]]
            for half in (0, 1):
                for by in (1, -1):
                    first = half == (0 if by == 1 else 1)
                    wait_block(phase, part, half, by, c if by == 1 else c + 2, slots[part, by][2 if first else 1])
                add_block(phase, part, c, half, [c, c + 2])
    finish_kernel(part_of, accs, outs, place, copies, local_sem)
    assert copies.used <= count, copies.used


def finish_kernel(part_of, accs, outs, place, copies, local_sem):
    n = len(part_of)

    def block(i, x, z):
        step = outs[i].shape[1] // 8
        return outs[i].at[:, pl.ds(pl.multiple_of(((x % 4) // 2 * 4 + z % 4) * step, 128), step)]

    def halves(i, x, z, half):
        step = outs[i].shape[1] // 8
        rows = outs[i].shape[0] // 2
        return outs[i].at[pl.ds(half * rows, rows), pl.ds(pl.multiple_of(((x % 4) // 2 * 4 + z % 4) * step, 128), step)]

    x, z = place["x"], place["z"]
    stores = []
    for i in range(n):
        step = outs[i].shape[1] // 8
        at = pl.ds(pl.multiple_of((x // 2 * 4 + z) * step, 128), step)
        store = pltpu.make_async_copy(accs[i].at[place["y"], x % 2, :, at], block(i, x, z), local_sem.at[i])
        store.start()
        stores.append(store)
    for store in stores:
        store.wait()
    far = device_at(shifted(place, "x", 2))
    up, down = device_at(shifted(place, "z", 1)), device_at(shifted(place, "z", -1))
    slots = {name: copies.slot(n) for name in ("far", "up", "down", "far_up", "far_down", "two_up", "two_down", "far_two_up", "far_two_down")}

    def send(name, view, device):
        for i in range(n):
            copies.start(slots[name][i], view(i), view(i), device)

    def wait(name, view, device):
        for i in range(n):
            copies.make(slots[name][i], view(i), view(i), device).wait_recv()

    send("far", lambda i: block(i, x, z), far)
    send("up", lambda i: block(i, x, z), up)
    send("down", lambda i: block(i, x, z), down)
    wait("far", lambda i: block(i, x + 2, z), far)
    send("far_up", lambda i: block(i, x + 2, z), up)
    send("far_down", lambda i: block(i, x + 2, z), down)
    wait("up", lambda i: block(i, x, z - 1), down)
    send("two_up", lambda i: halves(i, x, z - 1, 0), up)
    wait("down", lambda i: block(i, x, z + 1), up)
    send("two_down", lambda i: halves(i, x, z + 1, 1), down)
    wait("far_up", lambda i: block(i, x + 2, z - 1), down)
    send("far_two_up", lambda i: halves(i, x + 2, z - 1, 0), up)
    wait("far_down", lambda i: block(i, x + 2, z + 1), up)
    send("far_two_down", lambda i: halves(i, x + 2, z + 1, 1), down)
    wait("two_up", lambda i: halves(i, x, z + 2, 0), down)
    wait("two_down", lambda i: halves(i, x, z + 2, 1), up)
    wait("far_two_up", lambda i: halves(i, x + 2, z + 2, 0), down)
    wait("far_two_down", lambda i: halves(i, x + 2, z + 2, 1), up)
    copies.finish()


def reduce_grads(grads, part_of, collective_id, count):
    shapes = [g.shape for g in grads]
    return pl.pallas_call(
        functools.partial(reduce_kernel, part_of, count),
        out_shape=[jax.ShapeDtypeStruct(s[2:], jnp.bfloat16) for s in shapes],
        in_specs=[pl.BlockSpec(memory_space=pl.ANY)] * len(grads),
        out_specs=[pl.BlockSpec(memory_space=pl.ANY)] * len(grads),
        scratch_shapes=[pltpu.VMEM(s, jnp.bfloat16) for s in shapes] * 2
        + [pltpu.SemaphoreType.DMA((len(grads),)), pltpu.SemaphoreType.DMA((count,)), pltpu.SemaphoreType.DMA((count,))],
        compiler_params=pltpu.CompilerParams(collective_id=collective_id, has_side_effects=True, vmem_limit_bytes=50 << 20),
        name="reduce_grads",
    )(*grads)


HEAD = 128
SPAN = 64
TILE = 256
score_scale = HEAD ** (-0.5)


def dot(a, b, a_dim, b_dim):
    return lax.dot_general(a, b, (((a_dim,), (b_dim,)), ((), ())), preferred_element_type=jnp.float32)


def gather_sorted(order_ref, seq, ref, column, width, out, out_at):
    for j in range(16):
        slot = order_ref[seq, j]
        rows = ref[slot // 2, 0, pl.ds(slot % 2 * SPAN, SPAN), column:column + width]
        out[out_at + j * SPAN:out_at + (j + 1) * SPAN, :] = rows


def tile_scores(q, k, low, high):
    scores = dot(q, k, 1, 1) * score_scale
    rows = lax.broadcasted_iota(jnp.int32, scores.shape, 0) % TILE + low
    keys = lax.broadcasted_iota(jnp.int32, scores.shape, 1)
    return jnp.where(keys <= rows, scores, -1e30)


def forward_kernel(order_ref, qkv_ref, out_ref, lse_ref, q_s, k_s, v_s):
    seq = pl.program_id(0)
    gather_sorted(order_ref, seq, qkv_ref, 0, HEAD, q_s.at[0], 0)
    gather_sorted(order_ref, seq, qkv_ref, HEAD, HEAD, q_s.at[1], 0)
    gather_sorted(order_ref, seq, qkv_ref, 2 * HEAD, HEAD, k_s, 0)
    gather_sorted(order_ref, seq, qkv_ref, 3 * HEAD, HEAD, v_s, 0)
    for i in range(1024 // TILE):
        low, high = i * TILE, (i + 1) * TILE
        q = q_s[:, low:high, :].reshape(2 * TILE, HEAD)
        scores = tile_scores(q, k_s[:high], low, high)
        top = jnp.max(scores, -1, keepdims=True)
        raised = jnp.exp(scores - top)
        total = jnp.sum(raised, -1, keepdims=True)
        probs = (raised * (1.0 / total)).astype(jnp.bfloat16)
        out = dot(probs, v_s[:high], 1, 0).astype(jnp.bfloat16)
        lse_ref[0, :, low:high, :] = jnp.broadcast_to(top + jnp.log(total), (2 * TILE, HEAD)).reshape(2, TILE, HEAD)
        for j in range(TILE // SPAN):
            slot = order_ref[seq, low // SPAN + j]
            for h in range(2):
                out_ref[slot // 2, 0, pl.ds(slot % 2 * SPAN, SPAN), h * HEAD:(h + 1) * HEAD] = out[
                    h * TILE + j * SPAN:h * TILE + (j + 1) * SPAN]


def attention_forward(order, qkv):
    return pl.pallas_call(
        forward_kernel,
        grid_spec=pltpu.PrefetchScalarGridSpec(
            num_scalar_prefetch=1, grid=(2,),
            in_specs=[pl.BlockSpec((8, 1, 128, 4 * HEAD), lambda s, order: (0, s, 0, 0))],
            out_specs=[pl.BlockSpec((8, 1, 128, 2 * HEAD), lambda s, order: (0, s, 0, 0)),
                       pl.BlockSpec((1, 2, 1024, HEAD), lambda s, order: (s, 0, 0, 0))],
            scratch_shapes=[pltpu.VMEM((2, 1024, HEAD), jnp.bfloat16), pltpu.VMEM((1024, HEAD), jnp.bfloat16), pltpu.VMEM((1024, HEAD), jnp.bfloat16)]),
        out_shape=[jax.ShapeDtypeStruct((8, 2, 128, 2 * HEAD), jnp.bfloat16), jax.ShapeDtypeStruct((2, 2, 1024, HEAD), jnp.float32)],
        compiler_params=pltpu.CompilerParams(vmem_limit_bytes=40 << 20),
        cost_estimate=pl.CostEstimate(flops=1400000000, bytes_accessed=6 << 20, transcendentals=3 << 20),
        name="attention_forward",
    )(order, qkv)


def backward_kernel(order_ref, qkv_ref, grad_ref, lse_ref, out_ref, q_s, k_s, v_s, g_s, dk_s, dv_s):
    seq = pl.program_id(0)
    gather_sorted(order_ref, seq, qkv_ref, 0, HEAD, q_s.at[0], 0)
    gather_sorted(order_ref, seq, qkv_ref, HEAD, HEAD, q_s.at[1], 0)
    gather_sorted(order_ref, seq, qkv_ref, 2 * HEAD, HEAD, k_s, 0)
    gather_sorted(order_ref, seq, qkv_ref, 3 * HEAD, HEAD, v_s, 0)
    gather_sorted(order_ref, seq, grad_ref, 0, HEAD, g_s.at[0], 0)
    gather_sorted(order_ref, seq, grad_ref, HEAD, HEAD, g_s.at[1], 0)
    tiles = 1024 // TILE
    for i in reversed(range(tiles)):
        low, high = i * TILE, (i + 1) * TILE
        q = q_s[:, low:high, :].reshape(2 * TILE, HEAD)
        g = g_s[:, low:high, :].reshape(2 * TILE, HEAD)
        k, v = k_s[:high], v_s[:high]
        lse = lse_ref[0, :, low:high, :].reshape(2 * TILE, HEAD)[:, :1]
        probs = jnp.exp(tile_scores(q, k, low, high) - lse)
        grad_probs = dot(g, v, 1, 1)
        inner = jnp.sum(probs * grad_probs, -1, keepdims=True)
        grad_scores = (probs * (grad_probs - inner)).astype(jnp.bfloat16)
        probs_low = probs.astype(jnp.bfloat16)
        dq = (dot(grad_scores, k, 1, 0) * score_scale).astype(jnp.bfloat16)
        dk = dot(grad_scores, q, 0, 0)
        dv = dot(probs_low, g, 0, 0)
        if i == tiles - 1:
            dk_s[...] = dk
            dv_s[...] = dv
        else:
            dk_s[:high] += dk
            dv_s[:high] += dv
        for j in range(TILE // SPAN):
            slot = order_ref[seq, low // SPAN + j]
            for h in range(2):
                out_ref[slot // 2, 0, pl.ds(slot % 2 * SPAN, SPAN), h * HEAD:(h + 1) * HEAD] = dq[
                    h * TILE + j * SPAN:h * TILE + (j + 1) * SPAN]
    for j in range(16):
        slot = order_ref[seq, j]
        rows = pl.ds(slot % 2 * SPAN, SPAN)
        at = slice(j * SPAN, (j + 1) * SPAN)
        out_ref[slot // 2, 0, rows, 2 * HEAD:3 * HEAD] = (dk_s[at] * score_scale).astype(jnp.bfloat16)
        out_ref[slot // 2, 0, rows, 3 * HEAD:] = dv_s[at].astype(jnp.bfloat16)


def attention_backward(order, qkv, grad, lse):
    return pl.pallas_call(
        backward_kernel,
        grid_spec=pltpu.PrefetchScalarGridSpec(
            num_scalar_prefetch=1, grid=(2,),
            in_specs=[pl.BlockSpec((8, 1, 128, 4 * HEAD), lambda s, order: (0, s, 0, 0)),
                      pl.BlockSpec((8, 1, 128, 2 * HEAD), lambda s, order: (0, s, 0, 0)),
                      pl.BlockSpec((1, 2, 1024, HEAD), lambda s, order: (s, 0, 0, 0))],
            out_specs=pl.BlockSpec((8, 1, 128, 4 * HEAD), lambda s, order: (0, s, 0, 0)),
            scratch_shapes=[pltpu.VMEM((2, 1024, HEAD), jnp.bfloat16), pltpu.VMEM((1024, HEAD), jnp.bfloat16), pltpu.VMEM((1024, HEAD), jnp.bfloat16),
                            pltpu.VMEM((2, 1024, HEAD), jnp.bfloat16), pltpu.VMEM((1024, HEAD), jnp.float32), pltpu.VMEM((1024, HEAD), jnp.float32)]),
        out_shape=jax.ShapeDtypeStruct((8, 2, 128, 4 * HEAD), jnp.bfloat16),
        compiler_params=pltpu.CompilerParams(vmem_limit_bytes=40 << 20),
        cost_estimate=pl.CostEstimate(flops=3400000000, bytes_accessed=8 << 20, transcendentals=3 << 20),
        name="attention_backward",
    )(order, qkv, grad, lse)


HEADS = 16
KV_HEADS = 8
rope_base = 1000000.0
norm_eps = 1e-06
PART = (1, 2, 2, 0, 0, 1, 2)


def rms_forward(values, norm_gain):
    inverse = lax.rsqrt(jnp.mean(values * values, -1, keepdims=True) + norm_eps)
    return (values * inverse * norm_gain, inverse)


def rms_backward(values, inverse, norm_gain, upstream):
    scaled = upstream * norm_gain
    row_inner = jnp.mean(scaled * values, -1, keepdims=True)
    grad_values = inverse * scaled - values * (inverse * inverse * inverse) * row_inner
    grad_gain = jnp.sum(upstream * values * inverse, 0)
    return (grad_values, grad_gain)


def angles(positions):
    steps_half = jnp.arange(HEAD // 2, dtype=jnp.float32)
    inverse_freq = rope_base ** (-2.0 * steps_half / HEAD)
    phase = positions.astype(jnp.float32)[..., None] * inverse_freq
    phase = jnp.concatenate([phase, phase], -1)
    return (jnp.cos(phase), jnp.sin(phase))


def rotate(values, cosine, sine):
    half_width = values.shape[-1] // 2
    turned = jnp.concatenate([-values[..., half_width:], values[..., :half_width]], -1)
    return values * cosine + turned * sine


def to_sibling(array):
    return lax.ppermute(array, "fsdp", [(i, i ^ 1) for i in range(16)])


def split_columns(rows, core):
    count, width = rows.shape
    stripe = width // 16
    both = rows.reshape(count, 8, 2, stripe).transpose(2, 0, 1, 3).reshape(2, count, width // 2)
    return (lax.dynamic_index_in_dim(both, core, 0, keepdims=False), lax.dynamic_index_in_dim(both, 1 - core, 0, keepdims=False))


def join_columns(own, sibling, core):
    count, half = own.shape
    even = jnp.where(core == 0, own, sibling)
    odd = jnp.where(core == 0, sibling, own)
    both = jnp.stack([even.reshape(count, 8, half // 8), odd.reshape(count, 8, half // 8)], 2)
    return both.reshape(count, 2 * half)


def fold_rows(parts, weights):
    return dot(parts[0], weights[0], 1, 0) + dot(parts[1], weights[1], 1, 0)


def fold_back(grad_rows, weights):
    return [dot(grad_rows, w, 1, 1) for w in weights]


def weight_grad(parts, grad_rows):
    from_sibling = to_sibling(dot(parts[1], grad_rows, 0, 0).astype(jnp.bfloat16))
    total = (dot(parts[0], grad_rows, 0, 0) + from_sibling.astype(jnp.float32)).astype(jnp.bfloat16)
    return total.reshape(4, 2, total.shape[0] // 8, total.shape[1])


def per_device(
    tokens,
    span_order,
    w_query,
    w_key,
    w_value,
    w_out,
    w_gate,
    w_up,
    w_down,
    query_gain,
    key_gain,
    attn_gain,
    ffn_gain,
    cotangent,
):
    seq_local, rows_local, width = tokens.shape
    span_rows = rows_local // 2
    total_rows = seq_local * rows_local
    query_width = HEADS * HEAD
    key_width = KV_HEADS * HEAD
    core = lax.axis_index("fsdp") % 2
    ctx_index = lax.axis_index("ctx")
    token_rows = tokens.reshape(total_rows, width)

    gains_here = jnp.concatenate([query_gain, key_gain, attn_gain, ffn_gain, jnp.zeros((704,), jnp.float32)])
    *gathered, gains_all = gather_weights(
        (w_query, w_key, w_value, w_out, w_gate, w_up, w_down), PART, gains_here.reshape(8, 128), 1, 200)
    own_weights = [w.reshape(8 * w.shape[2], w.shape[3]) for w in gathered]
    pairs = [(w, to_sibling(w)) for w in own_weights]
    wq, wk, wv, wo, wg, wu, wd = pairs
    gains_all = gains_all.reshape(16, 1024)
    q_gain_all = gains_all[:, :128].reshape(-1)
    k_gain_all = gains_all[:, 128:192].reshape(-1)
    a_gain_all = gains_all[:, 192:256].reshape(-1)
    f_gain_all = gains_all[:, 256:320].reshape(-1)

    own_spans = lax.dynamic_slice_in_dim(span_order, 2 * ctx_index, 2, 1)
    offsets = jnp.arange(span_rows, dtype=jnp.int32)
    query_pos = (own_spans[:, :, None] * span_rows + offsets).reshape(seq_local, rows_local)
    cosine, sine = angles(query_pos)
    cosine = cosine[:, :, None, :]
    sine = sine[:, :, None, :]
    numbers = jnp.arange(16, dtype=jnp.int32)
    slot_of = jnp.sum(jnp.where(span_order[:, :, None] == numbers, numbers[None, :, None], 0), 1)

    token_parts = split_columns(token_rows, core)
    query_raw = fold_rows(token_parts, wq)
    key_raw = fold_rows(token_parts, wk)
    value_raw = fold_rows(token_parts, wv)
    query_normed, query_inverse = rms_forward(query_raw, q_gain_all)
    key_normed, key_inverse = rms_forward(key_raw, k_gain_all)
    query_rot = rotate(query_normed.reshape(seq_local, rows_local, HEADS, HEAD), cosine, sine)
    key_rot = rotate(key_normed.reshape(seq_local, rows_local, KV_HEADS, HEAD), cosine, sine)

    def by_heads(array, heads):
        array = array.astype(jnp.bfloat16).reshape(seq_local, rows_local, KV_HEADS, heads * HEAD)
        return array.transpose(2, 0, 1, 3)

    def by_rows(array):
        return array.transpose(1, 2, 0, 3).reshape(total_rows, -1)

    sent = jnp.concatenate([by_heads(query_rot, 2), by_heads(key_rot, 1), by_heads(value_raw, 1)], -1)
    qkv = lax.all_to_all(sent, "ctx", split_axis=0, concat_axis=0, tiled=True)
    out_heads, lse = attention_forward(slot_of, qkv)
    attended = lax.all_to_all(out_heads, "ctx", split_axis=0, concat_axis=0, tiled=True)
    attended_low = by_rows(attended)
    attended_parts = split_columns(attended_low, core)
    branch = fold_rows(attended_parts, wo)
    branch_normed, branch_inverse = rms_forward(branch, a_gain_all)
    mixed = token_rows.astype(jnp.float32) + branch_normed
    mixed_low = mixed.astype(jnp.bfloat16)
    mixed_parts = split_columns(mixed_low, core)
    gate = fold_rows(mixed_parts, wg)
    upward = fold_rows(mixed_parts, wu)
    middle_low = (jax.nn.silu(gate) * upward).astype(jnp.bfloat16)
    middle_parts = split_columns(middle_low, core)
    ffn_out = fold_rows(middle_parts, wd)
    ffn_normed, ffn_inverse = rms_forward(ffn_out, f_gain_all)
    layer_out = (mixed + ffn_normed).astype(jnp.bfloat16).reshape(seq_local, rows_local, width)

    grad_rows_out = cotangent.reshape(total_rows, width).astype(jnp.float32)
    grad_ffn, grad_ffn_gain = rms_backward(ffn_out, ffn_inverse, f_gain_all, grad_rows_out)
    grad_ffn_low = grad_ffn.astype(jnp.bfloat16)
    grad_middle = join_columns(*fold_back(grad_ffn_low, wd), core)
    sigmoid_gate = jax.nn.sigmoid(gate)
    grad_gate = (grad_middle * upward * sigmoid_gate * (1.0 + gate * (1.0 - sigmoid_gate))).astype(jnp.bfloat16)
    grad_upward = (grad_middle * jax.nn.silu(gate)).astype(jnp.bfloat16)
    from_gate = fold_back(grad_gate, wg)
    from_up = fold_back(grad_upward, wu)
    grad_mixed = grad_rows_out + join_columns(from_gate[0] + from_up[0], from_gate[1] + from_up[1], core)
    grad_branch, grad_attn_gain = rms_backward(branch, branch_inverse, a_gain_all, grad_mixed)
    grad_branch_low = grad_branch.astype(jnp.bfloat16)
    grad_attended = join_columns(*fold_back(grad_branch_low, wo), core).astype(jnp.bfloat16)
    grad_sent = grad_attended.reshape(seq_local, rows_local, KV_HEADS, 2 * HEAD).transpose(2, 0, 1, 3)
    grad_heads = lax.all_to_all(grad_sent, "ctx", split_axis=0, concat_axis=0, tiled=True)
    grad_qkv_heads = attention_backward(slot_of, qkv, grad_heads, lse)
    grad_qkv = lax.all_to_all(grad_qkv_heads, "ctx", split_axis=0, concat_axis=0, tiled=True)
    shard_down = weight_grad(middle_parts, grad_ffn_low)
    shard_gate = weight_grad(mixed_parts, grad_gate)
    shard_up = weight_grad(mixed_parts, grad_upward)
    shard_out = weight_grad(attended_parts, grad_branch_low)

    def rows_of(first, heads):
        return grad_qkv[..., first * HEAD : (first + heads) * HEAD].transpose(1, 2, 0, 3).astype(jnp.float32)

    grad_query_rot = rotate(rows_of(0, 2).reshape(seq_local, rows_local, HEADS, HEAD), cosine, -sine)
    grad_query_raw, grad_query_gain = rms_backward(
        query_raw, query_inverse, q_gain_all, grad_query_rot.reshape(total_rows, query_width))
    grad_key_rot = rotate(rows_of(2, 1), cosine, -sine)
    grad_key_raw, grad_key_gain = rms_backward(
        key_raw, key_inverse, k_gain_all, grad_key_rot.reshape(total_rows, key_width))
    grad_query_low = grad_query_raw.astype(jnp.bfloat16)
    grad_key_low = grad_key_raw.astype(jnp.bfloat16)
    grad_value_low = rows_of(3, 1).reshape(total_rows, key_width).astype(jnp.bfloat16)
    shard_query = weight_grad(token_parts, grad_query_low)
    shard_key = weight_grad(token_parts, grad_key_low)
    shard_value = weight_grad(token_parts, grad_value_low)
    from_query = fold_back(grad_query_low, wq)
    from_key = fold_back(grad_key_low, wk)
    from_value = fold_back(grad_value_low, wv)
    grad_tokens = grad_mixed + join_columns(*(a + b + c for a, b, c in zip(from_query, from_key, from_value)), core)
    grad_tokens = grad_tokens.astype(jnp.bfloat16).reshape(seq_local, rows_local, width)
    gain_totals = lax.psum(jnp.concatenate([grad_query_gain, grad_key_gain, grad_attn_gain, grad_ffn_gain]), ("ctx", "fsdp"))
    at = lax.axis_index("fsdp")

    def own_gain(first, count):
        return lax.dynamic_slice_in_dim(gain_totals, first + at * count, count)

    totals = reduce_grads(
        (shard_query, shard_key, shard_value, shard_out, shard_gate, shard_up, shard_down), PART, 2, 400)
    return (
        layer_out,
        grad_tokens,
        *(total.astype(jnp.float32) for total in totals),
        own_gain(0, 128),
        own_gain(2048, 64),
        own_gain(3072, 64),
        own_gain(4096, 64),
    )


def solution(mesh):
    rows, shard, gain = P("fsdp", "ctx", None), P("fsdp", None), P("fsdp")
    return jax.shard_map(
        per_device,
        mesh=mesh,
        in_specs=(rows, shard) + (shard,) * 7 + (gain,) * 4 + (rows,),
        out_specs=(rows, rows) + (shard,) * 7 + (gain,) * 4,
        check_vma=False,
    )
```

```python
import functools

import jax
import jax.numpy as jnp
from jax import lax
from jax.experimental import pallas as pl
from jax.experimental.pallas import tpu as pltpu
from jax.sharding import PartitionSpec as P

MESH = pl.DeviceIdType.MESH


def torus_place():
    at_ctx, at_fsdp = lax.axis_index("ctx"), lax.axis_index("fsdp")
    x = at_ctx // 4 * 2 + at_fsdp // 2 % 2
    return {"x": x, "y": at_fsdp // 4, "z": at_ctx % 4, "core": at_fsdp % 2}


def device_at(place):
    at_ctx = place["x"] // 2 * 4 + place["z"]
    at_fsdp = place["y"] * 4 + place["x"] % 2 * 2 + place["core"]
    return (at_ctx, at_fsdp)


def shifted(place, axis, by):
    return {**place, axis: (place[axis] + by) % 4}


def regions(place, axis, at, whole, columns, rows, first=0):
    here = {**place, axis: at}
    step = columns // 8
    row = pl.ds(rows[0], rows[1])
    ys = pl.ds(0, 4) if "y" in whole else pl.ds(here["y"], 1)
    los = pl.ds(0, 2) if "x" in whole else pl.ds(here["x"] % 2, 1)
    if "x" in whole and "z" in whole:
        return [(ys, los, row, pl.ds(first, columns))]
    if "z" in whole:
        return [(ys, los, row, pl.ds(pl.multiple_of(first + here["x"] // 2 * (4 * step), 128), 4 * step))]
    his = [0, 1] if "x" in whole else [here["x"] // 2]
    return [(ys, los, row, pl.ds(pl.multiple_of(first + (hi * 4 + here["z"]) * step, 128), step)) for hi in his]


def greet(place, axes, sibling):
    barrier = pltpu.get_barrier_semaphore()
    others = [device_at(shifted(place, axis, by)) for axis in axes for by in (1, -1)]
    if sibling:
        others.append(device_at({**place, "core": 1 - place["core"]}))
    for other in others:
        pl.semaphore_signal(barrier, inc=1, device_id=other, device_id_type=MESH)
    pl.semaphore_wait(barrier, len(others))


class Copies:
    def __init__(self, send, recv):
        self.send, self.recv, self.used, self.sent = send, recv, 0, []

    def slot(self, count):
        first = self.used
        self.used += count
        return list(range(first, first + count))

    def make(self, slot, src, dst, device):
        return pltpu.make_async_remote_copy(
            src_ref=src, dst_ref=dst, send_sem=self.send.at[slot], recv_sem=self.recv.at[slot],
            device_id=device, device_id_type=MESH)

    def start(self, slot, src, dst, device):
        copy = self.make(slot, src, dst, device)
        copy.start()
        self.sent.append(copy)

    def finish(self):
        for copy in self.sent:
            copy.wait_send()
        self.sent = []


GATHER_ORDER = ("xyz", "yzx", "zxy")


def gather_kernel(members, gains, count, *refs):
    n, n_out = len(members), 1 + max(m[1] for m in members)
    shards, gain_in = refs[:n], refs[n] if gains else None
    refs = refs[n + gains:]
    outs, gain_out = refs[:n_out], refs[n_out] if gains else None
    local_sem, send, recv = refs[n_out + gains:]
    place = torus_place()
    copies = Copies(send, recv)
    greet(place, "xyz", gains)
    mine = []
    for i, (_, o, first) in enumerate(members):
        step = shards[i].shape[1] // 8
        at = (place["x"] // 2 * 4 + place["z"]) * step
        copy = pltpu.make_async_copy(
            shards[i].at[:, pl.ds(pl.multiple_of(at, 128), step)],
            outs[o].at[place["y"], place["x"] % 2, :, pl.ds(pl.multiple_of(first + at, 128), step)], local_sem.at[i])
        copy.start()
        mine.append(copy)
    if gains:
        own_gain = pltpu.make_async_copy(gain_in, gain_out.at[place["y"], place["x"] % 2, place["core"]], local_sem.at[n])
        own_gain.start()
        own_gain.wait()
    for copy in mine:
        copy.wait()
    parts = [[i for i in range(n) if members[i][0] == part] for part in range(3)]

    def views(group, axis, at, whole, half):
        for i in group:
            _, o, first = members[i]
            rows = shards[i].shape[0]
            rows = (0, rows) if half is None else (half * (rows // 2), rows // 2)
            for where in regions(place, axis, at, whole, shards[i].shape[1], rows, first):
                yield outs[o].at[where]

    def send_all(group, axis, at, whole, half, by, slots):
        for slot, view in zip(slots, views(group, axis, at, whole, half), strict=True):
            copies.start(slot, view, view, device_at(shifted(place, axis, by)))

    def wait_all(group, axis, at, whole, half, by, slots):
        for slot, view in zip(slots, views(group, axis, at, whole, half), strict=True):
            copies.make(slot, view, view, device_at(shifted(place, axis, by))).wait_recv()

    for phase in range(3):
        held = []
        for part in range(3):
            axis, whole = GATHER_ORDER[part][phase], GATHER_ORDER[part][:phase]
            pieces = len(list(views(parts[part], axis, place[axis], whole, None)))
            slots = {(step, by): copies.slot(pieces) for step in (0, 1) for by in (1, -1)}
            held.append((parts[part], axis, whole, slots))
            for by in (1, -1):
                send_all(parts[part], axis, place[axis], whole, None, by, slots[0, by])
        if gains and phase == 0:
            gain_slots = {(step, by): copies.slot(1)[0] for step in (0, 1) for by in (1, -1)}
            for by in (1, -1):
                where = gain_out.at[place["y"], place["x"] % 2, place["core"]]
                copies.start(gain_slots[0, by], where, where, device_at(shifted(place, "y", by)))
        for group, axis, whole, slots in held:
            for by in (1, -1):
                behind = (place[axis] - by) % 4
                wait_all(group, axis, behind, whole, None, -by, slots[0, by])
                send_all(group, axis, behind, whole, 0 if by == 1 else 1, by, slots[1, by])
        if gains and phase == 0:
            for by in (1, -1):
                behind = (place["y"] - by) % 4
                where = gain_out.at[behind, place["x"] % 2, place["core"]]
                copies.make(gain_slots[0, by], where, where, device_at(shifted(place, "y", -by))).wait_recv()
            behind = (place["y"] - 1) % 4
            where = gain_out.at[behind, place["x"] % 2, place["core"]]
            copies.start(gain_slots[1, 1], where, where, device_at(shifted(place, "y", 1)))
        for group, axis, whole, slots in held:
            for by in (1, -1):
                wait_all(group, axis, (place[axis] + 2) % 4, whole, 0 if by == 1 else 1, -by, slots[1, by])
        if gains and phase == 0:
            where = gain_out.at[(place["y"] + 2) % 4, place["x"] % 2, place["core"]]
            copies.make(gain_slots[1, 1], where, where, device_at(shifted(place, "y", -1))).wait_recv()
        if gains and phase == 1:
            other = {**place, "x": place["x"] // 2 * 2 + (1 - place["x"] % 2)}
            slot = copies.slot(1)[0]
            where = gain_out.at[:, place["x"] % 2, place["core"]]
            copies.start(slot, where, where, device_at(other))
            where = gain_out.at[:, 1 - place["x"] % 2, place["core"]]
            copies.make(slot, where, where, device_at(other)).wait_recv()
    copies.finish()
    if gains:
        other = device_at({**place, "core": 1 - place["core"]})
        slot = copies.slot(1)[0]
        where = gain_out.at[:, :, place["core"]]
        copies.start(slot, where, where, other)
        where = gain_out.at[:, :, 1 - place["core"]]
        copies.make(slot, where, where, other).wait_recv()
        copies.finish()
    assert copies.used <= count, copies.used


def gather_weights(shards, members, gain_tile, collective_id, count):
    gains = gain_tile is not None
    widths = [0] * (1 + max(m[1] for m in members))
    rows = list(widths)
    for shard, (_, o, first) in zip(shards, members):
        rows[o], widths[o] = shard.shape[0], max(widths[o], first + shard.shape[1])
    outs = [jax.ShapeDtypeStruct((4, 2, r, w), jnp.bfloat16) for r, w in zip(rows, widths)]
    operands = list(shards)
    if gains:
        outs.append(jax.ShapeDtypeStruct((4, 2, 2) + gain_tile.shape, gain_tile.dtype))
        operands.append(gain_tile)
    return pl.pallas_call(
        functools.partial(gather_kernel, members, gains, count),
        out_shape=outs,
        in_specs=[pl.BlockSpec(memory_space=pl.ANY)] * len(operands),
        out_specs=[pl.BlockSpec(memory_space=pl.ANY)] * len(outs),
        scratch_shapes=[pltpu.SemaphoreType.DMA((len(operands),)), pltpu.SemaphoreType.DMA((count,)), pltpu.SemaphoreType.DMA((count,))],
        compiler_params=pltpu.CompilerParams(collective_id=collective_id, has_side_effects=True),
        name="gather_weights",
    )(*operands)


def add_region(acc, temp, at, extra=()):
    ys, los, rows, columns = at
    chunk = 32
    per = rows.size // chunk

    def one(step, carry):
        del carry
        row = step % per * chunk
        lo = step // per % los.size
        y = step // (per * los.size)

        def view(ref, where):
            r = pl.ds(pl.multiple_of(where[2].start + row, 16), chunk)
            return ref.at[where[0].start + y, where[1].start + lo, r, where[3]]

        total = view(acc, at)[...].astype(jnp.float32)
        for t in extra:
            total += view(temp, t)[...].astype(jnp.float32)
        view(acc, at)[...] = total.astype(jnp.bfloat16)
        return 0

    lax.fori_loop(0, per * los.size * ys.size, one, 0)


def reduce_kernel(members, count, *refs):
    n = 1 + max(m[1] for m in members)
    grads, gain_in = refs[:n], refs[n]
    outs, gain_out = refs[n + 1:2 * n + 1], refs[2 * n + 1]
    accs, temps = refs[2 * n + 2:3 * n + 2], refs[3 * n + 2:4 * n + 2]
    gain_rings, local_sem, send, recv = refs[4 * n + 2:]
    place = torus_place()
    copies = Copies(send, recv)
    loads = []
    for i in range(n):
        load = pltpu.make_async_copy(grads[i], accs[i], local_sem.at[i])
        load.start()
        loads.append(load)
    barrier = pltpu.get_barrier_semaphore()
    far = device_at(shifted(place, "x", 2))
    sibling = device_at({**place, "core": 1 - place["core"]})
    others = [device_at(shifted(place, axis, by)) for axis in "xyz" for by in (1, -1)] + [far, sibling]
    for other in others:
        pl.semaphore_signal(barrier, inc=1, device_id=other, device_id_type=MESH)
    pl.semaphore_wait(barrier, len(others))
    parts = [[m for m in members if m[0] == part] for part in range(3)]

    def blocks(member, phase, at, half, landing):
        part, array, first, columns = member
        order = GATHER_ORDER[part]
        rows = accs[array].shape[2] // 2
        here = place
        if landing:
            for axis in order[phase + 1:]:
                here = shifted(here, axis, 1 if half else -1)
        return regions(here, order[phase], at % 4, order[:phase], columns, (half * rows, rows), first)

    def send_block(phase, part, at, half, by, land_at, slots):
        slots = iter(slots)
        device = device_at(shifted(place, GATHER_ORDER[part][phase], by))
        for m in parts[part]:
            for src, dst in zip(blocks(m, phase, at, half, False), blocks(m, phase, land_at, half, True)):
                copies.start(next(slots), accs[m[1]].at[src], temps[m[1]].at[dst], device)

    def wait_block(phase, part, half, by, land_at, slots):
        slots = iter(slots)
        device = device_at(shifted(place, GATHER_ORDER[part][phase], -by))
        for m in parts[part]:
            for dst in blocks(m, phase, land_at, half, True):
                copies.make(next(slots), temps[m[1]].at[dst], temps[m[1]].at[dst], device).wait_recv()

    def add_block(phase, part, at, half, land_ats):
        for m in parts[part]:
            where = blocks(m, phase, at, half, False)
            landed = [blocks(m, phase, land_at, half, True) for land_at in land_ats]
            for k, region in enumerate(where):
                add_region(accs[m[1]], temps[m[1]], region, [t[k] for t in landed])

    load = pltpu.make_async_copy(gain_in, gain_rings.at[0, place["core"]], local_sem.at[n])
    load.start()
    load.wait()
    slot = copies.slot(1)[0]
    copies.start(slot, gain_rings.at[0, place["core"]], gain_rings.at[0, place["core"]], sibling)
    copies.make(slot, gain_rings.at[0, 1 - place["core"]], gain_rings.at[0, 1 - place["core"]], sibling).wait_recv()
    gain_total = gain_rings[0, 0] + gain_rings[0, 1]

    for phase in (2, 1, 0):
        slots = {}
        for part in range(3):
            c = place[GATHER_ORDER[part][phase]]
            pieces = sum(len(blocks(m, phase, c, 0, False)) for m in parts[part])
            if phase == 2:
                for m in parts[part]:
                    if loads[m[1]] is not None:
                        loads[m[1]].wait()
                        loads[m[1]] = None
            for by in (1, -1):
                half = 0 if by == 1 else 1
                slots[part, by] = [copies.slot(pieces) for _ in range(3)]
                send_block(phase, part, c + 2, half, by, c + 2, slots[part, by][0])
            for by in (1, -1):
                half = 0 if by == 1 else 1
                send_block(phase, part, c + by, 1 - half, by, c + by if by == 1 else c + 1, slots[part, by][1])
        axis, ring = "zyx"[2 - phase], gain_rings.at[3 - phase]
        at = place[axis]
        ring[at] = gain_total
        gain_slots = copies.slot(3)
        for k, by in enumerate((1, -1)):
            copies.start(gain_slots[k], ring.at[at], ring.at[at], device_at(shifted(place, axis, by)))
        for part in range(3):
            c = place[GATHER_ORDER[part][phase]]
            for by in (1, -1):
                half = 0 if by == 1 else 1
                wait_block(phase, part, half, by, c + by, slots[part, by][0])
                add_block(phase, part, c + by, half, [c + by])
                send_block(phase, part, c + by, half, by, c + by if by == 1 else c + 1, slots[part, by][2])
        for k, by in enumerate((1, -1)):
            view = ring.at[(at - by) % 4]
            copies.make(gain_slots[k], view, view, device_at(shifted(place, axis, -by))).wait_recv()
        copies.start(gain_slots[2], ring.at[(at - 1) % 4], ring.at[(at - 1) % 4], device_at(shifted(place, axis, 1)))
        for part in range(3):
            c = place[GATHER_ORDER[part][phase]]
            for half in (0, 1):
                for by in (1, -1):
                    first = half == (0 if by == 1 else 1)
                    wait_block(phase, part, half, by, c if by == 1 else c + 2, slots[part, by][2 if first else 1])
                add_block(phase, part, c, half, [c, c + 2])
        view = ring.at[(at + 2) % 4]
        copies.make(gain_slots[2], view, view, device_at(shifted(place, axis, -1))).wait_recv()
        gain_total = (ring[0] + ring[1]) + (ring[2] + ring[3])
    gain_out[...] = gain_total
    finish_kernel(members, accs, outs, place, copies, local_sem)
    assert copies.used <= count, copies.used


def finish_kernel(members, accs, outs, place, copies, local_sem):
    n = len(members)

    def columns(i, x, z):
        _, _, first, width = members[i]
        step = width // 8
        return pl.ds(pl.multiple_of(first + ((x % 4) // 2 * 4 + z % 4) * step, 128), step)

    def block(i, x, z):
        return outs[members[i][1]].at[:, columns(i, x, z)]

    def halves(i, x, z, half):
        rows = outs[members[i][1]].shape[0] // 2
        return outs[members[i][1]].at[pl.ds(half * rows, rows), columns(i, x, z)]

    x, z = place["x"], place["z"]
    stores = []
    for i in range(n):
        store = pltpu.make_async_copy(accs[members[i][1]].at[place["y"], x % 2, :, columns(i, x, z)], block(i, x, z), local_sem.at[i])
        store.start()
        stores.append(store)
    for store in stores:
        store.wait()
    far = device_at(shifted(place, "x", 2))
    up, down = device_at(shifted(place, "z", 1)), device_at(shifted(place, "z", -1))
    slots = {name: copies.slot(n) for name in ("far", "up", "down", "far_up", "far_down", "two_up", "two_down", "far_two_up", "far_two_down")}

    def send(name, view, device):
        for i in range(n):
            copies.start(slots[name][i], view(i), view(i), device)

    def wait(name, view, device):
        for i in range(n):
            copies.make(slots[name][i], view(i), view(i), device).wait_recv()

    send("far", lambda i: block(i, x, z), far)
    send("up", lambda i: block(i, x, z), up)
    send("down", lambda i: block(i, x, z), down)
    wait("far", lambda i: block(i, x + 2, z), far)
    send("far_up", lambda i: block(i, x + 2, z), up)
    send("far_down", lambda i: block(i, x + 2, z), down)
    wait("up", lambda i: block(i, x, z - 1), down)
    send("two_up", lambda i: halves(i, x, z - 1, 0), up)
    wait("down", lambda i: block(i, x, z + 1), up)
    send("two_down", lambda i: halves(i, x, z + 1, 1), down)
    wait("far_up", lambda i: block(i, x + 2, z - 1), down)
    send("far_two_up", lambda i: halves(i, x + 2, z - 1, 0), up)
    wait("far_down", lambda i: block(i, x + 2, z + 1), up)
    send("far_two_down", lambda i: halves(i, x + 2, z + 1, 1), down)
    wait("two_up", lambda i: halves(i, x, z + 2, 0), down)
    wait("two_down", lambda i: halves(i, x, z + 2, 1), up)
    wait("far_two_up", lambda i: halves(i, x + 2, z + 2, 0), down)
    wait("far_two_down", lambda i: halves(i, x + 2, z + 2, 1), up)
    copies.finish()


def reduce_grads(grads, gain_grads, members, collective_id, count):
    shapes = [g.shape for g in grads]
    return pl.pallas_call(
        functools.partial(reduce_kernel, members, count),
        out_shape=[jax.ShapeDtypeStruct(s[2:], jnp.bfloat16) for s in shapes] + [jax.ShapeDtypeStruct(gain_grads.shape, jnp.float32)],
        in_specs=[pl.BlockSpec(memory_space=pl.ANY)] * (len(grads) + 1),
        out_specs=[pl.BlockSpec(memory_space=pl.ANY)] * len(grads) + [pl.BlockSpec(memory_space=pltpu.VMEM)],
        scratch_shapes=[pltpu.VMEM(s, jnp.bfloat16) for s in shapes] * 2
        + [pltpu.VMEM((4, 4) + gain_grads.shape, jnp.float32), pltpu.SemaphoreType.DMA((8,)),
           pltpu.SemaphoreType.DMA((count,)), pltpu.SemaphoreType.DMA((count,))],
        compiler_params=pltpu.CompilerParams(collective_id=collective_id, has_side_effects=True, vmem_limit_bytes=50 << 20),
        name="reduce_grads",
    )(*grads, gain_grads)


HEAD = 128
SPAN = 64
TILE = 256
score_scale = HEAD ** (-0.5)


def dot(a, b, a_dim, b_dim):
    return lax.dot_general(a, b, (((a_dim,), (b_dim,)), ((), ())), preferred_element_type=jnp.float32)


def gather_sorted(order_ref, seq, ref, column, width, out, out_at):
    for j in range(16):
        slot = order_ref[seq, j]
        rows = ref[slot // 2, 0, pl.ds(slot % 2 * SPAN, SPAN), column:column + width]
        out[out_at + j * SPAN:out_at + (j + 1) * SPAN, :] = rows


def tile_scores(q, k, low, high):
    scores = dot(q, k, 1, 1) * score_scale
    rows = lax.broadcasted_iota(jnp.int32, scores.shape, 0) % TILE + low
    keys = lax.broadcasted_iota(jnp.int32, scores.shape, 1)
    return jnp.where(keys <= rows, scores, -1e30)


def forward_kernel(order_ref, qkv_ref, out_ref, lse_ref, q_s, k_s, v_s):
    seq = pl.program_id(0)
    gather_sorted(order_ref, seq, qkv_ref, 0, HEAD, q_s.at[0], 0)
    gather_sorted(order_ref, seq, qkv_ref, HEAD, HEAD, q_s.at[1], 0)
    gather_sorted(order_ref, seq, qkv_ref, 2 * HEAD, HEAD, k_s, 0)
    gather_sorted(order_ref, seq, qkv_ref, 3 * HEAD, HEAD, v_s, 0)
    for i in range(1024 // TILE):
        low, high = i * TILE, (i + 1) * TILE
        q = q_s[:, low:high, :].reshape(2 * TILE, HEAD)
        scores = tile_scores(q, k_s[:high], low, high)
        top = jnp.max(scores, -1, keepdims=True)
        raised = jnp.exp(scores - top)
        total = jnp.sum(raised, -1, keepdims=True)
        probs = (raised * (1.0 / total)).astype(jnp.bfloat16)
        out = dot(probs, v_s[:high], 1, 0).astype(jnp.bfloat16)
        lse_ref[0, :, low:high, :] = jnp.broadcast_to(top + jnp.log(total), (2 * TILE, HEAD)).reshape(2, TILE, HEAD)
        for j in range(TILE // SPAN):
            slot = order_ref[seq, low // SPAN + j]
            for h in range(2):
                out_ref[slot // 2, 0, pl.ds(slot % 2 * SPAN, SPAN), h * HEAD:(h + 1) * HEAD] = out[
                    h * TILE + j * SPAN:h * TILE + (j + 1) * SPAN]


def attention_forward(order, qkv):
    return pl.pallas_call(
        forward_kernel,
        grid_spec=pltpu.PrefetchScalarGridSpec(
            num_scalar_prefetch=1, grid=(2,),
            in_specs=[pl.BlockSpec((8, 1, 128, 4 * HEAD), lambda s, order: (0, s, 0, 0))],
            out_specs=[pl.BlockSpec((8, 1, 128, 2 * HEAD), lambda s, order: (0, s, 0, 0)),
                       pl.BlockSpec((1, 2, 1024, HEAD), lambda s, order: (s, 0, 0, 0))],
            scratch_shapes=[pltpu.VMEM((2, 1024, HEAD), jnp.bfloat16), pltpu.VMEM((1024, HEAD), jnp.bfloat16), pltpu.VMEM((1024, HEAD), jnp.bfloat16)]),
        out_shape=[jax.ShapeDtypeStruct((8, 2, 128, 2 * HEAD), jnp.bfloat16), jax.ShapeDtypeStruct((2, 2, 1024, HEAD), jnp.float32)],
        compiler_params=pltpu.CompilerParams(vmem_limit_bytes=40 << 20),
        cost_estimate=pl.CostEstimate(flops=1400000000, bytes_accessed=6 << 20, transcendentals=3 << 20),
        name="attention_forward",
    )(order, qkv)


def backward_kernel(order_ref, qkv_ref, grad_ref, lse_ref, out_ref, q_s, k_s, v_s, g_s, dk_s, dv_s):
    seq = pl.program_id(0)
    gather_sorted(order_ref, seq, qkv_ref, 0, HEAD, q_s.at[0], 0)
    gather_sorted(order_ref, seq, qkv_ref, HEAD, HEAD, q_s.at[1], 0)
    gather_sorted(order_ref, seq, qkv_ref, 2 * HEAD, HEAD, k_s, 0)
    gather_sorted(order_ref, seq, qkv_ref, 3 * HEAD, HEAD, v_s, 0)
    gather_sorted(order_ref, seq, grad_ref, 0, HEAD, g_s.at[0], 0)
    gather_sorted(order_ref, seq, grad_ref, HEAD, HEAD, g_s.at[1], 0)
    tiles = 1024 // TILE
    for i in reversed(range(tiles)):
        low, high = i * TILE, (i + 1) * TILE
        q = q_s[:, low:high, :].reshape(2 * TILE, HEAD)
        g = g_s[:, low:high, :].reshape(2 * TILE, HEAD)
        k, v = k_s[:high], v_s[:high]
        lse = lse_ref[0, :, low:high, :].reshape(2 * TILE, HEAD)[:, :1]
        probs = jnp.exp(tile_scores(q, k, low, high) - lse)
        grad_probs = dot(g, v, 1, 1)
        inner = jnp.sum(probs * grad_probs, -1, keepdims=True)
        grad_scores = (probs * (grad_probs - inner)).astype(jnp.bfloat16)
        probs_low = probs.astype(jnp.bfloat16)
        dq = (dot(grad_scores, k, 1, 0) * score_scale).astype(jnp.bfloat16)
        dk = dot(grad_scores, q, 0, 0)
        dv = dot(probs_low, g, 0, 0)
        if i == tiles - 1:
            dk_s[...] = dk
            dv_s[...] = dv
        else:
            dk_s[:high] += dk
            dv_s[:high] += dv
        for j in range(TILE // SPAN):
            slot = order_ref[seq, low // SPAN + j]
            for h in range(2):
                out_ref[slot // 2, 0, pl.ds(slot % 2 * SPAN, SPAN), h * HEAD:(h + 1) * HEAD] = dq[
                    h * TILE + j * SPAN:h * TILE + (j + 1) * SPAN]
    for j in range(16):
        slot = order_ref[seq, j]
        rows = pl.ds(slot % 2 * SPAN, SPAN)
        at = slice(j * SPAN, (j + 1) * SPAN)
        out_ref[slot // 2, 0, rows, 2 * HEAD:3 * HEAD] = (dk_s[at] * score_scale).astype(jnp.bfloat16)
        out_ref[slot // 2, 0, rows, 3 * HEAD:] = dv_s[at].astype(jnp.bfloat16)


def attention_backward(order, qkv, grad, lse):
    return pl.pallas_call(
        backward_kernel,
        grid_spec=pltpu.PrefetchScalarGridSpec(
            num_scalar_prefetch=1, grid=(2,),
            in_specs=[pl.BlockSpec((8, 1, 128, 4 * HEAD), lambda s, order: (0, s, 0, 0)),
                      pl.BlockSpec((8, 1, 128, 2 * HEAD), lambda s, order: (0, s, 0, 0)),
                      pl.BlockSpec((1, 2, 1024, HEAD), lambda s, order: (s, 0, 0, 0))],
            out_specs=pl.BlockSpec((8, 1, 128, 4 * HEAD), lambda s, order: (0, s, 0, 0)),
            scratch_shapes=[pltpu.VMEM((2, 1024, HEAD), jnp.bfloat16), pltpu.VMEM((1024, HEAD), jnp.bfloat16), pltpu.VMEM((1024, HEAD), jnp.bfloat16),
                            pltpu.VMEM((2, 1024, HEAD), jnp.bfloat16), pltpu.VMEM((1024, HEAD), jnp.float32), pltpu.VMEM((1024, HEAD), jnp.float32)]),
        out_shape=jax.ShapeDtypeStruct((8, 2, 128, 4 * HEAD), jnp.bfloat16),
        compiler_params=pltpu.CompilerParams(vmem_limit_bytes=40 << 20),
        cost_estimate=pl.CostEstimate(flops=3400000000, bytes_accessed=8 << 20, transcendentals=3 << 20),
        name="attention_backward",
    )(order, qkv, grad, lse)


HEADS = 16
KV_HEADS = 8
rope_base = 1000000.0
norm_eps = 1e-06
ROWS = 256
WIDTH = 1024
QUERY = HEADS * HEAD
KEY = KV_HEADS * HEAD
FF = 3072


def load_pair(own, sibling, buffer, core, sems):
    copies = [pltpu.make_async_copy(own, buffer.at[:, core], sems.at[0]),
              pltpu.make_async_copy(sibling, buffer.at[:, 1 - core], sems.at[1])]
    for copy in copies:
        copy.start()
    return copies


def wait_all_of(copies):
    for copy in copies:
        copy.wait()


def inverse_rms(values):
    return lax.rsqrt(jnp.mean(values * values, -1, keepdims=True) + norm_eps)


def rms_back(values, inverse, norm_gain, upstream):
    scaled = upstream * norm_gain
    inner = jnp.mean(scaled * values, -1, keepdims=True)
    grad_gain = jnp.sum(upstream * values * inverse, 0, keepdims=True)
    return inverse * scaled - values * (inverse * inverse * inverse * inner), grad_gain


def store_stripes(rows, scratch, width):
    turned = rows.T
    stripe = width // 16
    for j in range(16):
        scratch[j // 2, j % 2] = turned[j * stripe:(j + 1) * stripe]


def project_kernel(core_ref, x_ref, own_ref, sib_ref, qg_ref, kg_ref, cos_ref, sin_ref,
                   sent_ref, q_raw_ref, k_raw_ref, x_own_ref, x_sib_ref, w_s, x_s, sems):
    core = core_ref[0]
    loads = load_pair(own_ref, sib_ref, w_s, core, sems)
    x = x_ref[...]
    store_stripes(x, x_s, WIDTH)
    x_own_ref[...] = x_s[:, core]
    x_sib_ref[...] = x_s[:, 1 - core]
    wait_all_of(loads)

    def block(n, carry):
        at = pl.ds(pl.multiple_of(n * 512, 512), 512)
        q_raw_ref[:, at] = dot(x, w_s[:, :, :, at].reshape(WIDTH, 512), 1, 0)
        return carry

    lax.fori_loop(0, 4, block, 0)
    for n in range(2):
        at = slice(n * 512, (n + 1) * 512)
        k_raw_ref[:, at] = dot(x, w_s[:, :, :, QUERY + n * 512:QUERY + (n + 1) * 512].reshape(WIDTH, 512), 1, 0)
    for n in range(2):
        value = dot(x, w_s[:, :, :, QUERY + KEY + n * 512:QUERY + KEY + (n + 1) * 512].reshape(WIDTH, 512), 1, 0).astype(jnp.bfloat16)
        for h in range(4):
            sent_ref[4 * n + h, :, :, 3 * HEAD:] = value[:, h * HEAD:(h + 1) * HEAD].reshape(2, 128, HEAD)
    cosine, sine = cos_ref[...], sin_ref[...]

    def place_heads(raw_ref, gain_ref, heads, column, each):
        inverse = inverse_rms(raw_ref[...])
        for h in range(heads):
            at = slice(h * HEAD, (h + 1) * HEAD)
            normed = raw_ref[:, at] * inverse * gain_ref[:, at]
            turned = normed * cosine + pltpu.roll(normed, HEAD // 2, 1) * sine
            first = column + h % each * HEAD
            sent_ref[h // each, :, :, first:first + HEAD] = turned.astype(jnp.bfloat16).reshape(2, 128, HEAD)

    place_heads(q_raw_ref, qg_ref, HEADS, 0, 2)
    place_heads(k_raw_ref, kg_ref, KV_HEADS, 2 * HEAD, 1)


def vmem(n):
    return [pl.BlockSpec(memory_space=pltpu.VMEM)] * n


def anywhere(n):
    return [pl.BlockSpec(memory_space=pl.ANY)] * n


SMEM = pl.BlockSpec(memory_space=pltpu.SMEM)
BF16 = jnp.bfloat16
F32 = jnp.float32


def project(core, rows, own, sibling, q_gain, k_gain, cosine, sine):
    return pl.pallas_call(
        project_kernel,
        in_specs=[SMEM] + vmem(1) + anywhere(2) + vmem(4),
        out_specs=vmem(5),
        out_shape=[jax.ShapeDtypeStruct((8, 2, 128, 4 * HEAD), BF16), jax.ShapeDtypeStruct((ROWS, QUERY), F32),
                   jax.ShapeDtypeStruct((ROWS, KEY), F32), jax.ShapeDtypeStruct((8, 64, ROWS), BF16), jax.ShapeDtypeStruct((8, 64, ROWS), BF16)],
        scratch_shapes=[pltpu.VMEM((8, 2, 64, 4096), BF16), pltpu.VMEM((8, 2, 64, ROWS), BF16), pltpu.SemaphoreType.DMA((2,))],
        compiler_params=pltpu.CompilerParams(vmem_limit_bytes=40 << 20),
        cost_estimate=pl.CostEstimate(flops=2200000000, bytes_accessed=16 << 20, transcendentals=0),
        name="project",
    )(core, rows, own, sibling, q_gain, k_gain, cosine, sine)


def middle_kernel(core_ref, heads_ref, x_ref, cot_ref, ag_ref, fg_ref, wo_own, wo_sib, wgu_own, wgu_sib, wd_own, wd_sib,
                  layer_ref, grad_heads_ref, grad_mixed_ref, grad_branch_ref, grad_gu_ref, grad_ffn_ref, gains_ref,
                  att_own_ref, att_sib_ref, mix_own_ref, mix_sib_ref, mid_own_ref, mid_sib_ref,
                  wo_s, wgu_s, wd_s, att_s, gu_s, branch_s, mixed_s, low_s, mid_s, ffn_s, att_t, mix_t, mid_t, sems):
    core = core_ref[0]
    load_o = load_pair(wo_own, wo_sib, wo_s, core, sems.at[0])
    load_gu = load_pair(wgu_own, wgu_sib, wgu_s, core, sems.at[1])
    load_d = load_pair(wd_own, wd_sib, wd_s, core, sems.at[2])
    for g in range(8):
        att_s[:, g * 256:(g + 1) * 256] = heads_ref[g].reshape(ROWS, 256)
    store_stripes(att_s[...], att_t, QUERY)
    wait_all_of(load_o)
    for n in range(2):
        at = slice(n * 512, (n + 1) * 512)
        branch_s[:, at] = dot(att_s[...], wo_s[:, :, :, at].reshape(QUERY, 512), 1, 0)
    branch_inverse = inverse_rms(branch_s[...])
    mixed = x_ref[...].astype(F32) + branch_s[...] * branch_inverse * ag_ref[...]
    mixed_s[...] = mixed
    low_s[...] = mixed.astype(BF16)
    store_stripes(low_s[...], mix_t, WIDTH)
    wait_all_of(load_gu)

    def forward_block(n, carry):
        at = pl.ds(pl.multiple_of(n * 512, 512), 512)
        up_at = pl.ds(pl.multiple_of(FF + n * 512, 512), 512)
        gate = dot(low_s[...], wgu_s[:, :, :, at].reshape(WIDTH, 512), 1, 0)
        up = dot(low_s[...], wgu_s[:, :, :, up_at].reshape(WIDTH, 512), 1, 0)
        gu_s[:, at] = gate
        gu_s[:, up_at] = up
        mid_s[:, at] = (gate * jax.nn.sigmoid(gate) * up).astype(BF16)
        return carry

    lax.fori_loop(0, FF // 512, forward_block, 0)
    wait_all_of(load_d)
    for n in range(2):
        at = slice(n * 512, (n + 1) * 512)
        ffn_s[:, at] = dot(mid_s[...], wd_s[:, :, :, at].reshape(FF, 512), 1, 0)
    store_stripes(mid_s[...], mid_t, FF)
    ffn_out = ffn_s[...]
    ffn_inverse = inverse_rms(ffn_out)
    layer_ref[...] = (mixed_s[...] + ffn_out * ffn_inverse * fg_ref[...]).astype(BF16)
    grad_ffn, grad_ffn_gain = rms_back(ffn_out, ffn_inverse, fg_ref[...], cot_ref[...].astype(F32))
    grad_ffn_ref[...] = grad_ffn.astype(BF16)

    def backward_block(n, carry):
        at = pl.ds(pl.multiple_of(n * 768, 256), 768)
        up_at = pl.ds(pl.multiple_of(FF + n * 768, 256), 768)
        grad_middle = dot(grad_ffn_ref[...], wd_s[pl.ds(n * 2, 2)].reshape(768, WIDTH), 1, 1)
        gate, up = gu_s[:, at], gu_s[:, up_at]
        sigmoid_gate = jax.nn.sigmoid(gate)
        grad_gu_ref[:, at] = (grad_middle * up * sigmoid_gate * (1.0 + gate * (1.0 - sigmoid_gate))).astype(BF16)
        grad_gu_ref[:, up_at] = (grad_middle * (gate * sigmoid_gate)).astype(BF16)
        return carry

    lax.fori_loop(0, 4, backward_block, 0)
    for n in range(4):
        at = slice(n * 256, (n + 1) * 256)
        ffn_s[:, at] = cot_ref[:, at].astype(F32) + dot(grad_gu_ref[...], wgu_s[2 * n:2 * n + 2].reshape(256, 2 * FF), 1, 1)
    grad_mixed_ref[...] = ffn_s[...]
    grad_branch, grad_attn_gain = rms_back(branch_s[...], branch_inverse, ag_ref[...], ffn_s[...])
    grad_branch_ref[...] = grad_branch.astype(BF16)
    for g in range(8):
        grad = dot(grad_branch_ref[...], wo_s[g].reshape(256, WIDTH), 1, 1)
        grad_heads_ref[g] = grad.astype(BF16).reshape(2, 128, 256)
    gains_ref[...] = jnp.zeros_like(gains_ref)
    gains_ref[0:1] = grad_attn_gain
    gains_ref[1:2] = grad_ffn_gain
    for own, sib, turned in ((att_own_ref, att_sib_ref, att_t), (mix_own_ref, mix_sib_ref, mix_t), (mid_own_ref, mid_sib_ref, mid_t)):
        own[...] = turned[:, core]
        sib[...] = turned[:, 1 - core]


def middle(core, heads, rows, cotangent, a_gain, f_gain, wo, wgu, wd):
    def stripes(width):
        return [jax.ShapeDtypeStruct((8, width // 16, ROWS), BF16)] * 2

    return pl.pallas_call(
        middle_kernel,
        in_specs=[SMEM] + vmem(5) + anywhere(6),
        out_specs=vmem(13),
        out_shape=[jax.ShapeDtypeStruct((ROWS, WIDTH), BF16), jax.ShapeDtypeStruct((8, 2, 128, 256), BF16), jax.ShapeDtypeStruct((ROWS, WIDTH), F32),
                   jax.ShapeDtypeStruct((ROWS, WIDTH), BF16), jax.ShapeDtypeStruct((ROWS, 2 * FF), BF16), jax.ShapeDtypeStruct((ROWS, WIDTH), BF16),
                   jax.ShapeDtypeStruct((8, WIDTH), F32)] + stripes(QUERY) + stripes(WIDTH) + stripes(FF),
        scratch_shapes=[pltpu.VMEM((8, 2, 128, WIDTH), BF16), pltpu.VMEM((8, 2, 64, 2 * FF), BF16), pltpu.VMEM((8, 2, 192, WIDTH), BF16),
                        pltpu.VMEM((ROWS, QUERY), BF16), pltpu.VMEM((ROWS, 2 * FF), F32), pltpu.VMEM((ROWS, WIDTH), F32), pltpu.VMEM((ROWS, WIDTH), F32),
                        pltpu.VMEM((ROWS, WIDTH), BF16), pltpu.VMEM((ROWS, FF), BF16), pltpu.VMEM((ROWS, WIDTH), F32),
                        pltpu.VMEM((8, 2, 128, ROWS), BF16), pltpu.VMEM((8, 2, 64, ROWS), BF16), pltpu.VMEM((8, 2, 192, ROWS), BF16),
                        pltpu.SemaphoreType.DMA((3, 2))],
        compiler_params=pltpu.CompilerParams(vmem_limit_bytes=60 << 20),
        cost_estimate=pl.CostEstimate(flops=12000000000, bytes_accessed=40 << 20, transcendentals=3 << 20),
        name="middle",
    )(core, heads, rows, cotangent, a_gain, f_gain, *wo, *wgu, *wd)


def last_kernel(core_ref, grad_ref, q_raw_ref, k_raw_ref, mixed_ref, qg_ref, kg_ref, cos_ref, sin_ref, own_ref, sib_ref,
                tokens_ref, grad_out_ref, gains_ref, w_s, dy_s, sems):
    loads = load_pair(own_ref, sib_ref, w_s, core_ref[0], sems)
    cosine, sine = cos_ref[...], sin_ref[...]

    def one(raw_ref, gain_ref, heads, column, each, out_at):
        width = heads * HEAD
        for h in range(heads):
            first = column + h % each * HEAD
            u = grad_ref[h // each, :, :, first:first + HEAD].reshape(ROWS, HEAD).astype(F32)
            dy_s[:, h * HEAD:(h + 1) * HEAD] = u * cosine - pltpu.roll(u, HEAD // 2, 1) * sine
        raw = raw_ref[...]
        grad, grad_gain = rms_back(raw, inverse_rms(raw), gain_ref[...], dy_s[:, :width])
        grad_out_ref[:, out_at:out_at + width] = grad.astype(BF16)
        return grad_gain

    q_gain = one(q_raw_ref, qg_ref, HEADS, 0, 2, 0)
    k_gain = one(k_raw_ref, kg_ref, KV_HEADS, 2 * HEAD, 1, QUERY)
    for g in range(8):
        grad_out_ref[:, QUERY + KEY + g * HEAD:QUERY + KEY + (g + 1) * HEAD] = grad_ref[g, :, :, 3 * HEAD:].reshape(ROWS, HEAD)
    gains_ref[...] = jnp.zeros_like(gains_ref)
    gains_ref[0:1] = q_gain[:, :WIDTH]
    gains_ref[1:2] = q_gain[:, WIDTH:]
    gains_ref[2:3] = k_gain
    wait_all_of(loads)
    for n in range(4):
        at = slice(n * 256, (n + 1) * 256)
        tokens_ref[:, at] = (mixed_ref[:, at] + dot(grad_out_ref[...], w_s[2 * n:2 * n + 2].reshape(256, 4096), 1, 1)).astype(BF16)


def last(core, grad, q_raw, k_raw, grad_mixed, q_gain, k_gain, cosine, sine, own, sibling):
    return pl.pallas_call(
        last_kernel,
        in_specs=[SMEM] + vmem(8) + anywhere(2),
        out_specs=vmem(3),
        out_shape=[jax.ShapeDtypeStruct((ROWS, WIDTH), BF16), jax.ShapeDtypeStruct((ROWS, 4096), BF16), jax.ShapeDtypeStruct((8, WIDTH), F32)],
        scratch_shapes=[pltpu.VMEM((8, 2, 64, 4096), BF16), pltpu.VMEM((ROWS, QUERY), F32), pltpu.SemaphoreType.DMA((2,))],
        compiler_params=pltpu.CompilerParams(vmem_limit_bytes=40 << 20),
        cost_estimate=pl.CostEstimate(flops=2200000000, bytes_accessed=16 << 20, transcendentals=0),
        name="last",
    )(core, grad, q_raw, k_raw, grad_mixed, q_gain, k_gain, cosine, sine, own, sibling)
MEMBERS = ((1, 0, 0, 2048), (2, 0, 2048, 1024), (2, 0, 3072, 1024), (0, 1, 0, 1024), (0, 2, 0, 3072), (1, 2, 3072, 3072), (2, 3, 0, 1024))


def angles(positions):
    steps_half = jnp.arange(HEAD // 2, dtype=jnp.float32)
    inverse_freq = rope_base ** (-2.0 * steps_half / HEAD)
    phase = positions.astype(jnp.float32)[..., None] * inverse_freq
    cosine, sine = jnp.cos(phase), jnp.sin(phase)
    return jnp.concatenate([cosine, cosine], -1), jnp.concatenate([-sine, sine], -1)


def to_sibling(array):
    return lax.ppermute(array, "fsdp", [(i, i ^ 1) for i in range(16)])


def weight_grad(own, sibling, grad_rows):
    count = own.shape[1]
    from_sibling = to_sibling(dot(sibling.reshape(8 * count, ROWS), grad_rows, 1, 0).astype(BF16))
    total = (dot(own.reshape(8 * count, ROWS), grad_rows, 1, 0) + from_sibling.astype(F32)).astype(BF16)
    return total.reshape(4, 2, count, total.shape[1])


def per_device(
    tokens,
    span_order,
    w_query,
    w_key,
    w_value,
    w_out,
    w_gate,
    w_up,
    w_down,
    query_gain,
    key_gain,
    attn_gain,
    ffn_gain,
    cotangent,
):
    seq_local, rows_local, width = tokens.shape
    span_rows = rows_local // 2
    at_fsdp = lax.axis_index("fsdp")
    core = (at_fsdp % 2).astype(jnp.int32).reshape(1)
    token_rows = tokens.reshape(ROWS, width)

    gains_here = jnp.concatenate([query_gain, key_gain, attn_gain, ffn_gain, jnp.zeros((704,), F32)])
    *gathered, gains_all = gather_weights(
        (w_query, w_key, w_value, w_out, w_gate, w_up, w_down), tuple(m[:3] for m in MEMBERS), gains_here.reshape(8, 128), 1, 200)
    own_weights = [w.reshape((8,) + w.shape[2:]) for w in gathered]
    wqkv, wo, wgu, wd = [(w, to_sibling(w)) for w in own_weights]
    gains_all = gains_all.reshape(16, 1024)
    q_gain_all = gains_all[:, :128].reshape(1, QUERY)
    k_gain_all = gains_all[:, 128:192].reshape(1, KEY)
    a_gain_all = gains_all[:, 192:256].reshape(1, WIDTH)
    f_gain_all = gains_all[:, 256:320].reshape(1, WIDTH)

    own_spans = lax.dynamic_slice_in_dim(span_order, 2 * lax.axis_index("ctx"), 2, 1)
    offsets = jnp.arange(span_rows, dtype=jnp.int32)
    cosine, sine = angles((own_spans[:, :, None] * span_rows + offsets).reshape(ROWS))
    numbers = jnp.arange(16, dtype=jnp.int32)
    slot_of = jnp.sum(jnp.where(span_order[:, :, None] == numbers, numbers[None, :, None], 0), 1)

    def exchange(array):
        return lax.all_to_all(array, "ctx", split_axis=0, concat_axis=0, tiled=True)

    sent, query_raw, key_raw, tok_own, tok_sib = project(core, token_rows, *wqkv, q_gain_all, k_gain_all, cosine, sine)
    qkv = exchange(sent)
    out_heads, lse = attention_forward(slot_of, qkv)
    (layer_out, grad_sent, grad_mixed, grad_branch, grad_gu, grad_ffn, gains_af,
     att_own, att_sib, mix_own, mix_sib, mid_own, mid_sib) = middle(
        core, exchange(out_heads), token_rows, cotangent.reshape(ROWS, width), a_gain_all, f_gain_all, wo, wgu, wd)
    grad_heads = exchange(grad_sent)
    shard_down = weight_grad(mid_own, mid_sib, grad_ffn)
    shard_gu = weight_grad(mix_own, mix_sib, grad_gu)
    shard_out = weight_grad(att_own, att_sib, grad_branch)
    grad_qkv_heads = attention_backward(slot_of, qkv, grad_heads, lse)
    grad_tokens, grad_qkv, gains_qk = last(
        core, exchange(grad_qkv_heads), query_raw, key_raw, grad_mixed, q_gain_all, k_gain_all, cosine, sine, *wqkv)
    shard_qkv = weight_grad(tok_own, tok_sib, grad_qkv)
    gain_grads = jnp.concatenate([gains_qk[:3], gains_af[:2], jnp.zeros((3, WIDTH), F32)])
    *totals, gain_totals = reduce_grads((shard_qkv, shard_out, shard_gu, shard_down), gain_grads, MEMBERS, 2, 400)
    qkv_total, out_total, gu_total, down_total = [t.astype(F32) for t in totals]
    gain_totals = gain_totals.reshape(-1)

    def own_gain(first, count):
        return lax.dynamic_slice_in_dim(gain_totals, first + at_fsdp * count, count)

    return (
        layer_out.reshape(tokens.shape),
        grad_tokens.reshape(tokens.shape),
        qkv_total[:, :QUERY],
        qkv_total[:, QUERY:QUERY + KEY],
        qkv_total[:, QUERY + KEY:],
        out_total,
        gu_total[:, :FF],
        gu_total[:, FF:],
        down_total,
        own_gain(0, 128),
        own_gain(2048, 64),
        own_gain(3072, 64),
        own_gain(4096, 64),
    )


def solution(mesh):
    rows, shard, gain = P("fsdp", "ctx", None), P("fsdp", None), P("fsdp")
    return jax.shard_map(
        per_device,
        mesh=mesh,
        in_specs=(rows, shard) + (shard,) * 7 + (gain,) * 4 + (rows,),
        out_specs=(rows, rows) + (shard,) * 7 + (gain,) * 4,
        check_vma=False,
    )
```

```python
import functools

import jax
import jax.numpy as jnp
from jax import lax
from jax.experimental import pallas as pl
from jax.experimental.pallas import tpu as pltpu
from jax.sharding import PartitionSpec as P

MESH = pl.DeviceIdType.MESH
SMEM = pl.BlockSpec(memory_space=pltpu.SMEM)
BF16 = jnp.bfloat16
F32 = jnp.float32
HEADS = 16
KV_HEADS = 8
HEAD = 128
SPAN = 64
TILE = 256
LENGTH = 1024
ROWS = 256
WIDTH = 1024
QUERY = HEADS * HEAD
KEY = KV_HEADS * HEAD
QKV = QUERY + 2 * KEY
FF = 3072
rope_base = 1000000.0
norm_eps = 1e-06
score_scale = HEAD ** (-0.5)


def vmem(n):
    return [pl.BlockSpec(memory_space=pltpu.VMEM)] * n


def anywhere(n):
    return [pl.BlockSpec(memory_space=pl.ANY)] * n


def dot(a, b, a_dim, b_dim):
    return lax.dot_general(a, b, (((a_dim,), (b_dim,)), ((), ())), preferred_element_type=F32)


def torus_place():
    at_ctx, at_fsdp = lax.axis_index("ctx"), lax.axis_index("fsdp")
    x = at_ctx // 4 * 2 + at_fsdp // 2 % 2
    return {"x": x, "y": at_fsdp // 4, "z": at_ctx % 4, "core": at_fsdp % 2}


def device_at(place):
    at_ctx = place["x"] // 2 * 4 + place["z"]
    at_fsdp = place["y"] * 4 + place["x"] % 2 * 2 + place["core"]
    return (at_ctx, at_fsdp)


def shifted(place, axis, by):
    return {**place, axis: (place[axis] + by) % 4}


def other_core(place):
    return device_at({**place, "core": 1 - place["core"]})


def ctx_device(offset):
    return ((lax.axis_index("ctx") + offset) % 8, lax.axis_index("fsdp"))


def greet(others):
    barrier = pltpu.get_barrier_semaphore()
    for other in others:
        pl.semaphore_signal(barrier, inc=1, device_id=other, device_id_type=MESH)
    pl.semaphore_wait(barrier, len(others))


class Copies:
    def __init__(self, send, recv, count):
        self.send, self.recv, self.count, self.used, self.sent = send, recv, count, 0, []

    def slot(self, count):
        first = self.used
        self.used += count
        assert self.used <= self.count, self.used
        return list(range(first, first + count))

    def make(self, slot, src, dst, device):
        return pltpu.make_async_remote_copy(
            src_ref=src, dst_ref=dst, send_sem=self.send.at[slot], recv_sem=self.recv.at[slot],
            device_id=device, device_id_type=MESH)

    def start(self, slot, src, dst, device):
        copy = self.make(slot, src, dst, device)
        copy.start()
        self.sent.append(copy)

    def arrived(self, slot, dst, device):
        self.make(slot, dst, dst, device).wait_recv()

    def finish(self):
        for copy in self.sent:
            copy.wait_send()
        self.sent = []


class Member:
    def __init__(self, array, row, rows, first, columns):
        self.array, self.row, self.rows, self.first, self.columns = array, row, rows, first, columns

    def half(self, half):
        return (self.row, self.rows) if half is None else (self.row + half * (self.rows // 2), self.rows // 2)

    def block(self, x, z):
        step = self.columns // 8
        return pl.ds(pl.multiple_of(self.first + ((x % 4) // 2 * 4 + z % 4) * step, 128), step)

    def regions(self, place, axis, at, whole, half):
        here = {**place, axis: at % 4}
        step = self.columns // 8
        row = pl.ds(*self.half(half))
        ys = pl.ds(0, 4) if "y" in whole else pl.ds(here["y"], 1)
        los = pl.ds(0, 2) if "x" in whole else pl.ds(here["x"] % 2, 1)
        if "x" in whole and "z" in whole:
            return [(ys, los, row, pl.ds(self.first, self.columns))]
        if "z" in whole:
            return [(ys, los, row, pl.ds(pl.multiple_of(self.first + here["x"] // 2 * (4 * step), 128), 4 * step))]
        his = [0, 1] if "x" in whole else [here["x"] // 2]
        return [(ys, los, row, pl.ds(pl.multiple_of(self.first + (hi * 4 + here["z"]) * step, 128), step)) for hi in his]


ORDERS = ("xyz", "yzx", "zxy")


def gather_part(copies, place, order, members, refs):
    def views(axis, at, whole, half):
        return [refs[m.array].at[where] for m in members for where in m.regions(place, axis, at, whole, half)]

    def send(axis, at, whole, half, by, slots):
        for slot, view in zip(slots, views(axis, at, whole, half), strict=True):
            copies.start(slot, view, view, device_at(shifted(place, axis, by)))

    def wait(axis, at, whole, half, by, slots):
        for slot, view in zip(slots, views(axis, at, whole, half), strict=True):
            copies.arrived(slot, view, device_at(shifted(place, axis, -by)))

    for phase, axis in enumerate(order):
        whole, c = order[:phase], place[axis]
        pieces = len(views(axis, c, whole, None))
        slots = {(step, by): copies.slot(pieces) for step in (0, 1) for by in (1, -1)}
        for by in (1, -1):
            send(axis, c, whole, None, by, slots[0, by])
        yield
        for by in (1, -1):
            wait(axis, c - by, whole, None, by, slots[0, by])
            send(axis, c - by, whole, 0 if by == 1 else 1, by, slots[1, by])
        yield
        for by in (1, -1):
            wait(axis, c + 2, whole, 0 if by == 1 else 1, by, slots[1, by])


def run(steps):
    steps = list(steps)
    while steps:
        steps = [s for s in steps if next(s, "end") is None]


def advance(steps):
    for s in steps:
        next(s, None)


def inverse_rms(values):
    return lax.rsqrt(jnp.mean(values * values, -1, keepdims=True) + norm_eps)


def rms_back(values, inverse, norm_gain, upstream):
    scaled = upstream * norm_gain
    inner = jnp.mean(scaled * values, -1, keepdims=True)
    grad_gain = jnp.sum(upstream * values * inverse, 0, keepdims=True)
    return inverse * scaled - values * (inverse * inverse * inverse * inner), grad_gain


def store_stripes(rows, scratch, width):
    turned = rows.T
    stripe = width // 16
    for j in range(16):
        scratch[j // 2, j % 2] = turned[j * stripe:(j + 1) * stripe]


def sorted_blocks(slot_ref, seq, ref, outs):
    for j in range(16):
        block = ref[slot_ref[seq, j]]
        for k, out in enumerate(outs):
            out[j * SPAN:(j + 1) * SPAN, :] = block[:, k * HEAD:(k + 1) * HEAD]


def sent_blocks(span_ref, seq, ref, out):
    for j in range(16):
        out[j // 2, seq, j % 2] = ref[span_ref[seq, j]]


def tile_scores(q, k, low):
    scores = dot(q, k, 1, 1) * score_scale
    rows = lax.broadcasted_iota(jnp.int32, scores.shape, 0) % TILE + low
    keys = lax.broadcasted_iota(jnp.int32, scores.shape, 1)
    return jnp.where(keys <= rows, scores, -1e30)


QKV_MEMBERS = (
    (Member(0, 0, 32, 0, QUERY), Member(0, 0, 32, QUERY, KEY)),
    (Member(0, 32, 32, 0, QUERY),),
    (Member(0, 0, 64, QUERY + KEY, KEY), Member(0, 32, 32, QUERY, KEY)),
)
REST_MEMBERS = (
    (Member(1, 0, 64, FF, FF),),
    (Member(0, 0, 128, 0, WIDTH),),
    (Member(1, 0, 64, 0, FF), Member(2, 0, 192, 0, WIDTH)),
)
FRONT_COPIES = 260


def front_kernel(slot_ref, span_ref, x_ref, cos_ref, sin_ref, wq, wk, wv, wo, wg, wu, wd, gain_in,
                 wqkv_out, wo_out, wgu_out, wd_out, gain_out, q_raw_ref, k_raw_ref, qkv_out, lse_ref, heads_out,
                 w_s, gain_s, sent_s, qkv_0, qkv_1, q_s, k_s, v_s, o_s, out_s, heads_s, local_sem, send, recv):
    place = torus_place()
    core, y, lo = place["core"], place["y"], place["x"] % 2
    me = lax.axis_index("ctx")
    copies = Copies(send, recv, FRONT_COPIES)
    own_w = w_s.at[:, :, core]
    greet([device_at(shifted(place, axis, by)) for axis in "xyz" for by in (1, -1)] + [other_core(place)]
          + [ctx_device(o) for o in range(1, 8)])
    starts = []
    for i, (shard, out, first) in enumerate((
            (wq, own_w, 0), (wk, own_w, QUERY), (wv, own_w, QUERY + KEY),
            (wo, wo_out, 0), (wg, wgu_out, 0), (wu, wgu_out, FF), (wd, wd_out, 0))):
        whole = Member(0, 0, shard.shape[0], 0, shard.shape[1])
        at = Member(0, 0, shard.shape[0], first, shard.shape[1]).block(place["x"], place["z"])
        copy = pltpu.make_async_copy(shard.at[:, whole.block(place["x"], place["z"])], out.at[y, lo, :, at], local_sem.at[i])
        copy.start()
        starts.append(copy)
    own_gain = gain_s.at[y, lo, core]
    gain_copy = pltpu.make_async_copy(gain_in, own_gain, local_sem.at[7])
    gain_copy.start()
    for copy in starts:
        copy.wait()
    gain_copy.wait()

    def gain_steps():
        slots = copies.slot(5)
        for k, by in enumerate((1, -1)):
            copies.start(slots[k], own_gain, own_gain, device_at(shifted(place, "y", by)))
        yield
        for k, by in enumerate((1, -1)):
            copies.arrived(slots[k], gain_s.at[(y - by) % 4, lo, core], device_at(shifted(place, "y", -by)))
        behind = gain_s.at[(y - 1) % 4, lo, core]
        copies.start(slots[2], behind, behind, device_at(shifted(place, "y", 1)))
        yield
        copies.arrived(slots[2], gain_s.at[(y + 2) % 4, lo, core], device_at(shifted(place, "y", -1)))
        across = device_at({**place, "x": place["x"] // 2 * 2 + (1 - lo)})
        copies.start(slots[3], gain_s.at[:, lo, core], gain_s.at[:, lo, core], across)
        yield
        copies.arrived(slots[3], gain_s.at[:, 1 - lo, core], across)
        yield

    first = [gather_part(copies, place, ORDERS[p], QKV_MEMBERS[p], [own_w]) for p in range(3)] + [gain_steps()]
    rest = [gather_part(copies, place, ORDERS[p], REST_MEMBERS[p], [wo_out, wgu_out, wd_out]) for p in range(3)]
    for step in range(6):
        advance(first)
        if step in (0, 1, 4, 5):
            advance(rest)
    run(first)
    advance(rest)
    sibling = other_core(place)
    pair_slots = copies.slot(2)
    copies.start(pair_slots[0], gain_s.at[:, :, core], gain_s.at[:, :, core], sibling)
    copies.start(pair_slots[1], own_w, own_w, sibling)
    copies.arrived(pair_slots[0], gain_s.at[:, :, 1 - core], sibling)
    copies.arrived(pair_slots[1], w_s.at[:, :, 1 - core], sibling)
    keep = pltpu.make_async_copy(w_s, wqkv_out, local_sem.at[0])
    keep.start()

    x = x_ref[...]

    def block(n, carry):
        at = pl.ds(pl.multiple_of(n * 512, 512), 512)
        q_raw_ref[:, at] = dot(x, w_s[:, :, :, :, at].reshape(WIDTH, 512), 1, 0)
        return carry

    lax.fori_loop(0, 4, block, 0)
    for n in range(2):
        at = slice(n * 512, (n + 1) * 512)
        k_raw_ref[:, at] = dot(x, w_s[:, :, :, :, QUERY + n * 512:QUERY + (n + 1) * 512].reshape(WIDTH, 512), 1, 0)
    for n in range(2):
        value = dot(x, w_s[:, :, :, :, QUERY + KEY + n * 512:QUERY + KEY + (n + 1) * 512].reshape(WIDTH, 512), 1, 0).astype(BF16)
        for h in range(4):
            sent_s[4 * n + h, :, :, :, 3 * HEAD:] = value[:, h * HEAD:(h + 1) * HEAD].reshape(2, 2, SPAN, HEAD)
    cosine, sine = cos_ref[...], sin_ref[...]

    def place_heads(raw_ref, gain_of, heads, column, each):
        inverse = inverse_rms(raw_ref[...])
        for h in range(heads):
            normed = raw_ref[:, h * HEAD:(h + 1) * HEAD] * inverse * gain_of(h)
            turned = normed * cosine + pltpu.roll(normed, HEAD // 2, 1) * sine
            first = column + h % each * HEAD
            sent_s[h // each, :, :, :, first:first + HEAD] = turned.astype(BF16).reshape(2, 2, SPAN, HEAD)

    place_heads(q_raw_ref, lambda h: gain_s[h // 4, h // 2 % 2, h % 2, 0:1], HEADS, 0, 2)
    place_heads(k_raw_ref, lambda h: gain_s[h // 2, h % 2, 0, 1:2] + gain_s[h // 2, h % 2, 1, 1:2], KV_HEADS, 2 * HEAD, 1)

    there, own = {}, []
    qkv_s = (qkv_0, qkv_1)
    for seq in range(2):
        own.append(pltpu.make_async_copy(sent_s.at[me, seq], qkv_s[seq].at[pl.ds(2 * me, 2)], local_sem.at[1 + seq]))
        own[seq].start()
        for o in range(1, 8):
            there[seq, o] = copies.slot(1)[0]
            copies.start(there[seq, o], sent_s.at[(me + o) % 8, seq], qkv_s[seq].at[pl.ds(2 * me, 2)], ctx_device(o))
    back, kept = {}, [keep]
    for seq in range(2):
        own[seq].wait()
        for o in range(1, 8):
            copies.arrived(there[seq, o], qkv_s[seq].at[pl.ds(2 * ((me - o) % 8), 2)], ctx_device(-o))
        kept.append(pltpu.make_async_copy(qkv_s[seq], qkv_out.at[seq], local_sem.at[3 + seq]))
        kept[-1].start()
        sorted_blocks(slot_ref, seq, qkv_s[seq], (q_s.at[0], q_s.at[1], k_s, v_s))
        for i in range(LENGTH // TILE):
            low, high = i * TILE, (i + 1) * TILE
            q = q_s[:, low:high, :].reshape(2 * TILE, HEAD)
            scores = tile_scores(q, k_s[:high], low)
            top = jnp.max(scores, -1, keepdims=True)
            raised = jnp.exp(scores - top)
            total = jnp.sum(raised, -1, keepdims=True)
            probs = (raised * (1.0 / total)).astype(BF16)
            out = dot(probs, v_s[:high], 1, 0).astype(BF16).reshape(2, TILE // SPAN, SPAN, HEAD)
            for h in range(2):
                o_s[low // SPAN:high // SPAN, :, h * HEAD:(h + 1) * HEAD] = out[h]
            lse_ref[seq, :, low:high, :] = jnp.broadcast_to(top + jnp.log(total), (2 * TILE, HEAD)).reshape(2, TILE, HEAD)
        sent_blocks(span_ref, seq, o_s, out_s)
        for o in range(1, 8):
            back[seq, o] = copies.slot(1)[0]
            copies.start(back[seq, o], out_s.at[(me + o) % 8, seq], heads_s.at[me, seq], ctx_device(o))
        if seq == 0:
            advance(rest)
    own = pltpu.make_async_copy(out_s.at[me], heads_s.at[me], local_sem.at[1])
    own.start()
    kept.append(pltpu.make_async_copy(gain_s, gain_out, local_sem.at[2]))
    kept[-1].start()
    run(rest)
    for seq in range(2):
        for o in range(1, 8):
            copies.arrived(back[seq, o], heads_s.at[(me - o) % 8, seq], ctx_device(-o))
    own.wait()
    kept.append(pltpu.make_async_copy(heads_s, heads_out, local_sem.at[5]))
    kept[-1].start()
    for copy in kept:
        copy.wait()
    copies.finish()


def front(slot_of, span_order, rows, cosine, sine, shards, gain_tile):
    return pl.pallas_call(
        front_kernel,
        in_specs=[SMEM, SMEM] + vmem(3) + anywhere(8),
        out_specs=anywhere(5) + vmem(2) + anywhere(1) + vmem(1) + anywhere(1),
        out_shape=[jax.ShapeDtypeStruct((4, 2, 2, 64, QKV), BF16), jax.ShapeDtypeStruct((4, 2, 128, WIDTH), BF16),
                   jax.ShapeDtypeStruct((4, 2, 64, 2 * FF), BF16), jax.ShapeDtypeStruct((4, 2, 192, WIDTH), BF16),
                   jax.ShapeDtypeStruct((4, 2, 2, 8, 128), F32), jax.ShapeDtypeStruct((ROWS, QUERY), F32), jax.ShapeDtypeStruct((ROWS, KEY), F32),
                   jax.ShapeDtypeStruct((2, 16, SPAN, 4 * HEAD), BF16), jax.ShapeDtypeStruct((2, 2, LENGTH, HEAD), F32),
                   jax.ShapeDtypeStruct((8, 2, 2, SPAN, 2 * HEAD), BF16)],
        scratch_shapes=[pltpu.VMEM((4, 2, 2, 64, QKV), BF16), pltpu.VMEM((4, 2, 2, 8, 128), F32), pltpu.VMEM((8, 2, 2, SPAN, 4 * HEAD), BF16),
                        pltpu.VMEM((16, SPAN, 4 * HEAD), BF16), pltpu.VMEM((16, SPAN, 4 * HEAD), BF16), pltpu.VMEM((2, LENGTH, HEAD), BF16), pltpu.VMEM((LENGTH, HEAD), BF16),
                        pltpu.VMEM((LENGTH, HEAD), BF16), pltpu.VMEM((16, SPAN, 2 * HEAD), BF16), pltpu.VMEM((8, 2, 2, SPAN, 2 * HEAD), BF16),
                        pltpu.VMEM((8, 2, 2, SPAN, 2 * HEAD), BF16), pltpu.SemaphoreType.DMA((8,)),
                        pltpu.SemaphoreType.DMA((FRONT_COPIES,)), pltpu.SemaphoreType.DMA((FRONT_COPIES,))],
        compiler_params=pltpu.CompilerParams(collective_id=1, has_side_effects=True, vmem_limit_bytes=60 << 20),
        cost_estimate=pl.CostEstimate(flops=4000000000, bytes_accessed=60 << 20, transcendentals=3 << 20),
        name="front",
    )(slot_of, span_order, rows, cosine, sine, *shards, gain_tile)


MIDDLE_COPIES = 40


def middle_kernel(heads_ref, x_ref, cot_ref, ag_ref, fg_ref, wo_own, wgu_own, wd_own,
                  layer_ref, grad_mixed_ref, gains_ref, grad_heads_out, out_grad, gu_grad, down_grad,
                  wo_s, wgu_s, wd_s, att_s, gu_s, branch_s, mixed_s, low_s, mid_s, ffn_s, att_t, mix_t, mid_t,
                  grad_branch_s, grad_gu_s, grad_ffn_s, sent_s, heads_s, local_sem, free_sem, send, recv):
    place = torus_place()
    core, sibling = place["core"], other_core(place)
    me = lax.axis_index("ctx")
    copies = Copies(send, recv, MIDDLE_COPIES)
    greet([sibling] + [ctx_device(o) for o in range(1, 8)])
    pieces = [(wo_own, wo_s, slice(None))]
    for n in range(FF // 512):
        pieces += [(wgu_own, wgu_s, slice(n * 512, (n + 1) * 512)), (wgu_own, wgu_s, slice(FF + n * 512, FF + (n + 1) * 512))]
    pieces += [(wd_own, wd_s, slice(None))]
    slots, here = copies.slot(len(pieces)), []
    for i, (own, buffer, at) in enumerate(pieces):
        copies.start(slots[i], own.at[:, :, at], buffer.at[:, core, :, at], sibling)
        copy = pltpu.make_async_copy(own.at[:, :, at], buffer.at[:, core, :, at], local_sem.at[i])
        copy.start()
        here.append(copy)

    def ready(i):
        _, buffer, at = pieces[i]
        here[i].wait()
        copies.arrived(slots[i], buffer.at[:, 1 - core, :, at], sibling)

    for g in range(8):
        att_s[:, g * 256:(g + 1) * 256] = heads_ref[g].reshape(ROWS, 256)
    store_stripes(att_s[...], att_t, QUERY)
    ready(0)
    for n in range(2):
        at = slice(n * 512, (n + 1) * 512)
        branch_s[:, at] = dot(att_s[...], wo_s[:, :, :, at].reshape(QUERY, 512), 1, 0)
    branch_inverse = inverse_rms(branch_s[...])
    mixed = x_ref[...].astype(F32) + branch_s[...] * branch_inverse * ag_ref[...]
    mixed_s[...] = mixed
    low_s[...] = mixed.astype(BF16)
    store_stripes(low_s[...], mix_t, WIDTH)
    for n in range(FF // 512):
        at, up_at = slice(n * 512, (n + 1) * 512), slice(FF + n * 512, FF + (n + 1) * 512)
        ready(1 + 2 * n)
        ready(2 + 2 * n)
        gate = dot(low_s[...], wgu_s[:, :, :, at].reshape(WIDTH, 512), 1, 0)
        up = dot(low_s[...], wgu_s[:, :, :, up_at].reshape(WIDTH, 512), 1, 0)
        gu_s[:, at] = gate
        gu_s[:, up_at] = up
        mid_s[:, at] = (gate * jax.nn.sigmoid(gate) * up).astype(BF16)
    store_stripes(mid_s[...], mid_t, FF)
    ready(len(pieces) - 1)
    for n in range(2):
        at = slice(n * 512, (n + 1) * 512)
        ffn_s[:, at] = dot(mid_s[...], wd_s[:, :, :, at].reshape(FF, 512), 1, 0)
    ffn_out = ffn_s[...]
    ffn_inverse = inverse_rms(ffn_out)
    layer_ref[...] = (mixed_s[...] + ffn_out * ffn_inverse * fg_ref[...]).astype(BF16)
    grad_ffn, grad_ffn_gain = rms_back(ffn_out, ffn_inverse, fg_ref[...], cot_ref[...].astype(F32))
    grad_ffn_s[...] = grad_ffn.astype(BF16)

    def backward_block(n, carry):
        at = pl.ds(pl.multiple_of(n * 768, 256), 768)
        up_at = pl.ds(pl.multiple_of(FF + n * 768, 256), 768)
        grad_middle = dot(grad_ffn_s[...], wd_s[pl.ds(n * 2, 2)].reshape(768, WIDTH), 1, 1)
        gate, up = gu_s[:, at], gu_s[:, up_at]
        sigmoid_gate = jax.nn.sigmoid(gate)
        grad_gu_s[:, at] = (grad_middle * up * sigmoid_gate * (1.0 + gate * (1.0 - sigmoid_gate))).astype(BF16)
        grad_gu_s[:, up_at] = (grad_middle * (gate * sigmoid_gate)).astype(BF16)
        return carry

    lax.fori_loop(0, 4, backward_block, 0)

    def sibling_half(k, turned, grad, buffer):
        pl.semaphore_signal(free_sem.at[k], inc=1, device_id=sibling, device_id_type=MESH)
        stripes = turned[:, 1 - core]
        stripes = stripes.reshape(8 * stripes.shape[1], ROWS)
        for n in range(buffer.shape[3] // 512):
            at = slice(n * 512, (n + 1) * 512)
            buffer[:, 1, :, at] = dot(stripes, grad[:, at], 1, 0).astype(BF16).reshape(8, -1, 512)
        pl.semaphore_wait(free_sem.at[k], 1)
        slot = copies.slot(1)[0]
        copies.start(slot, buffer.at[:, 1], buffer.at[:, 0], sibling)
        return slot

    def own_half(slot, k, turned, grad, buffer, out):
        stripes = turned[:, core]
        stripes = stripes.reshape(8 * stripes.shape[1], ROWS)
        copies.arrived(slot, buffer.at[:, 0], sibling)
        for n in range(buffer.shape[3] // 512):
            at = slice(n * 512, (n + 1) * 512)
            total = dot(stripes, grad[:, at], 1, 0) + buffer[:, 0, :, at].reshape(stripes.shape[0], 512).astype(F32)
            buffer[:, 0, :, at] = total.astype(BF16).reshape(8, -1, 512)
        copy = pltpu.make_async_copy(buffer.at[:, 0], out, local_sem.at[k])
        copy.start()
        return copy

    down_slot = sibling_half(0, mid_t, grad_ffn_s, wd_s)
    for n in range(4):
        at = slice(n * 256, (n + 1) * 256)
        ffn_s[:, at] = cot_ref[:, at].astype(F32) + dot(grad_gu_s[...], wgu_s[2 * n:2 * n + 2].reshape(256, 2 * FF), 1, 1)
    grad_mixed_ref[...] = ffn_s[...]
    grad_branch, grad_attn_gain = rms_back(branch_s[...], branch_inverse, ag_ref[...], ffn_s[...])
    grad_branch_s[...] = grad_branch.astype(BF16)
    for g in range(8):
        grad = dot(grad_branch_s[...], wo_s[g].reshape(256, WIDTH), 1, 1)
        sent_s[g] = grad.astype(BF16).reshape(2, 128, 256)
    own = pltpu.make_async_copy(sent_s.at[me], heads_s.at[me], local_sem.at[3])
    own.start()
    there = copies.slot(7)
    for o in range(1, 8):
        copies.start(there[o - 1], sent_s.at[(me + o) % 8], heads_s.at[me], ctx_device(o))
    gains_ref[...] = jnp.zeros_like(gains_ref)
    gains_ref[0:1] = grad_attn_gain
    gains_ref[1:2] = grad_ffn_gain
    gu_slot = sibling_half(1, mix_t, grad_gu_s, wgu_s)
    out_slot = sibling_half(2, att_t, grad_branch_s, wo_s)
    kept = [own_half(down_slot, 0, mid_t, grad_ffn_s, wd_s, down_grad)]
    own.wait()
    for o in range(1, 8):
        copies.arrived(there[o - 1], heads_s.at[(me - o) % 8], ctx_device(-o))
    kept.append(pltpu.make_async_copy(heads_s, grad_heads_out, local_sem.at[4]))
    kept[-1].start()
    kept.append(own_half(gu_slot, 1, mix_t, grad_gu_s, wgu_s, gu_grad))
    kept.append(own_half(out_slot, 2, att_t, grad_branch_s, wo_s, out_grad))
    for copy in kept:
        copy.wait()
    copies.finish()


def middle(heads, rows, cotangent, a_gain, f_gain, wo, wgu, wd):
    return pl.pallas_call(
        middle_kernel,
        in_specs=vmem(5) + anywhere(3),
        out_specs=vmem(3) + anywhere(4),
        out_shape=[jax.ShapeDtypeStruct((ROWS, WIDTH), BF16), jax.ShapeDtypeStruct((ROWS, WIDTH), F32), jax.ShapeDtypeStruct((8, WIDTH), F32),
                   jax.ShapeDtypeStruct((8, 2, 128, 256), BF16), jax.ShapeDtypeStruct((8, 128, WIDTH), BF16),
                   jax.ShapeDtypeStruct((8, 64, 2 * FF), BF16), jax.ShapeDtypeStruct((8, 192, WIDTH), BF16)],
        scratch_shapes=[pltpu.VMEM((8, 2, 128, WIDTH), BF16), pltpu.VMEM((8, 2, 64, 2 * FF), BF16), pltpu.VMEM((8, 2, 192, WIDTH), BF16),
                        pltpu.VMEM((ROWS, QUERY), BF16), pltpu.VMEM((ROWS, 2 * FF), F32), pltpu.VMEM((ROWS, WIDTH), F32), pltpu.VMEM((ROWS, WIDTH), F32),
                        pltpu.VMEM((ROWS, WIDTH), BF16), pltpu.VMEM((ROWS, FF), BF16), pltpu.VMEM((ROWS, WIDTH), F32),
                        pltpu.VMEM((8, 2, 128, ROWS), BF16), pltpu.VMEM((8, 2, 64, ROWS), BF16), pltpu.VMEM((8, 2, 192, ROWS), BF16),
                        pltpu.VMEM((ROWS, WIDTH), BF16), pltpu.VMEM((ROWS, 2 * FF), BF16), pltpu.VMEM((ROWS, WIDTH), BF16),
                        pltpu.VMEM((8, 2, 128, 256), BF16), pltpu.VMEM((8, 2, 128, 256), BF16),
                        pltpu.SemaphoreType.DMA((16,)), pltpu.SemaphoreType.REGULAR((3,)),
                        pltpu.SemaphoreType.DMA((MIDDLE_COPIES,)), pltpu.SemaphoreType.DMA((MIDDLE_COPIES,))],
        compiler_params=pltpu.CompilerParams(collective_id=3, has_side_effects=True, vmem_limit_bytes=60 << 20),
        cost_estimate=pl.CostEstimate(flops=18000000000, bytes_accessed=40 << 20, transcendentals=3 << 20),
        name="middle",
    )(heads, rows, cotangent, a_gain, f_gain, wo, wgu, wd)


def regions(place, axis, at, whole, columns, rows, first=0):
    here = {**place, axis: at}
    step = columns // 8
    row = pl.ds(rows[0], rows[1])
    ys = pl.ds(0, 4) if "y" in whole else pl.ds(here["y"], 1)
    los = pl.ds(0, 2) if "x" in whole else pl.ds(here["x"] % 2, 1)
    if "x" in whole and "z" in whole:
        return [(ys, los, row, pl.ds(first, columns))]
    if "z" in whole:
        return [(ys, los, row, pl.ds(pl.multiple_of(first + here["x"] // 2 * (4 * step), 128), 4 * step))]
    his = [0, 1] if "x" in whole else [here["x"] // 2]
    return [(ys, los, row, pl.ds(pl.multiple_of(first + (hi * 4 + here["z"]) * step, 128), step)) for hi in his]


GATHER_ORDER = ("xyz", "yzx", "zxy")


def add_region(acc, temp, at, extra=()):
    ys, los, rows, columns = at
    chunk = 32
    per = rows.size // chunk

    def one(step, carry):
        del carry
        row = step % per * chunk
        lo = step // per % los.size
        y = step // (per * los.size)

        def view(ref, where):
            r = pl.ds(pl.multiple_of(where[2].start + row, 16), chunk)
            return ref.at[where[0].start + y, where[1].start + lo, r, where[3]]

        total = view(acc, at)[...].astype(jnp.float32)
        for t in extra:
            total += view(temp, t)[...].astype(jnp.float32)
        view(acc, at)[...] = total.astype(jnp.bfloat16)
        return 0

    lax.fori_loop(0, per * los.size * ys.size, one, 0)


def reduce_kernel(members, count, *refs):
    n = 1 + max(m[1] for m in members)
    grads, gain_in = refs[:n], refs[n]
    outs, gain_out = refs[n + 1:2 * n + 1], refs[2 * n + 1]
    accs, temps = refs[2 * n + 2:3 * n + 2], refs[3 * n + 2:4 * n + 2]
    gain_rings, local_sem, send, recv = refs[4 * n + 2:]
    place = torus_place()
    copies = Copies(send, recv, count)
    loads = []
    for i in range(n):
        load = pltpu.make_async_copy(grads[i], accs[i], local_sem.at[i])
        load.start()
        loads.append(load)
    barrier = pltpu.get_barrier_semaphore()
    far = device_at(shifted(place, "x", 2))
    sibling = device_at({**place, "core": 1 - place["core"]})
    others = [device_at(shifted(place, axis, by)) for axis in "xyz" for by in (1, -1)] + [far, sibling]
    for other in others:
        pl.semaphore_signal(barrier, inc=1, device_id=other, device_id_type=MESH)
    pl.semaphore_wait(barrier, len(others))
    parts = [[m for m in members if m[0] == part] for part in range(3)]

    def blocks(member, phase, at, half, landing):
        part, array, first, columns = member
        order = GATHER_ORDER[part]
        rows = accs[array].shape[2] // 2
        here = place
        if landing:
            for axis in order[phase + 1:]:
                here = shifted(here, axis, 1 if half else -1)
        return regions(here, order[phase], at % 4, order[:phase], columns, (half * rows, rows), first)

    def send_block(phase, part, at, half, by, land_at, slots):
        slots = iter(slots)
        device = device_at(shifted(place, GATHER_ORDER[part][phase], by))
        for m in parts[part]:
            for src, dst in zip(blocks(m, phase, at, half, False), blocks(m, phase, land_at, half, True)):
                copies.start(next(slots), accs[m[1]].at[src], temps[m[1]].at[dst], device)

    def wait_block(phase, part, half, by, land_at, slots):
        slots = iter(slots)
        device = device_at(shifted(place, GATHER_ORDER[part][phase], -by))
        for m in parts[part]:
            for dst in blocks(m, phase, land_at, half, True):
                copies.make(next(slots), temps[m[1]].at[dst], temps[m[1]].at[dst], device).wait_recv()

    def add_block(phase, part, at, half, land_ats):
        for m in parts[part]:
            where = blocks(m, phase, at, half, False)
            landed = [blocks(m, phase, land_at, half, True) for land_at in land_ats]
            for k, region in enumerate(where):
                add_region(accs[m[1]], temps[m[1]], region, [t[k] for t in landed])

    load = pltpu.make_async_copy(gain_in, gain_rings.at[0, place["core"]], local_sem.at[n])
    load.start()
    load.wait()
    slot = copies.slot(1)[0]
    copies.start(slot, gain_rings.at[0, place["core"]], gain_rings.at[0, place["core"]], sibling)
    copies.make(slot, gain_rings.at[0, 1 - place["core"]], gain_rings.at[0, 1 - place["core"]], sibling).wait_recv()
    gain_total = gain_rings[0, 0] + gain_rings[0, 1]

    for phase in (2, 1, 0):
        slots = {}
        for part in range(3):
            c = place[GATHER_ORDER[part][phase]]
            pieces = sum(len(blocks(m, phase, c, 0, False)) for m in parts[part])
            if phase == 2:
                for m in parts[part]:
                    if loads[m[1]] is not None:
                        loads[m[1]].wait()
                        loads[m[1]] = None
            for by in (1, -1):
                half = 0 if by == 1 else 1
                slots[part, by] = [copies.slot(pieces) for _ in range(3)]
                send_block(phase, part, c + 2, half, by, c + 2, slots[part, by][0])
            for by in (1, -1):
                half = 0 if by == 1 else 1
                send_block(phase, part, c + by, 1 - half, by, c + by if by == 1 else c + 1, slots[part, by][1])
        axis, ring = "zyx"[2 - phase], gain_rings.at[3 - phase]
        at = place[axis]
        ring[at] = gain_total
        gain_slots = copies.slot(3)
        for k, by in enumerate((1, -1)):
            copies.start(gain_slots[k], ring.at[at], ring.at[at], device_at(shifted(place, axis, by)))
        for part in range(3):
            c = place[GATHER_ORDER[part][phase]]
            for by in (1, -1):
                half = 0 if by == 1 else 1
                wait_block(phase, part, half, by, c + by, slots[part, by][0])
                add_block(phase, part, c + by, half, [c + by])
                send_block(phase, part, c + by, half, by, c + by if by == 1 else c + 1, slots[part, by][2])
        for k, by in enumerate((1, -1)):
            view = ring.at[(at - by) % 4]
            copies.make(gain_slots[k], view, view, device_at(shifted(place, axis, -by))).wait_recv()
        copies.start(gain_slots[2], ring.at[(at - 1) % 4], ring.at[(at - 1) % 4], device_at(shifted(place, axis, 1)))
        for part in range(3):
            c = place[GATHER_ORDER[part][phase]]
            for half in (0, 1):
                for by in (1, -1):
                    first = half == (0 if by == 1 else 1)
                    wait_block(phase, part, half, by, c if by == 1 else c + 2, slots[part, by][2 if first else 1])
                add_block(phase, part, c, half, [c, c + 2])
        view = ring.at[(at + 2) % 4]
        copies.make(gain_slots[2], view, view, device_at(shifted(place, axis, -1))).wait_recv()
        gain_total = (ring[0] + ring[1]) + (ring[2] + ring[3])
    gain_out[...] = gain_total
    finish_kernel(members, accs, outs, place, copies, local_sem)
    assert copies.used <= count, copies.used


def finish_kernel(members, accs, outs, place, copies, local_sem):
    n = len(members)

    def columns(i, x, z):
        _, _, first, width = members[i]
        step = width // 8
        return pl.ds(pl.multiple_of(first + ((x % 4) // 2 * 4 + z % 4) * step, 128), step)

    def block(i, x, z):
        return outs[members[i][1]].at[:, columns(i, x, z)]

    def halves(i, x, z, half):
        rows = outs[members[i][1]].shape[0] // 2
        return outs[members[i][1]].at[pl.ds(half * rows, rows), columns(i, x, z)]

    x, z = place["x"], place["z"]
    stores = []
    for i in range(n):
        store = pltpu.make_async_copy(accs[members[i][1]].at[place["y"], x % 2, :, columns(i, x, z)], block(i, x, z), local_sem.at[i])
        store.start()
        stores.append(store)
    for store in stores:
        store.wait()
    far = device_at(shifted(place, "x", 2))
    up, down = device_at(shifted(place, "z", 1)), device_at(shifted(place, "z", -1))
    slots = {name: copies.slot(n) for name in ("far", "up", "down", "far_up", "far_down", "two_up", "two_down", "far_two_up", "far_two_down")}

    def send(name, view, device):
        for i in range(n):
            copies.start(slots[name][i], view(i), view(i), device)

    def wait(name, view, device):
        for i in range(n):
            copies.make(slots[name][i], view(i), view(i), device).wait_recv()

    send("far", lambda i: block(i, x, z), far)
    send("up", lambda i: block(i, x, z), up)
    send("down", lambda i: block(i, x, z), down)
    wait("far", lambda i: block(i, x + 2, z), far)
    send("far_up", lambda i: block(i, x + 2, z), up)
    send("far_down", lambda i: block(i, x + 2, z), down)
    wait("up", lambda i: block(i, x, z - 1), down)
    send("two_up", lambda i: halves(i, x, z - 1, 0), up)
    wait("down", lambda i: block(i, x, z + 1), up)
    send("two_down", lambda i: halves(i, x, z + 1, 1), down)
    wait("far_up", lambda i: block(i, x + 2, z - 1), down)
    send("far_two_up", lambda i: halves(i, x + 2, z - 1, 0), up)
    wait("far_down", lambda i: block(i, x + 2, z + 1), up)
    send("far_two_down", lambda i: halves(i, x + 2, z + 1, 1), down)
    wait("two_up", lambda i: halves(i, x, z + 2, 0), down)
    wait("two_down", lambda i: halves(i, x, z + 2, 1), up)
    wait("far_two_up", lambda i: halves(i, x + 2, z + 2, 0), down)
    wait("far_two_down", lambda i: halves(i, x + 2, z + 2, 1), up)
    copies.finish()


def reduce_grads(grads, gain_grads, members, collective_id, count):
    shapes = [g.shape for g in grads]
    return pl.pallas_call(
        functools.partial(reduce_kernel, members, count),
        out_shape=[jax.ShapeDtypeStruct(s[2:], jnp.bfloat16) for s in shapes] + [jax.ShapeDtypeStruct(gain_grads.shape, jnp.float32)],
        in_specs=[pl.BlockSpec(memory_space=pl.ANY)] * (len(grads) + 1),
        out_specs=[pl.BlockSpec(memory_space=pl.ANY)] * len(grads) + [pl.BlockSpec(memory_space=pltpu.VMEM)],
        scratch_shapes=[pltpu.VMEM(s, jnp.bfloat16) for s in shapes] * 2
        + [pltpu.VMEM((4, 4) + gain_grads.shape, jnp.float32), pltpu.SemaphoreType.DMA((8,)),
           pltpu.SemaphoreType.DMA((count,)), pltpu.SemaphoreType.DMA((count,))],
        compiler_params=pltpu.CompilerParams(collective_id=collective_id, has_side_effects=True, vmem_limit_bytes=50 << 20),
        name="reduce_grads",
    )(*grads, gain_grads)


def gather_sorted(order_ref, seq, ref, column, width, out, out_at):
    for j in range(16):
        slot = order_ref[seq, j]
        rows = ref[slot // 2, 0, pl.ds(slot % 2 * SPAN, SPAN), column:column + width]
        out[out_at + j * SPAN:out_at + (j + 1) * SPAN, :] = rows


def backward_kernel(order_ref, qkv_ref, grad_ref, lse_ref, out_ref, q_s, k_s, v_s, g_s, dk_s, dv_s):
    seq = pl.program_id(0)
    gather_sorted(order_ref, seq, qkv_ref, 0, HEAD, q_s.at[0], 0)
    gather_sorted(order_ref, seq, qkv_ref, HEAD, HEAD, q_s.at[1], 0)
    gather_sorted(order_ref, seq, qkv_ref, 2 * HEAD, HEAD, k_s, 0)
    gather_sorted(order_ref, seq, qkv_ref, 3 * HEAD, HEAD, v_s, 0)
    gather_sorted(order_ref, seq, grad_ref, 0, HEAD, g_s.at[0], 0)
    gather_sorted(order_ref, seq, grad_ref, HEAD, HEAD, g_s.at[1], 0)
    tiles = 1024 // TILE
    for i in reversed(range(tiles)):
        low, high = i * TILE, (i + 1) * TILE
        q = q_s[:, low:high, :].reshape(2 * TILE, HEAD)
        g = g_s[:, low:high, :].reshape(2 * TILE, HEAD)
        k, v = k_s[:high], v_s[:high]
        lse = lse_ref[0, :, low:high, :].reshape(2 * TILE, HEAD)[:, :1]
        probs = jnp.exp(tile_scores(q, k, low) - lse)
        grad_probs = dot(g, v, 1, 1)
        inner = jnp.sum(probs * grad_probs, -1, keepdims=True)
        grad_scores = (probs * (grad_probs - inner)).astype(jnp.bfloat16)
        probs_low = probs.astype(jnp.bfloat16)
        dq = (dot(grad_scores, k, 1, 0) * score_scale).astype(jnp.bfloat16)
        dk = dot(grad_scores, q, 0, 0)
        dv = dot(probs_low, g, 0, 0)
        if i == tiles - 1:
            dk_s[...] = dk
            dv_s[...] = dv
        else:
            dk_s[:high] += dk
            dv_s[:high] += dv
        for j in range(TILE // SPAN):
            slot = order_ref[seq, low // SPAN + j]
            for h in range(2):
                out_ref[slot // 2, 0, pl.ds(slot % 2 * SPAN, SPAN), h * HEAD:(h + 1) * HEAD] = dq[
                    h * TILE + j * SPAN:h * TILE + (j + 1) * SPAN]
    for j in range(16):
        slot = order_ref[seq, j]
        rows = pl.ds(slot % 2 * SPAN, SPAN)
        at = slice(j * SPAN, (j + 1) * SPAN)
        out_ref[slot // 2, 0, rows, 2 * HEAD:3 * HEAD] = (dk_s[at] * score_scale).astype(jnp.bfloat16)
        out_ref[slot // 2, 0, rows, 3 * HEAD:] = dv_s[at].astype(jnp.bfloat16)


def attention_backward(order, qkv, grad, lse):
    return pl.pallas_call(
        backward_kernel,
        grid_spec=pltpu.PrefetchScalarGridSpec(
            num_scalar_prefetch=1, grid=(2,),
            in_specs=[pl.BlockSpec((8, 1, 128, 4 * HEAD), lambda s, order: (0, s, 0, 0)),
                      pl.BlockSpec((8, 1, 128, 2 * HEAD), lambda s, order: (0, s, 0, 0)),
                      pl.BlockSpec((1, 2, 1024, HEAD), lambda s, order: (s, 0, 0, 0))],
            out_specs=pl.BlockSpec((8, 1, 128, 4 * HEAD), lambda s, order: (0, s, 0, 0)),
            scratch_shapes=[pltpu.VMEM((2, 1024, HEAD), jnp.bfloat16), pltpu.VMEM((1024, HEAD), jnp.bfloat16), pltpu.VMEM((1024, HEAD), jnp.bfloat16),
                            pltpu.VMEM((2, 1024, HEAD), jnp.bfloat16), pltpu.VMEM((1024, HEAD), jnp.float32), pltpu.VMEM((1024, HEAD), jnp.float32)]),
        out_shape=jax.ShapeDtypeStruct((8, 2, 128, 4 * HEAD), jnp.bfloat16),
        compiler_params=pltpu.CompilerParams(vmem_limit_bytes=40 << 20),
        cost_estimate=pl.CostEstimate(flops=3400000000, bytes_accessed=8 << 20, transcendentals=3 << 20),
        name="attention_backward",
    )(order, qkv, grad, lse)


def load_pair(own, sibling, buffer, core, sems):
    copies = [pltpu.make_async_copy(own, buffer.at[:, core], sems.at[0]),
              pltpu.make_async_copy(sibling, buffer.at[:, 1 - core], sems.at[1])]
    for copy in copies:
        copy.start()
    return copies


def wait_all_of(copies):
    for copy in copies:
        copy.wait()


def last_kernel(core_ref, grad_ref, q_raw_ref, k_raw_ref, mixed_ref, qg_ref, kg_ref, cos_ref, sin_ref, own_ref,
                tokens_ref, grad_out_ref, gains_ref, w_s, dy_s, sems):
    loads = [pltpu.make_async_copy(own_ref, w_s, sems.at[0])]
    loads[0].start()
    cosine, sine = cos_ref[...], sin_ref[...]

    def one(raw_ref, gain_ref, heads, column, each, out_at):
        width = heads * HEAD
        for h in range(heads):
            first = column + h % each * HEAD
            u = grad_ref[h // each, :, :, first:first + HEAD].reshape(ROWS, HEAD).astype(F32)
            dy_s[:, h * HEAD:(h + 1) * HEAD] = u * cosine - pltpu.roll(u, HEAD // 2, 1) * sine
        raw = raw_ref[...]
        grad, grad_gain = rms_back(raw, inverse_rms(raw), gain_ref[...], dy_s[:, :width])
        grad_out_ref[:, out_at:out_at + width] = grad.astype(BF16)
        return grad_gain

    q_gain = one(q_raw_ref, qg_ref, HEADS, 0, 2, 0)
    k_gain = one(k_raw_ref, kg_ref, KV_HEADS, 2 * HEAD, 1, QUERY)
    for g in range(8):
        grad_out_ref[:, QUERY + KEY + g * HEAD:QUERY + KEY + (g + 1) * HEAD] = grad_ref[g, :, :, 3 * HEAD:].reshape(ROWS, HEAD)
    gains_ref[...] = jnp.zeros_like(gains_ref)
    gains_ref[0:1] = q_gain[:, :WIDTH]
    gains_ref[1:2] = q_gain[:, WIDTH:]
    gains_ref[2:3] = k_gain
    wait_all_of(loads)
    for n in range(4):
        at = slice(n * 256, (n + 1) * 256)
        tokens_ref[:, at] = (mixed_ref[:, at] + dot(grad_out_ref[...], w_s[2 * n:2 * n + 2].reshape(256, 4096), 1, 1)).astype(BF16)


def last(core, grad, q_raw, k_raw, grad_mixed, q_gain, k_gain, cosine, sine, own):
    return pl.pallas_call(
        last_kernel,
        in_specs=[SMEM] + vmem(8) + anywhere(1),
        out_specs=vmem(3),
        out_shape=[jax.ShapeDtypeStruct((ROWS, WIDTH), BF16), jax.ShapeDtypeStruct((ROWS, 4096), BF16), jax.ShapeDtypeStruct((8, WIDTH), F32)],
        scratch_shapes=[pltpu.VMEM((8, 2, 64, 4096), BF16), pltpu.VMEM((ROWS, QUERY), F32), pltpu.SemaphoreType.DMA((2,))],
        compiler_params=pltpu.CompilerParams(vmem_limit_bytes=40 << 20),
        cost_estimate=pl.CostEstimate(flops=2200000000, bytes_accessed=16 << 20, transcendentals=0),
        name="last",
    )(core, grad, q_raw, k_raw, grad_mixed, q_gain, k_gain, cosine, sine, own)


MEMBERS = ((1, 0, 0, 2048), (2, 0, 2048, 1024), (2, 0, 3072, 1024), (0, 1, 0, 1024), (0, 2, 0, 3072), (1, 2, 3072, 3072), (2, 3, 0, 1024))


def angles(positions):
    steps_half = jnp.arange(HEAD // 2, dtype=jnp.float32)
    inverse_freq = rope_base ** (-2.0 * steps_half / HEAD)
    phase = positions.astype(jnp.float32)[..., None] * inverse_freq
    cosine, sine = jnp.cos(phase), jnp.sin(phase)
    return jnp.concatenate([cosine, cosine], -1), jnp.concatenate([-sine, sine], -1)


def to_sibling(array):
    return lax.ppermute(array, "fsdp", [(i, i ^ 1) for i in range(16)])


def weight_grad(own, sibling, grad_rows):
    count = own.shape[1]
    from_sibling = to_sibling(dot(sibling.reshape(8 * count, ROWS), grad_rows, 1, 0).astype(BF16))
    total = (dot(own.reshape(8 * count, ROWS), grad_rows, 1, 0) + from_sibling.astype(F32)).astype(BF16)
    return total.reshape(4, 2, count, total.shape[1])


def per_device(
    tokens,
    span_order,
    w_query,
    w_key,
    w_value,
    w_out,
    w_gate,
    w_up,
    w_down,
    query_gain,
    key_gain,
    attn_gain,
    ffn_gain,
    cotangent,
):
    seq_local, rows_local, width = tokens.shape
    span_rows = rows_local // 2
    at_fsdp = lax.axis_index("fsdp")
    core = (at_fsdp % 2).astype(jnp.int32).reshape(1)
    token_rows = tokens.reshape(ROWS, width)

    def gain_row(gain):
        blank = jnp.zeros_like(gain)
        return jnp.where(core[0] == 0, jnp.concatenate([gain, blank]), jnp.concatenate([blank, gain]))

    gain_tile = jnp.concatenate([jnp.stack([query_gain, gain_row(key_gain), gain_row(attn_gain), gain_row(ffn_gain)]), jnp.zeros((4, 128), F32)])
    own_spans = lax.dynamic_slice_in_dim(span_order, 2 * lax.axis_index("ctx"), 2, 1)
    offsets = jnp.arange(span_rows, dtype=jnp.int32)
    cosine, sine = angles((own_spans[:, :, None] * span_rows + offsets).reshape(ROWS))
    numbers = jnp.arange(16, dtype=jnp.int32)
    slot_of = jnp.sum(jnp.where(span_order[:, :, None] == numbers, numbers[None, :, None], 0), 1)

    def exchange(array):
        return lax.all_to_all(array, "ctx", split_axis=0, concat_axis=0, tiled=True)

    wqkv, wo, wgu, wd, gains_all, query_raw, key_raw, qkv, lse, heads = front(
        slot_of, span_order, token_rows, cosine, sine, (w_query, w_key, w_value, w_out, w_gate, w_up, w_down), gain_tile)
    wqkv = wqkv.reshape(8, 2, 64, QKV)
    heads = heads.reshape(8, 2, 128, 2 * HEAD)
    qkv = qkv.reshape(2, 8, 128, 4 * HEAD).transpose(1, 0, 2, 3)
    wo, wgu, wd = [w.reshape((8,) + w.shape[2:]) for w in (wo, wgu, wd)]
    q_gain_all = gains_all[:, :, :, 0].reshape(1, QUERY)
    k_gain_all, a_gain_all, f_gain_all = [(gains_all[:, :, 0, k] + gains_all[:, :, 1, k]).reshape(1, WIDTH) for k in (1, 2, 3)]
    by_stripe = token_rows.T.reshape(8, 2, 64, ROWS)
    tok_own, tok_sib = [lax.dynamic_index_in_dim(by_stripe, k, 1, keepdims=False) for k in (core[0], 1 - core[0])]
    layer_out, grad_mixed, gains_af, grad_heads, shard_out, shard_gu, shard_down = middle(
        heads, token_rows, cotangent.reshape(ROWS, width), a_gain_all, f_gain_all, wo, wgu, wd)
    shard_out, shard_gu, shard_down = [g.reshape((4, 2) + g.shape[1:]) for g in (shard_out, shard_gu, shard_down)]
    grad_qkv_heads = attention_backward(slot_of, qkv, grad_heads, lse)
    grad_tokens, grad_qkv, gains_qk = last(
        core, exchange(grad_qkv_heads), query_raw, key_raw, grad_mixed, q_gain_all, k_gain_all, cosine, sine, wqkv)
    shard_qkv = weight_grad(tok_own, tok_sib, grad_qkv)
    gain_grads = jnp.concatenate([gains_qk[:3], gains_af[:2], jnp.zeros((3, WIDTH), F32)])
    *totals, gain_totals = reduce_grads((shard_qkv, shard_out, shard_gu, shard_down), gain_grads, MEMBERS, 2, 400)
    qkv_total, out_total, gu_total, down_total = [t.astype(F32) for t in totals]
    gain_totals = gain_totals.reshape(-1)

    def own_gain(first, count):
        return lax.dynamic_slice_in_dim(gain_totals, first + at_fsdp * count, count)

    return (
        layer_out.reshape(tokens.shape),
        grad_tokens.reshape(tokens.shape),
        qkv_total[:, :QUERY],
        qkv_total[:, QUERY:QUERY + KEY],
        qkv_total[:, QUERY + KEY:],
        out_total,
        gu_total[:, :FF],
        gu_total[:, FF:],
        down_total,
        own_gain(0, 128),
        own_gain(2048, 64),
        own_gain(3072, 64),
        own_gain(4096, 64),
    )


def solution(mesh):
    rows, shard, gain = P("fsdp", "ctx", None), P("fsdp", None), P("fsdp")
    return jax.shard_map(
        per_device,
        mesh=mesh,
        in_specs=(rows, shard) + (shard,) * 7 + (gain,) * 4 + (rows,),
        out_specs=(rows, rows) + (shard,) * 7 + (gain,) * 4,
        check_vma=False,
    )
```

```python
import functools

import jax
import jax.numpy as jnp
import numpy as np
from jax import lax
from jax.experimental import pallas as pl
from jax.experimental.pallas import tpu as pltpu
from jax.sharding import PartitionSpec as P

MESH = pl.DeviceIdType.MESH
SMEM = pl.BlockSpec(memory_space=pltpu.SMEM)
BF16 = jnp.bfloat16
F32 = jnp.float32
HEADS = 16
KV_HEADS = 8
HEAD = 128
SPAN = 64
TILE = 256
LENGTH = 1024
ROWS = 256
WIDTH = 1024
QUERY = HEADS * HEAD
KEY = KV_HEADS * HEAD
QKV = QUERY + 2 * KEY
FF = 3072
rope_base = 1000000.0
norm_eps = 1e-06
score_scale = HEAD ** (-0.5)


def vmem(n):
    return [pl.BlockSpec(memory_space=pltpu.VMEM)] * n


def anywhere(n):
    return [pl.BlockSpec(memory_space=pl.ANY)] * n


def dot(a, b, a_dim, b_dim):
    return lax.dot_general(a, b, (((a_dim,), (b_dim,)), ((), ())), preferred_element_type=F32)


def torus_place():
    at_ctx, at_fsdp = lax.axis_index("ctx"), lax.axis_index("fsdp")
    x = at_ctx // 4 * 2 + at_fsdp // 2 % 2
    return {"x": x, "y": at_fsdp // 4, "z": at_ctx % 4, "core": at_fsdp % 2}


def device_at(place):
    at_ctx = place["x"] // 2 * 4 + place["z"]
    at_fsdp = place["y"] * 4 + place["x"] % 2 * 2 + place["core"]
    return (at_ctx, at_fsdp)


def shifted(place, axis, by):
    return {**place, axis: (place[axis] + by) % 4}


def other_core(place):
    return device_at({**place, "core": 1 - place["core"]})


def ctx_device(offset):
    return ((lax.axis_index("ctx") + offset) % 8, lax.axis_index("fsdp"))


def hail(others):
    barrier = pltpu.get_barrier_semaphore()
    for other in others:
        pl.semaphore_signal(barrier, inc=1, device_id=other, device_id_type=MESH)
    return lambda: pl.semaphore_wait(barrier, len(others))


def partners(place):
    near = [device_at(shifted(place, axis, by)) for axis, by in (("x", 1), ("x", -1), ("y", 1), ("y", -1), ("y", 2))]
    return near + [other_core(place)] + [ctx_device(o) for o in range(1, 8)]


class Copies:
    def __init__(self, send, recv, count):
        self.send, self.recv, self.count, self.used, self.sent = send, recv, count, 0, []

    def slot(self, count):
        first = self.used
        self.used += count
        assert self.used <= self.count, self.used
        return list(range(first, first + count))

    def make(self, slot, src, dst, device):
        return pltpu.make_async_remote_copy(
            src_ref=src, dst_ref=dst, send_sem=self.send.at[slot], recv_sem=self.recv.at[slot],
            device_id=device, device_id_type=MESH)

    def start(self, slot, src, dst, device):
        copy = self.make(slot, src, dst, device)
        copy.start()
        self.sent.append(copy)

    def arrived(self, slot, dst, device):
        self.make(slot, dst, dst, device).wait_recv()

    def finish(self):
        for copy in self.sent:
            copy.wait_send()
        self.sent = []


class Member:
    def __init__(self, array, row, rows, first, columns):
        self.array, self.row, self.rows, self.first, self.columns = array, row, rows, first, columns

    def half(self, half):
        return (self.row, self.rows) if half is None else (self.row + half * (self.rows // 2), self.rows // 2)

    def block(self, x, z):
        step = self.columns // 8
        return pl.ds(pl.multiple_of(self.first + ((x % 4) // 2 * 4 + z % 4) * step, 128), step)

    def regions(self, place, axis, at, whole, half):
        here = {**place, axis: at % 4}
        step = self.columns // 8
        row = pl.ds(*self.half(half))
        ys = pl.ds(0, 4) if "y" in whole else pl.ds(here["y"], 1)
        los = pl.ds(0, 2) if "x" in whole else pl.ds(here["x"] % 2, 1)
        if "x" in whole and "z" in whole:
            return [(ys, los, row, pl.ds(self.first, self.columns))]
        if "z" in whole:
            return [(ys, los, row, pl.ds(pl.multiple_of(self.first + here["x"] // 2 * (4 * step), 128), 4 * step))]
        his = [0, 1] if "x" in whole else [here["x"] // 2]
        return [(ys, los, row, pl.ds(pl.multiple_of(self.first + (hi * 4 + here["z"]) * step, 128), step)) for hi in his]


ORDERS = ("xyz", "yzx", "zxy")


def gather_part(copies, place, order, members, refs):
    core, sibling = place["core"], other_core(place)

    def views(axis, at, whole, half, of=core):
        return [refs[m.array].at[:, :, of].at[where] for m in members for where in m.regions(place, axis, at, whole, half)]

    def send(axis, at, whole, half, by, slots):
        for slot, view in zip(slots, views(axis, at, whole, half), strict=True):
            copies.start(slot, view, view, device_at(shifted(place, axis, by)))

    def wait(axis, at, whole, half, by, slots):
        for slot, view in zip(slots, views(axis, at, whole, half), strict=True):
            copies.arrived(slot, view, device_at(shifted(place, axis, -by)))

    def hand_over(axis, off, whole):
        for slot, view in zip(pair[off], views(axis, place[axis] + off, whole, None), strict=True):
            copies.start(slot, view, view, sibling)

    axis, c = order[0], place[order[0]]
    slots = {by: copies.slot(len(views(axis, c, "", None))) for by in (1, -1, 2)}
    for by in (1, -1, 2):
        send(axis, c, "", None, by, slots[by])
    yield
    for by in (1, -1, 2):
        wait(axis, c - by, "", None, by, slots[by])
    for phase in (1, 2):
        axis, whole, c = order[phase], order[:phase], place[order[phase]]
        pieces = len(views(axis, c, whole, None))
        slots = {(step, by): copies.slot(pieces) for step in (0, 1) for by in (1, -1)}
        for by in (1, -1):
            send(axis, c, whole, None, by, slots[0, by])
        if phase == 2:
            pair = {off: copies.slot(pieces) for off in (0, -1, 1, 2)}
            hand_over(axis, 0, whole)
        yield
        for by in (1, -1):
            wait(axis, c - by, whole, None, by, slots[0, by])
            send(axis, c - by, whole, 0 if by == 1 else 1, by, slots[1, by])
            if phase == 2:
                hand_over(axis, -by, whole)
        yield
        for by in (1, -1):
            wait(axis, c + 2, whole, 0 if by == 1 else 1, by, slots[1, by])
    hand_over(axis, 2, whole)
    yield
    for off in (0, -1, 1, 2):
        for slot, view in zip(pair[off], views(axis, place[axis] + off, whole, None, 1 - core), strict=True):
            copies.arrived(slot, view, sibling)


def run(steps):
    steps = list(steps)
    while steps:
        steps = [s for s in steps if next(s, "end") is None]


def advance(steps):
    for s in steps:
        next(s, None)


def inverse_rms(values):
    return lax.rsqrt(jnp.mean(values * values, -1, keepdims=True) + norm_eps)


def rms_back(values, inverse, norm_gain, upstream):
    scaled = upstream * norm_gain
    inner = jnp.mean(scaled * values, -1, keepdims=True)
    grad_gain = jnp.sum(upstream * values * inverse, 0, keepdims=True)
    return inverse * scaled - values * (inverse * inverse * inverse * inner), grad_gain


def store_stripes(rows, scratch, width):
    turned = rows.T
    stripe = width // 16
    for j in range(16):
        scratch[j // 2, j % 2] = turned[j * stripe:(j + 1) * stripe]


def sorted_blocks(slot_ref, seq, ref, first, outs):
    for j in range(16):
        block = ref[slot_ref[seq, j] + first]
        for k, out in enumerate(outs):
            out[j * SPAN:(j + 1) * SPAN, :] = block[:, k * HEAD:(k + 1) * HEAD]


def sent_blocks(span_ref, seq, ref, out):
    for j in range(16):
        out[j // 2, seq, j % 2] = ref[span_ref[seq, j]]


def tile_scores(q, k, low):
    scores = dot(q, k, 1, 1) * score_scale
    rows = lax.broadcasted_iota(jnp.int32, scores.shape, 0) % TILE + low
    keys = lax.broadcasted_iota(jnp.int32, scores.shape, 1)
    return jnp.where(keys <= rows, scores, -1e30)


QKV_MEMBERS = (
    (Member(0, 0, 32, 0, QUERY), Member(0, 0, 32, QUERY, KEY)),
    (Member(0, 32, 32, 0, QUERY),),
    (Member(0, 0, 64, QUERY + KEY, KEY), Member(0, 32, 32, QUERY, KEY)),
)
REST_MEMBERS = (
    (Member(1, 0, 64, FF, FF),),
    (Member(0, 0, 128, 0, WIDTH),),
    (Member(1, 0, 64, 0, FF),),
    (Member(2, 0, 192, 0, WIDTH),),
)
REST_ORDERS = ("xyz", "yzx", "zxy", "zxy")
FRONT_COPIES = 320
FRONT_POINTS = {"s0": (0, 1, 2, 3), "s1": (0, 1, 2, 3), "s2": (0, 1, 2, 3), "s4": (0, 1, 2, 3), "sent": (0, 1), "attended 0": (2, 3)}


def front_kernel(span_ref, x_ref, freq_ref, qg_ref, kg_ref, ag_ref, fg_ref, wq, wk, wv, wo, wg, wu, wd,
                 slot_ref, wqkv_out, wo_out, wgu_out, wd_out, gains_ref, cos_ref, sin_ref, q_raw_ref, k_raw_ref, qkv_out, lse_ref, heads_out,
                 w_s, gain_s, sent_s, qkv_0, qkv_1, q_s, k_s, v_s, o_s, out_s, heads_s, local_sem, send, recv):
    place = torus_place()
    core, y, lo = place["core"], place["y"], place["x"] % 2
    me = lax.axis_index("ctx")
    copies = Copies(send, recv, FRONT_COPIES)
    all_here = hail(partners(place))
    starts = []
    for i, (shard, out, first) in enumerate((
            (wq, w_s, 0), (wk, w_s, QUERY), (wv, w_s, QUERY + KEY),
            (wo, wo_out, 0), (wg, wgu_out, 0), (wu, wgu_out, FF), (wd, wd_out, 0))):
        whole = Member(0, 0, shard.shape[0], 0, shard.shape[1])
        at = Member(0, 0, shard.shape[0], first, shard.shape[1]).block(place["x"], place["z"])
        copy = pltpu.make_async_copy(shard.at[:, whole.block(place["x"], place["z"])], out.at[y, lo, core, :, at], local_sem.at[i])
        copy.start()
        starts.append(copy)
    own_gain = gain_s.at[y, lo, core]
    own_gain[0:1] = qg_ref[...]
    for k, gain_ref in enumerate((kg_ref, ag_ref, fg_ref)):
        blank = jnp.zeros((1, 64), F32)
        even, odd = (jnp.concatenate(two, 1) for two in ((gain_ref[...], blank), (blank, gain_ref[...])))
        own_gain[k + 1:k + 2] = jnp.where(core == 0, even, odd)
    for seq in range(2):
        for block_number in range(16):
            slot = 0
            for j in range(16):
                slot = jnp.where(span_ref[seq, j] == block_number, j, slot)
            slot_ref[seq, block_number] = slot
    for seq in range(2):
        for j in range(2):
            at = slice(seq * 128 + j * SPAN, seq * 128 + (j + 1) * SPAN)
            rows = lax.broadcasted_iota(jnp.int32, (SPAN, HEAD), 0) + span_ref[seq, 2 * me + j] * SPAN
            phase = rows.astype(F32) * freq_ref[...]
            left = lax.broadcasted_iota(jnp.int32, (SPAN, HEAD), 1) < HEAD // 2
            cos_ref[at] = jnp.cos(phase)
            sin_ref[at] = jnp.where(left, -jnp.sin(phase), jnp.sin(phase))
    for copy in starts:
        copy.wait()
    all_here()

    def gain_steps():
        slots = copies.slot(5)
        for k, by in enumerate((1, -1)):
            copies.start(slots[k], own_gain, own_gain, device_at(shifted(place, "y", by)))
        yield
        for k, by in enumerate((1, -1)):
            copies.arrived(slots[k], gain_s.at[(y - by) % 4, lo, core], device_at(shifted(place, "y", -by)))
        behind = gain_s.at[(y - 1) % 4, lo, core]
        copies.start(slots[2], behind, behind, device_at(shifted(place, "y", 1)))
        yield
        copies.arrived(slots[2], gain_s.at[(y + 2) % 4, lo, core], device_at(shifted(place, "y", -1)))
        across = device_at({**place, "x": place["x"] // 2 * 2 + (1 - lo)})
        copies.start(slots[3], gain_s.at[:, lo, core], gain_s.at[:, lo, core], across)
        yield
        copies.arrived(slots[3], gain_s.at[:, 1 - lo, core], across)
        yield

    first = [gather_part(copies, place, ORDERS[p], QKV_MEMBERS[p], [w_s]) for p in range(3)] + [gain_steps()]
    rest = [gather_part(copies, place, REST_ORDERS[p], REST_MEMBERS[p], [wo_out, wgu_out, wd_out]) for p in range(4)]

    def background(point):
        advance([rest[p] for p in FRONT_POINTS.get(point, ())])

    for step in range(5):
        advance(first)
        background(f"s{step}")
    run(first)
    background("gathered")
    sibling = other_core(place)
    pair_slot = copies.slot(1)[0]
    copies.start(pair_slot, gain_s.at[:, :, core], gain_s.at[:, :, core], sibling)
    copies.arrived(pair_slot, gain_s.at[:, :, 1 - core], sibling)
    keep = pltpu.make_async_copy(w_s, wqkv_out, local_sem.at[0])
    keep.start()

    x = x_ref[...]

    def block(n, carry):
        at = pl.ds(pl.multiple_of(n * 512, 512), 512)
        q_raw_ref[:, at] = dot(x, w_s[:, :, :, :, at].reshape(WIDTH, 512), 1, 0)
        return carry

    lax.fori_loop(0, 4, block, 0)
    for n in range(2):
        at = slice(n * 512, (n + 1) * 512)
        k_raw_ref[:, at] = dot(x, w_s[:, :, :, :, QUERY + n * 512:QUERY + (n + 1) * 512].reshape(WIDTH, 512), 1, 0)
    for n in range(2):
        value = dot(x, w_s[:, :, :, :, QUERY + KEY + n * 512:QUERY + KEY + (n + 1) * 512].reshape(WIDTH, 512), 1, 0).astype(BF16)
        for h in range(4):
            sent_s[4 * n + h, :, :, :, 3 * HEAD:] = value[:, h * HEAD:(h + 1) * HEAD].reshape(2, 2, SPAN, HEAD)
    cosine, sine = cos_ref[...], sin_ref[...]

    def place_heads(raw_ref, gain_of, heads, column, each):
        inverse = inverse_rms(raw_ref[...])
        for h in range(heads):
            normed = raw_ref[:, h * HEAD:(h + 1) * HEAD] * inverse * gain_of(h)
            turned = normed * cosine + pltpu.roll(normed, HEAD // 2, 1) * sine
            first = column + h % each * HEAD
            sent_s[h // each, :, :, :, first:first + HEAD] = turned.astype(BF16).reshape(2, 2, SPAN, HEAD)

    gains_ref[...] = jnp.zeros_like(gains_ref)
    for h in range(HEADS):
        gains_ref[h // 8:h // 8 + 1, h % 8 * HEAD:(h % 8 + 1) * HEAD] = gain_s[h // 4, h // 2 % 2, h % 2, 0:1]
    for h in range(8):
        gains_ref[2:5, h * HEAD:(h + 1) * HEAD] = gain_s[h // 2, h % 2, 0, 1:4] + gain_s[h // 2, h % 2, 1, 1:4]
    place_heads(q_raw_ref, lambda h: gains_ref[h // 8:h // 8 + 1, h % 8 * HEAD:(h % 8 + 1) * HEAD], HEADS, 0, 2)
    place_heads(k_raw_ref, lambda h: gains_ref[2:3, h * HEAD:(h + 1) * HEAD], KV_HEADS, 2 * HEAD, 1)

    background("projected")
    there, own = {}, []
    qkv_s = (qkv_0, qkv_1)
    for seq in range(2):
        own.append(pltpu.make_async_copy(sent_s.at[me, seq], qkv_s[seq].at[pl.ds(2 * me, 2)], local_sem.at[1 + seq]))
        own[seq].start()
        for o in range(1, 8):
            there[seq, o] = copies.slot(1)[0]
            copies.start(there[seq, o], sent_s.at[(me + o) % 8, seq], qkv_s[seq].at[pl.ds(2 * me, 2)], ctx_device(o))
    background("sent")
    back, kept = {}, [keep]
    for seq in range(2):
        own[seq].wait()
        for o in range(1, 8):
            copies.arrived(there[seq, o], qkv_s[seq].at[pl.ds(2 * ((me - o) % 8), 2)], ctx_device(-o))
        kept.append(pltpu.make_async_copy(qkv_s[seq], qkv_out.at[seq], local_sem.at[3 + seq]))
        kept[-1].start()
        sorted_blocks(slot_ref, seq, qkv_s[seq], 0, (q_s.at[0], q_s.at[1], k_s, v_s))
        for i in range(LENGTH // TILE):
            low, high = i * TILE, (i + 1) * TILE
            q = q_s[:, low:high, :].reshape(2 * TILE, HEAD)
            scores = tile_scores(q, k_s[:high], low)
            top = jnp.max(scores, -1, keepdims=True)
            raised = jnp.exp(scores - top)
            total = jnp.sum(raised, -1, keepdims=True)
            probs = (raised * (1.0 / total)).astype(BF16)
            out = dot(probs, v_s[:high], 1, 0).astype(BF16).reshape(2, TILE // SPAN, SPAN, HEAD)
            for h in range(2):
                o_s[low // SPAN:high // SPAN, :, h * HEAD:(h + 1) * HEAD] = out[h]
            lse_ref[seq, :, low:high, :] = jnp.broadcast_to(top + jnp.log(total), (2 * TILE, HEAD)).reshape(2, TILE, HEAD)
        sent_blocks(span_ref, seq, o_s, out_s)
        for o in range(1, 8):
            back[seq, o] = copies.slot(1)[0]
            copies.start(back[seq, o], out_s.at[(me + o) % 8, seq], heads_s.at[me, seq], ctx_device(o))
        background(f"attended {seq}")
    own = pltpu.make_async_copy(out_s.at[me], heads_s.at[me], local_sem.at[1])
    own.start()
    run(rest)
    for seq in range(2):
        for o in range(1, 8):
            copies.arrived(back[seq, o], heads_s.at[(me - o) % 8, seq], ctx_device(-o))
    own.wait()
    kept.append(pltpu.make_async_copy(heads_s, heads_out, local_sem.at[5]))
    kept[-1].start()
    for copy in kept:
        copy.wait()
    copies.finish()


def front(span_order, rows, freq, gains, shards):
    return pl.pallas_call(
        front_kernel,
        in_specs=[SMEM] + vmem(6) + anywhere(7),
        out_specs=[SMEM] + anywhere(4) + vmem(5) + anywhere(1) + vmem(1) + anywhere(1),
        out_shape=[jax.ShapeDtypeStruct((2, 16), jnp.int32), jax.ShapeDtypeStruct((4, 2, 2, 64, QKV), BF16), jax.ShapeDtypeStruct((4, 2, 2, 128, WIDTH), BF16),
                   jax.ShapeDtypeStruct((4, 2, 2, 64, 2 * FF), BF16), jax.ShapeDtypeStruct((4, 2, 2, 192, WIDTH), BF16),
                   jax.ShapeDtypeStruct((8, WIDTH), F32), jax.ShapeDtypeStruct((ROWS, HEAD), F32), jax.ShapeDtypeStruct((ROWS, HEAD), F32),
                   jax.ShapeDtypeStruct((ROWS, QUERY), F32), jax.ShapeDtypeStruct((ROWS, KEY), F32),
                   jax.ShapeDtypeStruct((2, 16, SPAN, 4 * HEAD), BF16), jax.ShapeDtypeStruct((2, 2, LENGTH, HEAD), F32),
                   jax.ShapeDtypeStruct((8, 2, 2, SPAN, 2 * HEAD), BF16)],
        scratch_shapes=[pltpu.VMEM((4, 2, 2, 64, QKV), BF16), pltpu.VMEM((4, 2, 2, 8, 128), F32), pltpu.VMEM((8, 2, 2, SPAN, 4 * HEAD), BF16),
                        pltpu.VMEM((16, SPAN, 4 * HEAD), BF16), pltpu.VMEM((16, SPAN, 4 * HEAD), BF16), pltpu.VMEM((2, LENGTH, HEAD), BF16), pltpu.VMEM((LENGTH, HEAD), BF16),
                        pltpu.VMEM((LENGTH, HEAD), BF16), pltpu.VMEM((16, SPAN, 2 * HEAD), BF16), pltpu.VMEM((8, 2, 2, SPAN, 2 * HEAD), BF16),
                        pltpu.VMEM((8, 2, 2, SPAN, 2 * HEAD), BF16), pltpu.SemaphoreType.DMA((8,)),
                        pltpu.SemaphoreType.DMA((FRONT_COPIES,)), pltpu.SemaphoreType.DMA((FRONT_COPIES,))],
        compiler_params=pltpu.CompilerParams(collective_id=1, has_side_effects=True, vmem_limit_bytes=60 << 20),
        cost_estimate=pl.CostEstimate(flops=4000000000, bytes_accessed=60 << 20, transcendentals=3 << 20),
        name="front",
    )(span_order, rows, freq, *gains, *shards)


MIDDLE_COPIES = 40


def middle_kernel(heads_ref, x_ref, cot_ref, norm_ref, wo, wgu, wd,
                  layer_ref, grad_mixed_ref, gains_ref, grad_heads_out, out_grad, gu_grad, down_grad,
                  wo_s, wgu_s, wd_s, att_s, gu_s, branch_s, mixed_s, low_s, mid_s, ffn_s, att_t, mix_t, mid_t,
                  att_c, mix_c, mid_c, branch_c, gu_c, ffn_c, sent_s, heads_s, local_sem, send, recv):
    place = torus_place()
    core, sibling = place["core"], other_core(place)
    me = lax.axis_index("ctx")
    copies = Copies(send, recv, MIDDLE_COPIES)
    all_here = hail([sibling] + [ctx_device(o) for o in range(1, 8)])
    ag_ref, fg_ref = norm_ref.at[3:4], norm_ref.at[4:5]
    pieces = [(wo, wo_s, slice(None))]
    for n in range(3):
        pieces += [(wgu, wgu_s, slice(n * 1024, (n + 1) * 1024)), (wgu, wgu_s, slice(FF + n * 1024, FF + (n + 1) * 1024))]
    pieces += [(wd, wd_s, slice(None))]
    here = []
    for i, (weight, buffer, at) in enumerate(pieces):
        here.append(pltpu.make_async_copy(weight.at[:, :, :, at], buffer.at[:, :, :, at], local_sem.at[i]))
        here[i].start()

    def give_stripes(turned, both):
        both[:, :, :ROWS] = turned[:, core]
        slot = copies.slot(1)[0]
        copies.start(slot, turned.at[:, 1 - core], both.at[:, :, pl.ds(ROWS, ROWS)], sibling)
        return slot, both.at[:, :, pl.ds(ROWS, ROWS)]

    def give_rows(both):
        slot = copies.slot(1)[0]
        copies.start(slot, both.at[pl.ds(0, ROWS)], both.at[pl.ds(ROWS, ROWS)], sibling)
        return slot, both.at[pl.ds(ROWS, ROWS)]

    for g in range(8):
        att_s[:, g * 256:(g + 1) * 256] = heads_ref[g].reshape(ROWS, 256)
    store_stripes(att_s[...], att_t, QUERY)
    all_here()
    att_given = give_stripes(att_t, att_c)
    here[0].wait()
    for n in range(2):
        at = slice(n * 512, (n + 1) * 512)
        branch_s[:, at] = dot(att_s[...], wo_s[:, :, :, at].reshape(QUERY, 512), 1, 0)
    branch_inverse = inverse_rms(branch_s[...])
    mixed = x_ref[...].astype(F32) + branch_s[...] * branch_inverse * ag_ref[...]
    mixed_s[...] = mixed
    low_s[...] = mixed.astype(BF16)
    store_stripes(low_s[...], mix_t, WIDTH)
    mix_given = give_stripes(mix_t, mix_c)
    for n in range(FF // 512):
        at, up_at = slice(n * 512, (n + 1) * 512), slice(FF + n * 512, FF + (n + 1) * 512)
        if n % 2 == 0:
            here[1 + n].wait()
            here[2 + n].wait()
        gate = dot(low_s[...], wgu_s[:, :, :, at].reshape(WIDTH, 512), 1, 0)
        up = dot(low_s[...], wgu_s[:, :, :, up_at].reshape(WIDTH, 512), 1, 0)
        gu_s[:, at] = gate
        gu_s[:, up_at] = up
        mid_s[:, at] = (gate * jax.nn.sigmoid(gate) * up).astype(BF16)
    store_stripes(mid_s[...], mid_t, FF)
    mid_given = give_stripes(mid_t, mid_c)
    here[-1].wait()
    for n in range(2):
        at = slice(n * 512, (n + 1) * 512)
        ffn_s[:, at] = dot(mid_s[...], wd_s[:, :, :, at].reshape(FF, 512), 1, 0)
    ffn_out = ffn_s[...]
    ffn_inverse = inverse_rms(ffn_out)
    layer_ref[...] = (mixed_s[...] + ffn_out * ffn_inverse * fg_ref[...]).astype(BF16)
    grad_ffn, grad_ffn_gain = rms_back(ffn_out, ffn_inverse, fg_ref[...], cot_ref[...].astype(F32))
    ffn_c[:ROWS] = grad_ffn.astype(BF16)
    ffn_given = give_rows(ffn_c)

    def backward_block(n, carry):
        at = pl.ds(pl.multiple_of(n * 768, 256), 768)
        up_at = pl.ds(pl.multiple_of(FF + n * 768, 256), 768)
        grad_middle = dot(ffn_c[:ROWS], wd_s[pl.ds(n * 2, 2)].reshape(768, WIDTH), 1, 1)
        gate, up = gu_s[:, at], gu_s[:, up_at]
        sigmoid_gate = jax.nn.sigmoid(gate)
        gu_c[:ROWS, at] = (grad_middle * up * sigmoid_gate * (1.0 + gate * (1.0 - sigmoid_gate))).astype(BF16)
        gu_c[:ROWS, up_at] = (grad_middle * (gate * sigmoid_gate)).astype(BF16)
        return carry

    lax.fori_loop(0, 4, backward_block, 0)

    gu_given = give_rows(gu_c)
    for n in range(4):
        at = slice(n * 256, (n + 1) * 256)
        ffn_s[:, at] = cot_ref[:, at].astype(F32) + dot(gu_c[:ROWS], wgu_s[2 * n:2 * n + 2].reshape(256, 2 * FF), 1, 1)
    grad_mixed_ref[...] = ffn_s[...]
    grad_branch, grad_attn_gain = rms_back(branch_s[...], branch_inverse, ag_ref[...], ffn_s[...])
    branch_c[:ROWS] = grad_branch.astype(BF16)
    branch_given = give_rows(branch_c)
    for g in range(8):
        grad = dot(branch_c[:ROWS], wo_s[g].reshape(256, WIDTH), 1, 1)
        sent_s[g] = grad.astype(BF16).reshape(2, 128, 256)
    own = pltpu.make_async_copy(sent_s.at[me], heads_s.at[me], local_sem.at[3])
    own.start()
    there = copies.slot(7)
    for o in range(1, 8):
        copies.start(there[o - 1], sent_s.at[(me + o) % 8], heads_s.at[me], ctx_device(o))
    gains_ref[...] = jnp.zeros_like(gains_ref)
    gains_ref[0:1] = grad_attn_gain
    gains_ref[1:2] = grad_ffn_gain

    def weight_grad(k, given, turned, grad, buffer, out):
        for slot, view in given:
            copies.arrived(slot, view, sibling)
        stripes = turned[...].reshape(8 * turned.shape[1], 2 * ROWS)
        for n in range(buffer.shape[3] // 512):
            at = slice(n * 512, (n + 1) * 512)
            buffer[:, 0, :, at] = dot(stripes, grad[:, at], 1, 0).astype(BF16).reshape(8, -1, 512)
        copy = pltpu.make_async_copy(buffer.at[:, 0], out, local_sem.at[k])
        copy.start()
        return copy

    kept = [weight_grad(0, (mid_given, ffn_given), mid_c, ffn_c, wd_s, down_grad),
            weight_grad(1, (mix_given, gu_given), mix_c, gu_c, wgu_s, gu_grad),
            weight_grad(2, (att_given, branch_given), att_c, branch_c, wo_s, out_grad)]
    own.wait()
    for o in range(1, 8):
        copies.arrived(there[o - 1], heads_s.at[(me - o) % 8], ctx_device(-o))
    for seq in range(2):
        kept.append(pltpu.make_async_copy(heads_s.at[:, seq], grad_heads_out.at[seq], local_sem.at[4 + seq]))
        kept[-1].start()
    for copy in kept:
        copy.wait()
    copies.finish()


def middle(heads, rows, cotangent, gains, wo, wgu, wd):
    return pl.pallas_call(
        middle_kernel,
        in_specs=vmem(4) + anywhere(3),
        out_specs=vmem(3) + anywhere(4),
        out_shape=[jax.ShapeDtypeStruct((ROWS, WIDTH), BF16), jax.ShapeDtypeStruct((ROWS, WIDTH), F32), jax.ShapeDtypeStruct((8, WIDTH), F32),
                   jax.ShapeDtypeStruct((2, 8, 128, 256), BF16), jax.ShapeDtypeStruct((8, 128, WIDTH), BF16),
                   jax.ShapeDtypeStruct((8, 64, 2 * FF), BF16), jax.ShapeDtypeStruct((8, 192, WIDTH), BF16)],
        scratch_shapes=[pltpu.VMEM((8, 2, 128, WIDTH), BF16), pltpu.VMEM((8, 2, 64, 2 * FF), BF16), pltpu.VMEM((8, 2, 192, WIDTH), BF16),
                        pltpu.VMEM((ROWS, QUERY), BF16), pltpu.VMEM((ROWS, 2 * FF), F32), pltpu.VMEM((ROWS, WIDTH), F32), pltpu.VMEM((ROWS, WIDTH), F32),
                        pltpu.VMEM((ROWS, WIDTH), BF16), pltpu.VMEM((ROWS, FF), BF16), pltpu.VMEM((ROWS, WIDTH), F32),
                        pltpu.VMEM((8, 2, 128, ROWS), BF16), pltpu.VMEM((8, 2, 64, ROWS), BF16), pltpu.VMEM((8, 2, 192, ROWS), BF16),
                        pltpu.VMEM((8, 128, 2 * ROWS), BF16), pltpu.VMEM((8, 64, 2 * ROWS), BF16), pltpu.VMEM((8, 192, 2 * ROWS), BF16),
                        pltpu.VMEM((2 * ROWS, WIDTH), BF16), pltpu.VMEM((2 * ROWS, 2 * FF), BF16), pltpu.VMEM((2 * ROWS, WIDTH), BF16),
                        pltpu.VMEM((8, 2, 128, 256), BF16), pltpu.VMEM((8, 2, 128, 256), BF16),
                        pltpu.SemaphoreType.DMA((8,)),
                        pltpu.SemaphoreType.DMA((MIDDLE_COPIES,)), pltpu.SemaphoreType.DMA((MIDDLE_COPIES,))],
        compiler_params=pltpu.CompilerParams(collective_id=3, has_side_effects=True, vmem_limit_bytes=62 << 20),
        cost_estimate=pl.CostEstimate(flops=18000000000, bytes_accessed=40 << 20, transcendentals=3 << 20),
        name="middle",
    )(heads, rows, cotangent, gains, wo, wgu, wd)


BACK_COPIES = 460
BACK_POINTS = {"start": (0, 1, 2, 3), "turned": (0, 1, 2, 3), "given": (0, 1, 2), "summed": (3,), "s0": (0, 1, 2), "s1": (3,), "s2": (0, 1, 2), "s3": (3,)}
BACK_SHARE = 4


def add_region(acc, temp, at, extra):
    ys, los, rows, _ = at
    chunk = min(32, rows.size)
    per = rows.size // chunk

    def one(step, carry):
        row = step % per * chunk
        lo = step // per % los.size
        y = step // (per * los.size)

        def view(ref, where):
            r = pl.ds(pl.multiple_of(where[2].start + row, 16), chunk)
            return ref.at[where[0].start + y, where[1].start + lo, r, where[3]]

        total = view(acc, at)[...]
        for t in extra:
            total += view(temp, t)[...]
        view(acc, at)[...] = total
        return carry

    lax.fori_loop(0, per * los.size * ys.size, one, 0)


def reduce_part(copies, place, order, members, accs, temps):
    def blocks(m, phase, at, half, landing):
        here = place
        if landing:
            for axis in order[phase + 1:]:
                here = shifted(here, axis, 1 if half else -1)
        return m.regions(here, order[phase], at, order[:phase], half)

    def send(phase, at, half, by, land_at, slots):
        slots = iter(slots)
        device = device_at(shifted(place, order[phase], by))
        for m in members:
            for src, dst in zip(blocks(m, phase, at, half, False), blocks(m, phase, land_at, half, True)):
                copies.start(next(slots), accs[m.array].at[src], temps[m.array].at[dst], device)

    def wait(phase, half, by, land_at, slots):
        slots = iter(slots)
        device = device_at(shifted(place, order[phase], -by))
        for m in members:
            for dst in blocks(m, phase, land_at, half, True):
                copies.arrived(next(slots), temps[m.array].at[dst], device)

    def add(phase, at, half, land_ats):
        for m in members:
            landed = [blocks(m, phase, land_at, half, True) for land_at in land_ats]
            for k, region in enumerate(blocks(m, phase, at, half, False)):
                add_region(accs[m.array], temps[m.array], region, [t[k] for t in landed])

    for phase in (2, 1):
        c = place[order[phase]]
        pieces = sum(len(blocks(m, phase, c, 0, False)) for m in members)
        slots = {by: [copies.slot(pieces) for _ in range(3)] for by in (1, -1)}
        for by, half in ((1, 0), (-1, 1)):
            send(phase, c + 2, half, by, c + 2, slots[by][0])
        for by, half in ((1, 0), (-1, 1)):
            send(phase, c + by, 1 - half, by, c + 1, slots[by][1])
        yield
        for by, half in ((1, 0), (-1, 1)):
            wait(phase, half, by, c + by, slots[by][0])
            add(phase, c + by, half, [c + by])
            send(phase, c + by, half, by, c + 1, slots[by][2])
        yield
        for half in (0, 1):
            for by in (1, -1):
                first = half == (0 if by == 1 else 1)
                wait(phase, half, by, c if by == 1 else c + 2, slots[by][2 if first else 1])
            add(phase, c, half, [c, c + 2])
    c = place[order[0]]
    lands = {1: 1, -1: 1, 2: -1}
    slots = {(by, half): copies.slot(len(members)) for by in lands for half in (0, 1)}
    for by, land in lands.items():
        for half in (0, 1):
            send(0, c + by, half, by, c + land, slots[by, half])
    yield
    for half in (0, 1):
        for by, land in lands.items():
            wait(0, half, by, c - by + land, slots[by, half])
        add(0, c, half, [c - by + land for by, land in lands.items()])


def share_direct(copies, place, members, accs, outs, sem):
    me = lax.axis_index("ctx")

    def view(m, at):
        at = at % 8
        return outs[m.array].at[pl.ds(m.row, m.rows), m.block(at // 4 * 2, at % 4)]

    slots = {o: copies.slot(len(members)) for o in range(1, 8)}
    stores = []
    for i, m in enumerate(members):
        mine = accs[m.array].at[place["y"], place["x"] % 2, pl.ds(m.row, m.rows), m.block(place["x"], place["z"])]
        for o in range(1, 8):
            copies.start(slots[o][i], mine, view(m, me), ctx_device(o))
        stores.append(pltpu.make_async_copy(mine, view(m, me), sem.at[i]))
        stores[-1].start()
    yield
    for o in range(1, 8):
        for i, m in enumerate(members):
            copies.arrived(slots[o][i], view(m, me - o), ctx_device(-o))
    for store in stores:
        store.wait()


def back_kernel(slot_ref, span_ref, cos_ref, sin_ref, norm_ref, gains_ref, qkv_in, heads_in, lse_in, q_raw_in, k_raw_in,
                mixed_in, x_in, wqkv_in, out_grad, gu_grad, down_grad,
                tokens_ref, gain_total_ref, qkv_total, out_total, gu_total, down_total,
                acc_o, acc_gu, acc_d, temp_o, temp_gu, temp_d, temp_q, w_s, sent_s, arrived_s, gains_s, rings,
                qkv_s, g_s, lse_s, qs, k_s, v_s, gs, dk_s, dv_s, d_s, q_raw, k_raw, mixed, x_s, x_t, x_c, grad_c,
                local_sem, share_sem, send, recv):
    place = torus_place()
    core, sibling = place["core"], other_core(place)
    me = lax.axis_index("ctx")
    copies = Copies(send, recv, BACK_COPIES)
    all_here = hail(partners(place))
    loads = []

    def load(src, dst):
        copy = pltpu.make_async_copy(src, dst, local_sem.at[len(loads)])
        copy.start()
        loads.append(copy)
        return copy

    qg_ref, kg_ref = (norm_ref.at[0:1], norm_ref.at[1:2]), (norm_ref.at[2:3],)
    accs, temps = (acc_o, acc_gu, acc_d), (temp_o, temp_gu, temp_d)
    first = [load(qkv_in, qkv_s), load(heads_in, g_s), load(lse_in, lse_s)]
    acc_loads = [load(src, dst) for src, dst in zip((out_grad, gu_grad, down_grad), accs)]
    rest = [reduce_part(copies, place, REST_ORDERS[p], REST_MEMBERS[p], accs, temps) for p in range(4)]
    there = {}


    def background(point):
        advance([rest[p] for p in BACK_POINTS.get(point, ())])

    second = [load(wqkv_in, w_s), load(q_raw_in, q_raw), load(k_raw_in, k_raw), load(mixed_in, mixed), load(x_in, x_s)]
    own = []
    for seq in range(2):
        if seq == 0:
            for copy in first:
                copy.wait()
        sorted_blocks(slot_ref, seq, qkv_s, 16 * seq, (qs.at[0], qs.at[1], k_s, v_s))
        sorted_blocks(slot_ref, seq, g_s, 16 * seq, (gs.at[0], gs.at[1]))
        dk_s[...] = jnp.zeros_like(dk_s)
        dv_s[...] = jnp.zeros_like(dv_s)
        for i in range(LENGTH // TILE):
            if seq == 0 and i == 1:
                for copy in acc_loads:
                    copy.wait()
                all_here()
                background("start")
            low, high = i * TILE, (i + 1) * TILE
            k, v = k_s[:high], v_s[:high]
            for h in range(2):
                q, g = qs[h, low:high], gs[h, low:high]
                probs = jnp.exp(tile_scores(q, k, low) - lse_s[seq, h, low:high, :1])
                grad_probs = dot(g, v, 1, 1)
                inner = jnp.sum(probs * grad_probs, -1, keepdims=True)
                grad_scores = (probs * (grad_probs - inner)).astype(BF16)
                dq = (dot(grad_scores, k, 1, 0) * score_scale).astype(BF16).reshape(TILE // SPAN, SPAN, HEAD)
                d_s[low // SPAN:high // SPAN, :, h * HEAD:(h + 1) * HEAD] = dq
                dk_s[:high] += dot(grad_scores, q, 0, 0)
                dv_s[:high] += dot(probs.astype(BF16), g, 0, 0)
        d_s[:, :, 2 * HEAD:3 * HEAD] = (dk_s[...] * score_scale).astype(BF16).reshape(16, SPAN, HEAD)
        d_s[:, :, 3 * HEAD:] = dv_s[...].astype(BF16).reshape(16, SPAN, HEAD)
        sent_blocks(span_ref, seq, d_s, sent_s)
        own.append(load(sent_s.at[me, seq], arrived_s.at[me, seq]))
        for o in range(1, 8):
            there[seq, o] = copies.slot(1)[0]
            copies.start(there[seq, o], sent_s.at[(me + o) % 8, seq], arrived_s.at[me, seq], ctx_device(o))
        background(f"sent {seq}")
    for copy in second:
        copy.wait()
    store_stripes(x_s[...], x_t, WIDTH)
    x_c[:, :, :ROWS] = x_t[:, core]
    x_slot, x_there = copies.slot(1)[0], x_c.at[:, :, pl.ds(ROWS, ROWS)]
    copies.start(x_slot, x_t.at[:, 1 - core], x_there, sibling)
    background("turned")
    for seq in range(2):
        own[seq].wait()
        for o in range(1, 8):
            copies.arrived(there[seq, o], arrived_s.at[(me - o) % 8, seq], ctx_device(-o))
    background("arrived")
    cosine, sine = cos_ref[...], sin_ref[...]
    gains_s[...] = jnp.zeros_like(gains_s)
    gains_s[3:5] = gains_ref[0:2]

    def one(raw, gain_ref, heads, column, each, out_at, gain_rows):
        width = heads * HEAD
        inverse = inverse_rms(raw[...])
        inner = jnp.zeros((ROWS, 1), F32)

        def turned_back(h):
            first = column + h % each * HEAD
            u = arrived_s[h // each, :, :, :, first:first + HEAD].reshape(ROWS, HEAD).astype(F32)
            return u * cosine - pltpu.roll(u, HEAD // 2, 1) * sine

        def gain_of(h):
            return gain_ref[h // 8][:, h % 8 * HEAD:(h % 8 + 1) * HEAD]

        for h in range(heads):
            at = slice(h * HEAD, (h + 1) * HEAD)
            dy = turned_back(h)
            inner += jnp.sum(dy * gain_of(h) * raw[:, at], -1, keepdims=True)
            row, col = gain_rows + h // 8, h % 8 * HEAD
            gains_s[row:row + 1, col:col + HEAD] = jnp.sum(dy * raw[:, at] * inverse, 0, keepdims=True)
        back = inverse * inverse * inverse * (inner / width)
        for h in range(heads):
            at = slice(h * HEAD, (h + 1) * HEAD)
            grad = inverse * (turned_back(h) * gain_of(h)) - raw[:, at] * back
            grad_c[:ROWS, out_at + h * HEAD:out_at + (h + 1) * HEAD] = grad.astype(BF16)
            if h % 4 == 3:
                give(out_at // 512 + h // 4)

    grad_slots = copies.slot(QKV // 512)

    def give(n):
        at = slice(n * 512, (n + 1) * 512)
        copies.start(grad_slots[n], grad_c.at[pl.ds(0, ROWS), at], grad_c.at[pl.ds(ROWS, ROWS), at], sibling)

    for g in range(8):
        grad_c[:ROWS, QUERY + KEY + g * HEAD:QUERY + KEY + (g + 1) * HEAD] = arrived_s[g, :, :, :, 3 * HEAD:].reshape(ROWS, HEAD)
    give(6)
    give(7)
    one(k_raw, kg_ref, KV_HEADS, 2 * HEAD, 1, QUERY, 2)
    one(q_raw, qg_ref, HEADS, 0, 2, 0, 0)
    background("given")
    for n in range(4):
        at = slice(n * 256, (n + 1) * 256)
        tokens_ref[:, at] = (mixed[:, at] + dot(grad_c[:ROWS], w_s[n].reshape(256, QKV), 1, 1)).astype(BF16)
    acc_q = w_s.at[:, :, 0]
    copies.arrived(x_slot, x_there, sibling)
    stripes = x_c[...].reshape(512, 2 * ROWS)
    for n in (6, 7, 4, 5, 0, 1, 2, 3):
        at = slice(n * 512, (n + 1) * 512)
        copies.arrived(grad_slots[n], grad_c.at[pl.ds(ROWS, ROWS), at], sibling)
        acc_q[:, :, :, at] = dot(stripes, grad_c[:, at], 1, 0).astype(BF16).reshape(4, 2, 64, 512)

    def gain_steps():
        rings[0, core] = gains_s[...]
        slot = copies.slot(1)[0]
        copies.start(slot, rings.at[0, core], rings.at[0, core], sibling)
        yield
        copies.arrived(slot, rings.at[0, 1 - core], sibling)
        total = rings[0, 0] + rings[0, 1]
        for k, axis in enumerate("zyx"):
            ring, at = rings.at[1 + k], place[axis]
            ring[at] = total
            slots = copies.slot(3)
            for slot, by in zip(slots, (1, -1, 2)):
                copies.start(slot, ring.at[at], ring.at[at], device_at(shifted(place, axis, by)))
            yield
            for slot, by in zip(slots, (1, -1, 2)):
                copies.arrived(slot, ring.at[(at - by) % 4], device_at(shifted(place, axis, -by)))
            total = (ring[0] + ring[1]) + (ring[2] + ring[3])
        gain_total_ref[...] = total

    last = [reduce_part(copies, place, ORDERS[p], QKV_MEMBERS[p], [acc_q], [temp_q]) for p in range(3)]
    gains = [gain_steps()]
    outs = (out_total, gu_total, down_total)
    rest_share = share_direct(copies, place, [m for p in REST_MEMBERS for m in p], accs, outs, share_sem)
    last_share = share_direct(copies, place, [m for p in QKV_MEMBERS for m in p], [acc_q], [qkv_total], share_sem)
    background("summed")
    for step in range(5):
        advance(last)
        advance(gains)
        background(f"s{step}")
        if step == BACK_SHARE:
            run(rest)
        if step >= BACK_SHARE:
            advance([rest_share])
    run(last + gains)
    run(rest)
    run([rest_share, last_share])
    copies.finish()


def back(slot_of, span_order, cosine, sine, norm_gains, gains, qkv, heads, lse, q_raw, k_raw, mixed, rows, wqkv, rest):
    bf = lambda *shape: pltpu.VMEM(shape, BF16)
    rest_shapes = [(4, 2, 128, WIDTH), (4, 2, 64, 2 * FF), (4, 2, 192, WIDTH)]
    return pl.pallas_call(
        back_kernel,
        in_specs=[SMEM, SMEM] + vmem(4) + anywhere(11),
        out_specs=vmem(2) + anywhere(4),
        out_shape=[jax.ShapeDtypeStruct((ROWS, WIDTH), BF16), jax.ShapeDtypeStruct((8, WIDTH), F32), jax.ShapeDtypeStruct((64, QKV), BF16),
                   jax.ShapeDtypeStruct((128, WIDTH), BF16), jax.ShapeDtypeStruct((64, 2 * FF), BF16), jax.ShapeDtypeStruct((192, WIDTH), BF16)],
        scratch_shapes=[bf(*s) for s in rest_shapes] * 2 + [bf(4, 2, 64, QKV), bf(4, 2, 2, 64, QKV), bf(8, 2, 2, SPAN, 4 * HEAD), bf(8, 2, 2, SPAN, 4 * HEAD),
                        pltpu.VMEM((8, WIDTH), F32), pltpu.VMEM((4, 4, 8, WIDTH), F32),
                        bf(32, SPAN, 4 * HEAD), bf(32, SPAN, 2 * HEAD), pltpu.VMEM((2, 2, LENGTH, HEAD), F32),
                        bf(2, LENGTH, HEAD), bf(LENGTH, HEAD), bf(LENGTH, HEAD), bf(2, LENGTH, HEAD),
                        pltpu.VMEM((LENGTH, HEAD), F32), pltpu.VMEM((LENGTH, HEAD), F32), bf(16, SPAN, 4 * HEAD),
                        pltpu.VMEM((ROWS, QUERY), F32), pltpu.VMEM((ROWS, KEY), F32), pltpu.VMEM((ROWS, WIDTH), F32), bf(ROWS, WIDTH),
                        bf(8, 2, 64, ROWS), bf(8, 64, 2 * ROWS), bf(2 * ROWS, QKV),
                        pltpu.SemaphoreType.DMA((16,)), pltpu.SemaphoreType.DMA((8,)),
                        pltpu.SemaphoreType.DMA((BACK_COPIES,)), pltpu.SemaphoreType.DMA((BACK_COPIES,))],
        compiler_params=pltpu.CompilerParams(collective_id=2, has_side_effects=True, vmem_limit_bytes=62 << 20),
        cost_estimate=pl.CostEstimate(flops=10000000000, bytes_accessed=60 << 20, transcendentals=3 << 20),
        name="back",
    )(slot_of, span_order, cosine, sine, norm_gains, gains, qkv, heads, lse, q_raw, k_raw, mixed, rows, wqkv, *rest)


def finish_kernel(qkv_ref, out_ref, gu_ref, down_ref, layer_in, tokens_in,
                  q_ref, k_ref, v_ref, o_ref, g_ref, u_ref, d_ref, layer_ref, tokens_ref):
    q_ref[...] = qkv_ref[:, :QUERY].astype(F32)
    k_ref[...] = qkv_ref[:, QUERY:QUERY + KEY].astype(F32)
    v_ref[...] = qkv_ref[:, QUERY + KEY:].astype(F32)
    o_ref[...] = out_ref[...].astype(F32)
    g_ref[...] = gu_ref[:, :FF].astype(F32)
    u_ref[...] = gu_ref[:, FF:].astype(F32)
    d_ref[...] = down_ref[...].astype(F32)
    layer_ref[...] = layer_in[...]
    tokens_ref[...] = tokens_in[...]


def finish(qkv_total, out_total, gu_total, down_total, layer_out, grad_tokens):
    wide = [(64, QUERY), (64, KEY), (64, KEY), (128, WIDTH), (64, FF), (64, FF), (192, WIDTH)]
    return pl.pallas_call(
        finish_kernel,
        in_specs=vmem(6),
        out_specs=vmem(9),
        out_shape=[jax.ShapeDtypeStruct(s, F32) for s in wide] + [jax.ShapeDtypeStruct((ROWS, WIDTH), BF16)] * 2,
        compiler_params=pltpu.CompilerParams(vmem_limit_bytes=60 << 20),
        name="finish",
    )(qkv_total, out_total, gu_total, down_total, layer_out, grad_tokens)


def per_device(
    tokens,
    span_order,
    w_query,
    w_key,
    w_value,
    w_out,
    w_gate,
    w_up,
    w_down,
    query_gain,
    key_gain,
    attn_gain,
    ffn_gain,
    cotangent,
):
    at_fsdp = lax.axis_index("fsdp")
    token_rows = tokens.reshape(ROWS, WIDTH)

    freq = rope_base ** (-2.0 * (np.arange(HEAD) % (HEAD // 2)) / HEAD)
    slot_of, wqkv, wo, wgu, wd, norm_gains, cosine, sine, query_raw, key_raw, qkv, lse, heads = front(
        span_order, token_rows, freq.astype(np.float32)[None], [g[None] for g in (query_gain, key_gain, attn_gain, ffn_gain)],
        (w_query, w_key, w_value, w_out, w_gate, w_up, w_down))
    wo, wgu, wd = [w.reshape((8,) + w.shape[2:]) for w in (wo, wgu, wd)]
    layer_out, grad_mixed, gains_af, grad_heads, *rest = middle(
        heads.reshape(8, 2, 128, 2 * HEAD), token_rows, cotangent.reshape(ROWS, WIDTH), norm_gains, wo, wgu, wd)
    rest = [g.reshape((4, 2) + g.shape[1:]) for g in rest]
    grad_tokens, gain_totals, *totals = back(
        slot_of, span_order, cosine, sine, norm_gains, gains_af, qkv.reshape(32, SPAN, 4 * HEAD), grad_heads.reshape(32, SPAN, 2 * HEAD),
        lse, query_raw, key_raw, grad_mixed, token_rows, wqkv, rest)
    *weight_grads, layer_out, grad_tokens = finish(*totals, layer_out, grad_tokens)
    gain_totals = gain_totals.reshape(-1)

    def own_gain(first, count):
        return lax.dynamic_slice_in_dim(gain_totals, first + at_fsdp * count, count)

    return (
        layer_out.reshape(tokens.shape),
        grad_tokens.reshape(tokens.shape),
        *weight_grads,
        own_gain(0, 128),
        own_gain(2048, 64),
        own_gain(3072, 64),
        own_gain(4096, 64),
    )


def solution(mesh):
    rows, shard, gain = P("fsdp", "ctx", None), P("fsdp", None), P("fsdp")
    return jax.shard_map(
        per_device,
        mesh=mesh,
        in_specs=(rows, shard) + (shard,) * 7 + (gain,) * 4 + (rows,),
        out_specs=(rows, rows) + (shard,) * 7 + (gain,) * 4,
        check_vma=False,
    )
```
